256 devices in a mesh: batch: 16 (over z, y_lo), feat: 16 (over y_hi, x, core).
Axes of the slice: x: 4, y: 4 (y_hi: 2, y_lo: 2; y = y_hi * 2 + y_lo), z: 8, core: 2. Of those that a mesh axis runs over, the one named last changes fastest.
Arguments:
- view_a: float32 [16384, 8192], P('batch', 'feat'), may hold values from -1500 to 1500
- view_b: float32 [16384, 8192], P('batch', 'feat'), may hold values from -1500 to 1500
Outputs:
- grad_a: float32 [16384, 8192], P('batch', 'feat')
- grad_b: float32 [16384, 8192], P('batch', 'feat')
- loss: float32 [], replicated
The draws below stay inside these ranges and needn't reach their ends.
All inputs are finite; a program needn't handle non-finite values.
Results may differ from the reference program's by a relative error of at most 0.0003.
Values sent between devices are 32-bit elements; how exact they have to be, the bound alone decides.
A program may use at most 128 MiB of HBM per device.

```python
import math
import jax
import jax.numpy as jnp
from jax import lax

FEAT_DEV = 512
BAND = 4
ROWS = 16384
FEAT = 8192
N_FEAT = 16


def shared_base(key, loading):
    field = jax.random.normal(jax.random.fold_in(key, 1), (ROWS, FEAT), jnp.float32)
    common = jax.random.normal(jax.random.fold_in(key, 2), (ROWS, 1), jnp.float32)
    loads = jax.random.uniform(jax.random.fold_in(key, 3), (1, FEAT), jnp.float32, -loading, loading)
    return field + common * loads


def column_law(key, field):
    first, second = jax.random.split(key)
    scale = jnp.exp(jax.random.uniform(first, (1, FEAT), jnp.float32, 0.0, math.log(10.0)))
    offset = jax.random.uniform(second, (1, FEAT), jnp.float32, -2.0, 2.0)
    return (field + offset) * scale


def draw_view_a(key, part):
    base = shared_base(key, 0.3)
    key = jax.random.fold_in(key, 11)
    first = jax.random.fold_in(key, 0)
    return column_law(first, base)


def draw_view_b(key, part):
    base = shared_base(key, 0.3)
    key = jax.random.fold_in(key, 23)
    first, second = jax.random.split(key)
    ramp = jnp.arange(FEAT, dtype=jnp.float32)[None, :] / (FEAT - 1)
    mixing = 0.3 + 0.65 * ramp
    rest = jnp.sqrt(1.0 - mixing * mixing)
    noise = jax.random.normal(second, (ROWS, FEAT), jnp.float32)
    return column_law(first, mixing * base + rest * noise)


def setup_inputs(seed: int = 0) -> dict:
    splits = jax.random.split(jax.random.key(seed), 3)
    return {
        "view_a": draw_view_a(jax.random.fold_in(splits[2], 71), 0),
        "view_b": draw_view_b(jax.random.fold_in(splits[2], 71), 0),
    }


eps = 1e-05
off_weight = 0.25
highest = lax.Precision.HIGHEST

def normalize(field):
    mean = lax.optimization_barrier(jnp.mean(field, 0))
    centered = field - mean
    spread = jnp.sqrt(lax.optimization_barrier(jnp.mean(centered * centered, 0)) + eps)
    return (centered / spread, spread)

def reference(view_a, view_b):
    blocks = N_FEAT
    width = FEAT_DEV
    norm_a, sd_a = normalize(view_a)
    norm_b, sd_b = normalize(view_b)
    blocks_a = norm_a.reshape(ROWS, blocks, width).transpose(1, 0, 2)
    blocks_b = norm_b.reshape(ROWS, blocks, width).transpose(1, 0, 2)
    offsets = jnp.arange(BAND, dtype=jnp.int32)

    def tiles_of(index):
        chosen = blocks_b[(index + offsets) % blocks]
        return jnp.einsum('rf,krg->kfg', blocks_a[index], chosen, precision=highest) / ROWS
    tiles = lax.map(tiles_of, jnp.arange(blocks, dtype=jnp.int32))
    diagonal = jnp.diagonal(tiles[:, 0], axis1=1, axis2=2)
    loss = (jnp.sum((1.0 - diagonal) ** 2) + off_weight * (jnp.sum(tiles * tiles) - jnp.sum(diagonal * diagonal))) / FEAT
    eye = jnp.eye(width, dtype=jnp.float32)
    weights = off_weight * tiles
    first = weights[:, 0] + eye[None] * (-(1.0 - diagonal) - off_weight * diagonal)[:, None, :]
    weights = weights.at[:, 0].set(first)

    def grad_a_of(index):
        chosen = blocks_b[(index + offsets) % blocks]
        return jnp.einsum('krg,kfg->rf', chosen, weights[index], precision=highest)

    def grad_b_of(index):
        source = (index - offsets) % blocks
        return jnp.einsum('krf,kfg->rg', blocks_a[source], weights[source, offsets], precision=highest)
    every = jnp.arange(blocks, dtype=jnp.int32)
    g_a = lax.map(grad_a_of, every).transpose(1, 0, 2).reshape(ROWS, FEAT)
    g_b = lax.map(grad_b_of, every).transpose(1, 0, 2).reshape(ROWS, FEAT)
    grad_a = (g_a - lax.optimization_barrier(jnp.mean(g_a, 0)) - norm_a * lax.optimization_barrier(jnp.mean(g_a * norm_a, 0))) / sd_a
    grad_b = (g_b - lax.optimization_barrier(jnp.mean(g_b, 0)) - norm_b * lax.optimization_barrier(jnp.mean(g_b * norm_b, 0))) / sd_b
    return (grad_a, grad_b, loss)
```

```python
import functools

import jax
import jax.numpy as jnp
from jax import lax
from jax.experimental import pallas as pl
from jax.experimental.pallas import tpu as pltpu
from jax.sharding import PartitionSpec as P

MESH = pl.DeviceIdType.MESH
F32 = jnp.float32
BF16 = jnp.bfloat16

eps = 1e-05
off_weight = 0.25

NZ = 8
NX = 4
NY = 4
NF = 16
PARTS = 8
BANDS = 4
HOPS = 4


def mod(value, n):
    return lax.rem(value + n, n)


def split(value):
    hi = value.astype(BF16)
    return hi, (value - hi.astype(F32)).astype(BF16)


def dot3(left, right, transposed=False):
    dims = (((1,), (1 if transposed else 0,)), ((), ()))
    dot = functools.partial(lax.dot_general, dimension_numbers=dims, preferred_element_type=F32)
    return dot(left[0], right[0]) + dot(left[0], right[1]) + dot(left[1], right[0])


def kernel(
    a_hbm, b_hbm, ga_hbm, gb_hbm, loss_ref,
    raw_a, raw_b, at_hi, at_lo, b_hi, b_lo, tiles, rs_p, rs_m, y_recv, fin, cfull, c_hi, c_lo,
    g_a, g_b, relay, st_z, st_y, st_a, st_b, squares, columns, means, l_z, l_send, l_recv,
    in_sem, out_sem, direct_s, direct_r, fwd_s, fwd_r, far_s, far_r, rel_s, rel_r,
    stz_s, stz_r, sty_s, sty_r, stf_s, stf_r, rs_s, rs_r, y_s, y_r, hand_s, hand_r,
    ag_s, ag_r, ay_s, ay_r, lz_s, lz_r, loss_s, loss_r,
):
    rows, width = a_hbm.shape
    part = rows // PARTS
    band = rows // BANDS
    chunk = width // NZ
    half = chunk // 2
    total = float(rows * 2 * NZ)
    features = float(width * NF)

    batch = lax.axis_index("batch")
    feat = lax.axis_index("feat")
    z = lax.div(batch, 2)
    y_lo = lax.rem(batch, 2)
    y = lax.div(feat, 2 * NX) * 2 + y_lo
    x = lax.rem(lax.div(feat, 2), NX)
    core = lax.rem(feat, 2)
    even = core == 0
    odd = core == 1
    first_x = x == 0
    last_x = x == NX - 1
    seam = jnp.logical_or(first_x, last_x)

    def at_feat(f):
        return {"batch": batch, "feat": f}

    def at_z(z_other):
        return {"batch": z_other * 2 + y_lo, "feat": feat}

    def at_xy(x_other, y_other):
        f = lax.div(y_other, 2) * (2 * NX) + x_other * 2 + core
        return {"batch": z * 2 + lax.rem(y_other, 2), "feat": f}

    def neighbour(steps):
        return at_feat(mod(feat + steps, NF))

    def crossed(stride):
        return at_feat(feat + stride - 2 * stride * lax.rem(lax.div(feat, stride), 2))

    other_core = crossed(1)
    other_y = {"batch": batch + 1 - 2 * y_lo, "feat": feat}
    above = at_z(mod(z + 1, NZ))
    below = at_z(mod(z - 1, NZ))
    mirror_x = NX - 1 - x
    ahead_crossed = at_feat(mod(feat + 3 - 2 * core, NF))

    def send(src, dst, s_sem, r_sem, device):
        return pltpu.make_async_remote_copy(
            src_ref=src, dst_ref=dst, send_sem=s_sem, recv_sem=r_sem,
            device_id=device, device_id_type=MESH,
        )

    def landed(dst, r_sem, s_sem):
        send(dst, dst, s_sem, r_sem, other_core).wait_recv()

    load_b = pltpu.make_async_copy(b_hbm, raw_b.at[0], in_sem.at[0])
    load_a = pltpu.make_async_copy(a_hbm, raw_a.at[0], in_sem.at[1])
    load_b.start()
    load_a.start()

    barrier = pltpu.get_barrier_semaphore()
    friends = [neighbour(k) for k in (-3, -2, -1, 1, 2, 3)]
    friends += [crossed(k) for k in (2, 4, 8)]
    friends += [at_z(mod(z + d, NZ)) for d in range(1, NZ)]
    friends += [other_y]
    for friend in friends:
        pl.semaphore_signal(barrier, inc=1, device_id=friend, device_id_type=MESH)

    @pl.when(seam)
    def _():
        for friend in (
            at_xy(mirror_x, mod(y - 1, NY)), at_xy(mirror_x, mod(y + 1, NY)),
            at_xy(x, mod(y - 1, NY)), at_xy(x, mod(y + 1, NY)),
        ):
            pl.semaphore_signal(barrier, inc=1, device_id=friend, device_id_type=MESH)

    pl.semaphore_wait(barrier, jnp.where(seam, len(friends) + 4, len(friends)))


    def piece(c):
        return pl.ds(pl.multiple_of(c * part, part), part)

    def direct(view, c):
        src, raw, steps = ((a_hbm, raw_a, 2), (b_hbm, raw_b, -2))[view]
        return send(
            src.at[piece(c)], raw.at[1, piece(c)], direct_s.at[view, c], direct_r.at[view, c],
            neighbour(steps),
        )

    def to_relay(view, c):
        src = (a_hbm, b_hbm)[view]
        return send(
            src.at[piece(c)], relay.at[c - PARTS // 2], direct_s.at[view, c],
            rel_r.at[c - PARTS // 2], at_xy(mirror_x, mod(y - 1, NY)),
        )

    def from_relay(view, r):
        raw = (raw_a, raw_b)[view]
        c = r + PARTS // 2
        return send(
            relay.at[r], raw.at[1, piece(c)], rel_s.at[r], direct_r.at[view, c],
            at_xy(x, mod(y - 1, NY)),
        )

    for c in (0, 4, 1, 5, 2, 6, 3, 7):
        for view, edge in ((1, first_x), (0, last_x)):
            if c < PARTS // 2:
                direct(view, c).start()
            else:
                @pl.when(edge)
                def _():
                    to_relay(view, c).start()

                @pl.when(jnp.logical_not(edge))
                def _():
                    direct(view, c).start()

    def far_b(src):
        return send(src, raw_b.at[3], far_s.at[1], far_r.at[1], neighbour(-1))

    def far_a(src):
        return send(src, raw_a.at[3], far_s.at[0], far_r.at[0], neighbour(1))

    @pl.when(odd)
    def _():
        far_b(b_hbm).start()

    @pl.when(even)
    def _():
        far_a(a_hbm).start()

    load_b.wait()
    load_a.wait()
    strip = 128
    for view, raw in ((0, raw_a), (1, raw_b)):
        def add_up(i, acc):
            v = raw[0, pl.ds(pl.multiple_of(i * strip, strip), strip), :]
            return acc + jnp.sum(v.reshape(strip // 8, 8, width), axis=0)

        zeros = jnp.zeros((8, width), F32)
        acc = lax.fori_loop(0, rows // strip, add_up, zeros)
        mean = jnp.sum(acc, axis=0, keepdims=True) * (1.0 / rows)

        def add_up_squares(i, carry):
            rest, square = carry
            v = raw[0, pl.ds(pl.multiple_of(i * strip, strip), strip), :] - mean
            v = v.reshape(strip // 8, 8, width)
            return rest + jnp.sum(v, axis=0), square + jnp.sum(v * v, axis=0)

        rest, square = lax.fori_loop(0, rows // strip, add_up_squares, (zeros, zeros))
        st_z[z, pl.ds(3 * view, 1), :] = mean
        st_z[z, pl.ds(3 * view + 1, 1), :] = jnp.sum(square, axis=0, keepdims=True)
        st_z[z, pl.ds(3 * view + 2, 1), :] = jnp.sum(rest, axis=0, keepdims=True)

    def stat_z(d):
        return send(
            st_z.at[z], st_z.at[z], stz_s.at[d], stz_r.at[d], at_z(mod(z + d, NZ))
        )

    for d in range(1, NZ):
        stat_z(d).start()
    for d in range(1, NZ):
        landed(st_z.at[mod(z - d, NZ)], stz_r.at[d], stz_s.at[d])
    for view in (0, 1):
        means_z = [st_z[i, pl.ds(3 * view, 1), :] for i in range(NZ)]
        mean = sum(means_z[1:], means_z[0]) * (1.0 / NZ)
        square = jnp.zeros((1, width), F32)
        rest = jnp.zeros((1, width), F32)
        for i in range(NZ):
            off = means_z[i] - mean
            square = square + (st_z[i, pl.ds(3 * view + 1, 1), :] + float(rows) * off * off)
            rest = rest + (st_z[i, pl.ds(3 * view + 2, 1), :] + float(rows) * off)
        st_y[0, pl.ds(3 * view, 1), :] = mean
        st_y[0, pl.ds(3 * view + 1, 1), :] = square
        st_y[0, pl.ds(3 * view + 2, 1), :] = rest
    stat_y = send(st_y.at[0], st_y.at[1], sty_s, sty_r, other_y)
    stat_y.start()
    stat_y.wait_recv()
    rows_z = float(rows * NZ)
    for view, st in ((0, st_a), (1, st_b)):
        mean0, mean1 = (st_y[i, pl.ds(3 * view, 1), :] for i in (0, 1))
        mean = 0.5 * (mean0 + mean1)
        off0, off1 = mean0 - mean, mean1 - mean
        square = (
            st_y[0, pl.ds(3 * view + 1, 1), :] + st_y[1, pl.ds(3 * view + 1, 1), :]
            + rows_z * (off0 * off0 + off1 * off1)
        )
        rest = (
            st_y[0, pl.ds(3 * view + 2, 1), :] + st_y[1, pl.ds(3 * view + 2, 1), :]
            + rows_z * (off0 + off1)
        )
        inverse = 1.0 / jnp.sqrt(square * (1.0 / total) + eps)
        st[0, pl.ds(0, 1), :] = mean
        st[0, pl.ds(1, 1), :] = inverse
        st[0, pl.ds(2, 1), :] = rest * (1.0 / total) * inverse

    def stat_f(view, k):
        st = (st_a, st_b)[view]
        if k == 2:
            slot = 1
        elif (k == 1) == (view == 1):
            slot = 2 + core
        else:
            slot = 3 - core
        return send(
            st.at[0], st.at[slot], stf_s.at[view, k], stf_r.at[view, slot],
            neighbour(-k if view == 1 else k),
        )

    for k in (2, 1, 3):
        for view in (1, 0):
            stat_f(view, k).start()

    def normal(raw, st, slot, rows_here):
        return (raw[slot, rows_here, :] - st[slot, pl.ds(0, 1), :]) * st[slot, pl.ds(1, 1), :]

    def add_tile(t, c, left_hi, left_lo, first):
        right = (b_hi[...], b_lo[...])
        def rows_of(i, carry):
            here = pl.ds(pl.multiple_of(i * (width // 2), width // 2), width // 2)
            out = dot3((left_hi[c, here, :], left_lo[c, here, :]), right)
            if first:
                tiles[t, here, :] = out
            else:
                tiles[t, here, :] = tiles[t, here, :] + out
            return carry
        lax.fori_loop(0, 2, rows_of, 0)

    def band_of(c):
        return pl.ds(pl.multiple_of(c * band, band), band)

    def turn_a(slot, c, index):
        hi, lo = split(normal(raw_a, st_a, slot, band_of(c)).T)
        at_hi[index] = hi
        at_lo[index] = lo

    def take_b(slot, c):
        hi, lo = split(normal(raw_b, st_b, slot, band_of(c)))
        b_hi[...] = hi
        b_lo[...] = lo

    def clear(t, carry):
        tiles[t] = jnp.zeros((width, width), F32)
        return carry

    lax.fori_loop(0, 4, clear, 0)

    def own_tile(c, carry):
        turn_a(0, c, c)
        take_b(0, c)
        add_tile(0, c, at_hi, at_lo, False)
        return carry

    lax.fori_loop(0, BANDS, own_tile, 0)

    def dest(q):
        return pl.multiple_of(mod(q, NZ) * chunk, chunk)

    def sum_send(t, s):
        if s == 0:
            up = pl.ds(dest(z + HOPS), half)
            down = pl.ds(pl.multiple_of(dest(z + HOPS) + half, half), half)
            up_to, down_to = pl.ds(0, half), pl.ds(half, half)
        else:
            up, down = pl.ds(dest(z + HOPS - s), chunk), pl.ds(dest(z - HOPS + s), chunk)
            up_to = down_to = pl.ds(0, chunk)
        return (
            send(tiles.at[t, up], rs_p.at[t, s, up_to], rs_s.at[0, t, s], rs_r.at[0, t, s], above),
            send(tiles.at[t, down], rs_m.at[t, s, down_to], rs_s.at[1, t, s], rs_r.at[1, t, s], below),
        )

    def sum_start(t, s):
        for copy in sum_send(t, s):
            copy.start()

    def sum_take(t, s):
        for copy in sum_send(t, s):
            copy.wait_recv()
        for recv, q, low in ((rs_p, z + HOPS - 1 - s, 0), (rs_m, z - HOPS + 1 + s, half)):
            if s == 0:
                here = pl.ds(pl.multiple_of(dest(q) + low, half), half)
                tiles[t, here, :] = tiles[t, here, :] + recv[t, s, pl.ds(low, half), :]
            else:
                here = pl.ds(dest(q), chunk)
                tiles[t, here, :] = tiles[t, here, :] + recv[t, s]

    mine = pl.ds(dest(z), chunk)

    def y_copy(t):
        return send(tiles.at[t, mine], y_recv.at[t], y_s.at[t], y_r.at[t], other_y)

    def sum_end(t):
        sum_take(t, HOPS - 1)
        y_copy(t).start()

    def sum_all(t):
        y_copy(t).wait_recv()
        return (tiles[t, mine, :] + y_recv[t]) * (1.0 / total)

    def gather_part(s, mover):
        up, down = z - s - mover, z + s + mover
        if s < HOPS - 1:
            return pl.ds(dest(up), chunk), pl.ds(dest(down), chunk)
        return pl.ds(dest(up), half), pl.ds(pl.multiple_of(dest(down) + half, half), half)

    def gather_send(lane, u, s):
        up, down = gather_part(s, 0)
        return (
            send(cfull.at[u, up], cfull.at[u, up], ag_s.at[0, lane, s], ag_r.at[0, lane, s], above),
            send(cfull.at[u, down], cfull.at[u, down], ag_s.at[1, lane, s], ag_r.at[1, lane, s], below),
        )

    def gather_start(lane, u, s):
        for copy in gather_send(lane, u, s):
            copy.start()

    def across(lane, u, s, i):
        p = gather_part(s, 1)[i]
        return send(cfull.at[u, p], cfull.at[u, p], ay_s.at[i, lane, s], ay_r.at[i, lane, s], other_y)

    def gather_take(lane, u, s):
        for i, p in enumerate(gather_part(s, 1)):
            landed(cfull.at[u, p], ag_r.at[i, lane, s], ag_s.at[i, lane, s])
            if lane < 2:
                across(lane, u, s, i).start()
        if s < HOPS - 1:
            gather_start(lane, u, s + 1)

    def gather_other(lane, u):
        for s in range(HOPS):
            for i in (0, 1):
                across(lane, u, s, i).wait_recv()

    lane_tile = (1 + y_lo, 4 + y_lo, 0, 3 + 3 * core, 6 - 3 * core)
    other_tile = (2 - y_lo, 5 - y_lo)

    def gather(lane, s):
        if s < 0:
            gather_start(lane, lane_tile[lane], 0)
        else:
            gather_take(lane, lane_tile[lane], s)

    hand1 = send(cfull.at[1, mine], cfull.at[4, mine], hand_s.at[0], hand_r.at[4], neighbour(2))
    hand2 = send(cfull.at[2, mine], cfull.at[5, mine], hand_s.at[1], hand_r.at[5], ahead_crossed)
    hand3 = send(fin, cfull.at[3, mine], hand_s.at[2], hand_r.at[3], neighbour(-1))
    hand6 = send(fin, cfull.at[6, mine], hand_s.at[3], hand_r.at[6], neighbour(2))

    def hand_take(u):
        landed(cfull.at[u, mine], hand_r.at[u], hand_s.at[0])

    def when(cond, f, *args):
        @pl.when(cond)
        def _():
            f(*args)

    def sum_step(t, s):
        if s < HOPS - 1:
            sum_take(t, s)
            sum_start(t, s + 1)
        else:
            sum_end(t)

    def end_0():
        cfull[0, mine, :] = sum_all(0)

    def end_1():
        cfull[1, mine, :] = sum_all(1)
        hand1.start()

    def end_2():
        cfull[2, mine, :] = sum_all(2)
        hand2.start()

    def end_3_odd():
        last = sum_all(3)
        fin[...] = last
        hand3.start()
        cfull[6, mine, :] = last

    def end_3_even():
        fin[...] = sum_all(3)
        hand3.start()
        hand6.start()

    def forward(view, c):
        raw = (raw_a, raw_b)[view]
        return send(
            raw.at[1, piece(c)], raw.at[2, piece(c)], fwd_s.at[view, c], fwd_r.at[view, c],
            other_core,
        )

    sum_start(0, 0)
    for slot in (3, 1, 2):
        for view, st in ((1, st_b), (0, st_a)):
            landed(st.at[slot], stf_r.at[view, slot], stf_s.at[view, slot])

    @pl.when(odd)
    def _():
        far_a(a_hbm).wait_recv()

        def fourth_tile(c, carry):
            turn_a(3, c, BANDS)
            take_b(0, c)
            add_tile(3, BANDS, at_hi, at_lo, False)
            return carry

        lax.fori_loop(0, BANDS, fourth_tile, 0)
        sum_start(3, 0)

    def early(j):
        if j < HOPS:
            sum_step(0, j)
            when(odd, sum_step, 3, j)
        elif j == 4:
            end_0()
            gather(2, -1)
            when(odd, end_3_odd)
        elif j == 5:
            gather(2, 0)
            when(even, hand_take, 3)
            gather(3, -1)
        else:
            gather(2, j - 5)
            gather(3, j - 6)

    for c in range(BANDS):
        for j in (2 * c, 2 * c + 1):
            if j < PARTS // 2:
                for view, edge in ((1, last_x), (0, first_x)):
                    @pl.when(edge)
                    def _():
                        landed(relay.at[j], rel_r.at[j], rel_s.at[j])
                        from_relay(view, j).start()

            for view in (1, 0):
                direct(view, j).wait_recv()
                forward(view, j).start()
            early(j)
        take_b(1, c)
        add_tile(1, c, at_hi, at_lo, False)

        @pl.when(even)
        def _():
            for j in (2 * c, 2 * c + 1):
                forward(0, j).wait_recv()
            turn_a(2, c, BANDS)
            add_tile(3, BANDS, at_hi, at_lo, False)

        for j in (2 * c, 2 * c + 1):
            forward(1, j).wait_recv()
        take_b(2, c)
        add_tile(2, c, at_hi, at_lo, False)

    @pl.when(odd)
    def _():
        for j in range(PARTS):
            forward(0, j).wait_recv()

    for t in (1, 2):
        sum_start(t, 0)
    when(even, sum_start, 3, 0)
    when(even, far_b(raw_b.at[1]).start)
    when(odd, far_a(raw_a.at[1]).start)

    squares[...] = jnp.zeros_like(squares)
    columns[...] = jnp.zeros_like(columns)
    means[...] = jnp.zeros_like(means)

    def clear_g(i, carry):
        g_a[band_of(i), :] = jnp.zeros((band, width), F32)
        g_b[band_of(i), :] = jnp.zeros((band, width), F32)
        return carry

    lax.fori_loop(0, BANDS, clear_g, 0)

    def grow(view, slot, u):
        g, raw, st = ((g_a, raw_b, st_b), (g_b, raw_a, st_a))[view]
        c = cfull[u]
        hi, lo = split(c)
        c_hi[...] = hi
        c_lo[...] = lo
        if view == 0:
            acc = squares[...]
            for j in range(width // 128):
                part_j = c[:, j * 128:(j + 1) * 128]
                acc = acc + part_j * part_j
            squares[...] = acc
        else:
            columns[...] = columns[...] + jnp.sum((c * c).reshape(width // 8, 8, width), axis=0)

        def body(i, carry):
            here = band_of(i)
            n = split(normal(raw, st, slot, here))
            g[here, :] = g[here, :] + dot3(n, (c_hi[...], c_lo[...]), view == 0)
            return carry

        lax.fori_loop(0, BANDS, body, 0)
        m = split(jnp.broadcast_to(st[slot, pl.ds(2, 1), :], (16, width)))
        means[view] = means[view] + dot3(m, (c_hi[...], c_lo[...]), view == 0)

    def loss_part():
        value = jnp.zeros((8, 128), F32)
        for t in range(4):
            c = fin[...] if t == 3 else cfull[t, mine, :]
            terms = off_weight * c * c
            if t == 0:
                shape = (chunk, width)
                on = lax.broadcasted_iota(jnp.int32, shape, 1) == (
                    lax.broadcasted_iota(jnp.int32, shape, 0) + z * chunk
                )
                terms = jnp.where(on, (1.0 - c) * (1.0 - c), terms)
            terms = jnp.sum(terms.reshape(chunk // 8, 8, width), axis=0)
            for j in range(width // 128):
                value = value + terms[:, j * 128:(j + 1) * 128]
        l_z[z] = value

    def loss_z(d):
        return send(l_z.at[z], l_z.at[z], lz_s.at[d], lz_r.at[d], at_z(mod(z + d, NZ)))

    def loss_copy(r):
        return send(l_send.at[r], l_recv.at[r], loss_s.at[r], loss_r.at[r], crossed(1 << r))

    def loss_start():
        for d in range(1, NZ):
            landed(l_z.at[mod(z - d, NZ)], lz_r.at[d], lz_s.at[d])
        value = l_z[0]
        for i in range(1, NZ):
            value = value + l_z[i]
        l_send[0] = value
        loss_copy(0).start()

    def loss_step(r):
        loss_copy(r).wait_recv()
        l_send[r + 1] = l_send[r] + l_recv[r]
        if r < 3:
            loss_copy(r + 1).start()

    gather(2, 3)
    gather(3, 2)
    grow(0, 0, 0)
    gather(3, 3)
    for t in (1, 2):
        sum_step(t, 0)
    when(even, sum_step, 3, 0)
    grow(1, 0, 0)
    for t in (1, 2):
        sum_step(t, 1)
    when(even, sum_step, 3, 1)
    far_b_here = far_b(raw_b.at[1])
    far_a_here = far_a(raw_a.at[1])

    @pl.when(even)
    def _():
        far_b_here.wait_recv()
        grow(0, 3, 3)

    when(odd, grow, 1, 3, 6)
    for s in (2, 3):
        for t in (1, 2):
            sum_step(t, s)
        when(even, sum_step, 3, s)
    end_1()
    end_2()
    gather(0, -1)
    when(even, end_3_even)
    loss_part()
    for d in range(1, NZ):
        loss_z(d).start()
    hand_take(4)
    hand_take(5)
    gather(1, -1)
    gather(0, 0)
    when(even, hand_take, 6)
    when(odd, hand_take, 3)
    gather(4, -1)
    gather(1, 0)
    gather(0, 1)
    gather(4, 0)
    gather(1, 1)
    gather(0, 2)
    loss_start()
    gather(4, 1)
    gather(1, 2)
    gather(0, 3)
    grow(0, 1 + y_lo, lane_tile[0])
    loss_step(0)
    gather(4, 2)
    gather(1, 3)
    grow(1, 1 + y_lo, lane_tile[1])
    loss_step(1)
    gather(4, 3)
    gather_other(0, other_tile[0])
    grow(0, 2 - y_lo, other_tile[0])
    loss_step(2)
    gather_other(1, other_tile[1])
    grow(1, 2 - y_lo, other_tile[1])
    loss_step(3)

    @pl.when(odd)
    def _():
        far_b_here.wait_recv()
        grow(0, 3, 3)

    @pl.when(even)
    def _():
        far_a_here.wait_recv()
        grow(1, 3, 6)

    loss_ref[0, 0] = jnp.sum(l_send[4]) * (1.0 / features)

    diagonal = []
    one_block = (
        lax.broadcasted_iota(jnp.int32, (128, 128), 0) == lax.broadcasted_iota(jnp.int32, (128, 128), 1)
    )
    for j in range(width // 128):
        block = cfull[0, j * 128:(j + 1) * 128, j * 128:(j + 1) * 128]
        diagonal.append(jnp.sum(jnp.where(one_block, block, 0.0), axis=0, keepdims=True))
    diagonal = jnp.concatenate(diagonal, axis=1)
    change = -(1.0 - diagonal) - off_weight * diagonal
    row_squares = jnp.sum(squares[...].T, axis=0, keepdims=True)
    column_squares = jnp.sum(columns[...], axis=0, keepdims=True)
    back_a = off_weight * row_squares + change * diagonal
    back_b = off_weight * column_squares + change * diagonal
    mean_a = off_weight * means[0, pl.ds(0, 1), :] + st_b[0, pl.ds(2, 1), :] * change
    mean_b = off_weight * means[1, pl.ds(0, 1), :] + st_a[0, pl.ds(2, 1), :] * change

    def out_copy(view, i):
        src, dst = ((g_a, ga_hbm), (g_b, gb_hbm))[view]
        return pltpu.make_async_copy(src.at[band_of(i)], dst.at[band_of(i)], out_sem.at[view, i])

    def finish(i, carry):
        here = band_of(i)
        n_a = normal(raw_a, st_a, 0, here)
        n_b = normal(raw_b, st_b, 0, here)
        g_a[here, :] = (off_weight * g_a[here, :] + n_b * change - mean_a - n_a * back_a) * st_a[0, pl.ds(1, 1), :]
        out_copy(0, i).start()
        g_b[here, :] = (off_weight * g_b[here, :] + n_a * change - mean_b - n_b * back_b) * st_b[0, pl.ds(1, 1), :]
        out_copy(1, i).start()
        return carry

    lax.fori_loop(0, BANDS, finish, 0)

    for view, edge in ((1, first_x), (0, last_x)):
        for c in range(PARTS):
            direct(view, c).wait_send()
            forward(view, c).wait_send()
    far_a(a_hbm).wait_send()
    far_b(b_hbm).wait_send()

    @pl.when(seam)
    def _():
        for r in range(PARTS // 2):
            from_relay(0, r).wait_send()

    for d in range(1, NZ):
        stat_z(d).wait_send()
    stat_y.wait_send()
    for k in (1, 2, 3):
        for view in (0, 1):
            stat_f(view, k).wait_send()
    for t in range(4):
        for s in range(HOPS):
            for copy in sum_send(t, s):
                copy.wait_send()
        y_copy(t).wait_send()
    hand1.wait_send()
    hand2.wait_send()
    hand3.wait_send()

    @pl.when(even)
    def _():
        hand6.wait_send()

    for lane in range(5):
        for s in range(HOPS):
            for copy in gather_send(lane, lane_tile[lane], s):
                copy.wait_send()
            if lane < 2:
                for i in (0, 1):
                    across(lane, lane_tile[lane], s, i).wait_send()
    for d in range(1, NZ):
        loss_z(d).wait_send()
    for r in range(4):
        loss_copy(r).wait_send()
    for view in (0, 1):
        for i in range(BANDS):
            out_copy(view, i).wait()


def local(view_a, view_b):
    rows, width = view_a.shape
    part = rows // PARTS
    band = rows // BANDS
    chunk = width // NZ
    dma = pltpu.SemaphoreType.DMA
    anywhere = pl.BlockSpec(memory_space=pl.ANY)
    grad_a, grad_b, loss = pl.pallas_call(
        kernel,
        out_shape=(
            jax.ShapeDtypeStruct((rows, width), F32),
            jax.ShapeDtypeStruct((rows, width), F32),
            jax.ShapeDtypeStruct((1, 1), F32),
        ),
        in_specs=[anywhere, anywhere],
        out_specs=(anywhere, anywhere, pl.BlockSpec(memory_space=pltpu.SMEM)),
        scratch_shapes=[
            pltpu.VMEM((4, rows, width), F32),
            pltpu.VMEM((4, rows, width), F32),
            pltpu.VMEM((BANDS + 1, width, band), BF16),
            pltpu.VMEM((BANDS + 1, width, band), BF16),
            pltpu.VMEM((band, width), BF16),
            pltpu.VMEM((band, width), BF16),
            pltpu.VMEM((4, width, width), F32),
            pltpu.VMEM((4, HOPS, chunk, width), F32),
            pltpu.VMEM((4, HOPS, chunk, width), F32),
            pltpu.VMEM((4, chunk, width), F32),
            pltpu.VMEM((chunk, width), F32),
            pltpu.VMEM((7, width, width), F32),
            pltpu.VMEM((width, width), BF16),
            pltpu.VMEM((width, width), BF16),
            pltpu.VMEM((rows, width), F32),
            pltpu.VMEM((rows, width), F32),
            pltpu.VMEM((PARTS // 2, part, width), F32),
            pltpu.VMEM((NZ, 8, width), F32),
            pltpu.VMEM((2, 8, width), F32),
            pltpu.VMEM((4, 8, width), F32),
            pltpu.VMEM((4, 8, width), F32),
            pltpu.VMEM((width, 128), F32),
            pltpu.VMEM((8, width), F32),
            pltpu.VMEM((2, 16, width), F32),
            pltpu.VMEM((NZ, 8, 128), F32),
            pltpu.VMEM((5, 8, 128), F32),
            pltpu.VMEM((4, 8, 128), F32),
            dma((2,)),
            dma((2, BANDS)),
            dma((2, PARTS)), dma((2, PARTS)),
            dma((2, PARTS)), dma((2, PARTS)),
            dma((2,)), dma((2,)),
            dma((PARTS // 2,)), dma((PARTS // 2,)),
            dma((NZ,)), dma((NZ,)),
            dma(()), dma(()),
            dma((2, 4)), dma((2, 4)),
            dma((2, 4, HOPS)), dma((2, 4, HOPS)),
            dma((4,)), dma((4,)),
            dma((4,)), dma((7,)),
            dma((2, 5, HOPS)), dma((2, 5, HOPS)),
            dma((2, 2, HOPS)), dma((2, 2, HOPS)),
            dma((NZ,)), dma((NZ,)),
            dma((4,)), dma((4,)),
        ],
        compiler_params=pltpu.CompilerParams(
            collective_id=0, has_side_effects=True, vmem_limit_bytes=60 * 1024 * 1024
        ),
        cost_estimate=pl.CostEstimate(
            flops=2 * 3 * 12 * rows * width * width, bytes_accessed=16 * rows * width, transcendentals=0
        ),
    )(view_a, view_b)
    return grad_a, grad_b, loss[0, 0]


def solution(mesh):
    spec = P("batch", "feat")
    return jax.shard_map(
        local, mesh=mesh, in_specs=(spec, spec), out_specs=(spec, spec, P()), check_vma=False
    )
```

```python
import functools

import jax
import jax.numpy as jnp
from jax import lax
from jax.experimental import pallas as pl
from jax.experimental.pallas import tpu as pltpu
from jax.sharding import PartitionSpec as P

MESH = pl.DeviceIdType.MESH
F32 = jnp.float32
BF16 = jnp.bfloat16

eps = 1e-05
off_weight = 0.25

NZ = 8
NX = 4
NY = 4
NF = 16
PARTS = 8
BANDS = 4
HOPS = 4
AHEAD = 3

ORDER = (
    "OWN", "R0", "S0_0", "P0", "T3O", "C00", "S0_1", "S3o_0", "P1", "P2", "S0_2", "C01", "S3o_1",
    "R1", "C02", "S0_3", "S3o_2", "R2", "S0_4", "S3o_3", "P3", "P4", "F0", "G0_0", "S3o_4", "C03",
    "S10_0", "C10", "P5", "S20_0", "G0_1", "S10_1", "S20_1", "C11", "R3", "G0_2", "P6", "S10_2",
    "F3o", "S20_2", "GE_0", "C12", "G0_3", "P7", "LT0", "S10_3", "LT1", "S20_3", "GE_1", "C31",
    "C32", "C30", "RL0", "C33", "S3e_0", "S20_4", "GE_2", "S10_4", "C13", "S11_0", "S21_0", "S3e_1",
    "LT2", "LT3", "F20", "GE_3", "G0_4", "S11_1", "Wb0", "S21_1", "S3e_2", "F10", "GA0_0", "Wa0",
    "S21_2", "S3e_3", "S11_2", "RL1", "GE_4", "GA0_1", "S21_3", "WE", "GD0_0", "S11_3", "GA0_2",
    "S3e_4", "S21_4", "GC0_0", "GD0_1", "S11_4", "GA0_3", "GC0_1", "GD0_2", "F3e", "GA0_4", "F21",
    "GC0_2", "F11", "X0", "GA1_0", "GD0_3", "GC0_3", "X1", "GA1_1", "GD0_4", "GC0_4", "GL_0", "X2",
    "GA1_2", "X3", "X4", "GD1_0", "GL_1", "X5", "GA1_3", "GC1_0", "GD1_1", "GL_2", "GA1_4", "WA",
    "GC1_1", "GD1_2", "GL_3", "WO", "GC1_2", "GD1_3", "GL_4", "WL", "GD1_4", "GC1_3", "WD", "GC1_4",
    "WC", "END",
)


def mod(value, n):
    return lax.rem(value + n, n)


def split(value):
    hi = value.astype(BF16)
    return hi, (value - hi.astype(F32)).astype(BF16)


def dot3(left, right, transposed=False):
    dims = (((1,), (1 if transposed else 0,)), ((), ()))
    dot = functools.partial(lax.dot_general, dimension_numbers=dims, preferred_element_type=F32)
    return dot(left[0], right[0]) + dot(left[0], right[1]) + dot(left[1], right[0])


def kernel(
    a_hbm, b_hbm, ga_hbm, gb_hbm, loss_ref,
    raw_a, raw_b, at_hi, at_lo, b_hi, b_lo, tiles, rs_p, rs_m, y_recv, fin, cfull, c_hi, c_lo,
    g_a, g_b, relay_a, relay_b, relay_far, st_z, st_y, st_a, st_b, squares, columns, means, l_z, l_send, l_recv,
    in_sem, out_sem, direct_s, direct_r, fwd_s, fwd_r, far_s, far_r, rel_s, rel_r, rel_far_s, rel_far_r,
    stz_s, stz_r, sty_s, sty_r, stf_s, stf_r, rs_s, rs_r, y_s, y_r, hand_s, hand_r,
    ag_s, ag_r, ay_s, ay_r, ae_s, ae_r, lz_s, lz_r, loss_s, loss_r,
):
    rows, width = a_hbm.shape
    part = rows // PARTS
    band = rows // BANDS
    chunk = width // NZ
    half = chunk // 2
    total = float(rows * 2 * NZ)
    features = float(width * NF)

    batch = lax.axis_index("batch")
    feat = lax.axis_index("feat")
    z = lax.div(batch, 2)
    y_lo = lax.rem(batch, 2)
    y = lax.div(feat, 2 * NX) * 2 + y_lo
    x = lax.rem(lax.div(feat, 2), NX)
    core = lax.rem(feat, 2)
    even = core == 0
    odd = core == 1
    first_x = x == 0
    last_x = x == NX - 1
    seam = jnp.logical_or(first_x, last_x)

    def at_feat(f):
        return {"batch": batch, "feat": f}

    def at_z(z_other):
        return {"batch": z_other * 2 + y_lo, "feat": feat}

    def at_xy(x_other, y_other, core_other):
        f = lax.div(y_other, 2) * (2 * NX) + x_other * 2 + core_other
        return {"batch": z * 2 + lax.rem(y_other, 2), "feat": f}

    def neighbour(steps):
        return at_feat(mod(feat + steps, NF))

    def crossed(stride):
        return at_feat(feat + stride - 2 * stride * lax.rem(lax.div(feat, stride), 2))

    other_core = crossed(1)
    other_y = {"batch": batch + 1 - 2 * y_lo, "feat": feat}
    above = at_z(mod(z + 1, NZ))
    below = at_z(mod(z - 1, NZ))
    mirror_x = NX - 1 - x
    ahead_crossed = at_feat(mod(feat + 3 - 2 * core, NF))

    def send(src, dst, s_sem, r_sem, device):
        return pltpu.make_async_remote_copy(
            src_ref=src, dst_ref=dst, send_sem=s_sem, recv_sem=r_sem,
            device_id=device, device_id_type=MESH,
        )

    def landed(dst, r_sem, s_sem):
        send(dst, dst, s_sem, r_sem, other_core).wait_recv()

    load_b = pltpu.make_async_copy(b_hbm, raw_b.at[0], in_sem.at[0])
    load_a = pltpu.make_async_copy(a_hbm, raw_a.at[0], in_sem.at[1])
    load_b.start()
    load_a.start()

    barrier = pltpu.get_barrier_semaphore()
    friends = [neighbour(k) for k in (-3, -2, -1, 1, 2, 3)]
    friends += [crossed(k) for k in (2, 4, 8)]
    friends += [at_z(mod(z + d, NZ)) for d in range(1, NZ)]
    friends += [other_y]
    for friend in friends:
        pl.semaphore_signal(barrier, inc=1, device_id=friend, device_id_type=MESH)

    @pl.when(seam)
    def _():
        for friend in (
            at_xy(mirror_x, mod(y - 1, NY), core), at_xy(mirror_x, mod(y + 1, NY), core),
            at_xy(x, mod(y - 1, NY), core), at_xy(x, mod(y + 1, NY), core),
            at_xy(x, mod(y - 1, NY), 1 - core), at_xy(x, mod(y + 1, NY), 1 - core),
        ):
            pl.semaphore_signal(barrier, inc=1, device_id=friend, device_id_type=MESH)

    pl.semaphore_wait(barrier, jnp.where(seam, len(friends) + 6, len(friends)))


    def band_of(c):
        return pl.ds(pl.multiple_of(c * band, band), band)

    def span(i, size):
        return pl.ds(pl.multiple_of(i * size, size), size)

    halves = (pl.ds(0, width // 2), pl.ds(width // 2, width // 2))

    def piece(view, j):
        if view == 0:
            return span(j, part), pl.ds(0, width)
        return span(j % BANDS, band), halves[j // BANDS]

    raws = (raw_a, raw_b)
    relays = (relay_a, relay_b)

    def direct(view, j):
        src, raw, steps = ((a_hbm, raw_a, 2), (b_hbm, raw_b, -2))[view]
        return send(
            src.at[piece(view, j)], raw.at[1, *piece(view, j)], direct_s.at[view, j], direct_r.at[view, j],
            neighbour(steps),
        )

    def to_relay(view, j):
        src = (a_hbm, b_hbm)[view]
        return send(
            src.at[piece(view, j)], relays[view].at[j // 2], direct_s.at[view, j], rel_r.at[view, j // 2],
            at_xy(mirror_x, mod(y - 1, NY), core),
        )

    def from_relay(view, r):
        j = 2 * r + 1
        return send(
            relays[view].at[r], raws[view].at[1, *piece(view, j)], rel_s.at[view, r], direct_r.at[view, j],
            at_xy(x, mod(y - 1, NY), core),
        )

    leaves = (last_x, first_x)
    enters = (first_x, last_x)

    def when(cond, f, *args):
        @pl.when(cond)
        def _():
            f(*args)

    def piece_start(j):
        for view in (1, 0):
            if j % 2 == 0:
                direct(view, j).start()
            else:
                @pl.when(leaves[view])
                def _():
                    to_relay(view, j).start()

                @pl.when(jnp.logical_not(leaves[view]))
                def _():
                    direct(view, j).start()

    for j in range(AHEAD):
        piece_start(j)

    def far(view, j, src=None):
        raw = raws[view]
        src = raw.at[1] if src is None else src
        return send(
            src.at[band_of(j)], raw.at[3, band_of(j)], far_s.at[view, j], far_r.at[view, j],
            neighbour(1 - 2 * view),
        )

    def far_to_relay(view, j):
        return send(
            raws[view].at[1, band_of(j)], relay_far.at[j // 2], far_s.at[view, j], rel_far_r.at[j // 2],
            at_xy(mirror_x, mod(y - 1, NY), core),
        )

    def far_from_relay(view, r):
        j = 2 * r + 1
        return send(
            relay_far.at[r], raws[view].at[3, band_of(j)], rel_far_s.at[r], far_r.at[view, j],
            at_xy(x, mod(y - 1, NY), 1 - core),
        )

    for j in range(BANDS):
        when(odd, lambda: far(1, j, b_hbm).start())
        when(even, lambda: far(0, j, a_hbm).start())

    load_b.wait()
    load_a.wait()
    strip = 128
    for view, raw in ((0, raw_a), (1, raw_b)):
        def add_up(i, acc):
            v = raw[0, pl.ds(pl.multiple_of(i * strip, strip), strip), :]
            return acc + jnp.sum(v.reshape(strip // 8, 8, width), axis=0)

        zeros = jnp.zeros((8, width), F32)
        acc = lax.fori_loop(0, rows // strip, add_up, zeros)
        mean = jnp.sum(acc, axis=0, keepdims=True) * (1.0 / rows)

        def add_up_squares(i, carry):
            rest, square = carry
            v = raw[0, pl.ds(pl.multiple_of(i * strip, strip), strip), :] - mean
            v = v.reshape(strip // 8, 8, width)
            return rest + jnp.sum(v, axis=0), square + jnp.sum(v * v, axis=0)

        rest, square = lax.fori_loop(0, rows // strip, add_up_squares, (zeros, zeros))
        st_z[z, pl.ds(3 * view, 1), :] = mean
        st_z[z, pl.ds(3 * view + 1, 1), :] = jnp.sum(square, axis=0, keepdims=True)
        st_z[z, pl.ds(3 * view + 2, 1), :] = jnp.sum(rest, axis=0, keepdims=True)

    def stat_z(d):
        return send(
            st_z.at[z], st_z.at[z], stz_s.at[d], stz_r.at[d], at_z(mod(z + d, NZ))
        )

    for d in range(1, NZ):
        stat_z(d).start()
    for d in range(1, NZ):
        landed(st_z.at[mod(z - d, NZ)], stz_r.at[d], stz_s.at[d])
    for view in (0, 1):
        means_z = [st_z[i, pl.ds(3 * view, 1), :] for i in range(NZ)]
        mean = sum(means_z[1:], means_z[0]) * (1.0 / NZ)
        square = jnp.zeros((1, width), F32)
        rest = jnp.zeros((1, width), F32)
        for i in range(NZ):
            off = means_z[i] - mean
            square = square + (st_z[i, pl.ds(3 * view + 1, 1), :] + float(rows) * off * off)
            rest = rest + (st_z[i, pl.ds(3 * view + 2, 1), :] + float(rows) * off)
        st_y[0, pl.ds(3 * view, 1), :] = mean
        st_y[0, pl.ds(3 * view + 1, 1), :] = square
        st_y[0, pl.ds(3 * view + 2, 1), :] = rest
    stat_y = send(st_y.at[0], st_y.at[1], sty_s, sty_r, other_y)
    stat_y.start()
    stat_y.wait_recv()
    rows_z = float(rows * NZ)
    for view, st in ((0, st_a), (1, st_b)):
        mean0, mean1 = (st_y[i, pl.ds(3 * view, 1), :] for i in (0, 1))
        mean = 0.5 * (mean0 + mean1)
        off0, off1 = mean0 - mean, mean1 - mean
        square = (
            st_y[0, pl.ds(3 * view + 1, 1), :] + st_y[1, pl.ds(3 * view + 1, 1), :]
            + rows_z * (off0 * off0 + off1 * off1)
        )
        rest = (
            st_y[0, pl.ds(3 * view + 2, 1), :] + st_y[1, pl.ds(3 * view + 2, 1), :]
            + rows_z * (off0 + off1)
        )
        inverse = 1.0 / jnp.sqrt(square * (1.0 / total) + eps)
        st[0, pl.ds(0, 1), :] = mean
        st[0, pl.ds(1, 1), :] = inverse
        st[0, pl.ds(2, 1), :] = rest * (1.0 / total) * inverse

    def stat_f(view, k):
        st = (st_a, st_b)[view]
        if k == 2:
            slot = 1
        elif (k == 1) == (view == 1):
            slot = 2 + core
        else:
            slot = 3 - core
        return send(
            st.at[0], st.at[slot], stf_s.at[view, k], stf_r.at[view, slot],
            neighbour(-k if view == 1 else k),
        )

    for k in (2, 1, 3):
        for view in (1, 0):
            stat_f(view, k).start()

    def normal(raw, st, slot, rows_here, cols=slice(None)):
        return (raw[slot, rows_here, cols] - st[slot, pl.ds(0, 1), cols]) * st[slot, pl.ds(1, 1), cols]

    def products(c, store):
        def rows_of(i, carry):
            here = span(i, width // 2)
            store(here, dot3((at_hi[c, here, :], at_lo[c, here, :]), (b_hi[...], b_lo[...])))
            return carry
        lax.fori_loop(0, 2, rows_of, 0)

    def add_tile(t, c):
        def store(here, out):
            tiles[t, here, :] = tiles[t, here, :] + out
        products(c, store)

    def add_halves(h, c):
        cols, mid = halves[h], width // 2
        def store(here, out):
            tiles[1, here, cols] = tiles[1, here, cols] + out[:, :mid]
            tiles[2, here, cols] = tiles[2, here, cols] + out[:, mid:]
        products(c, store)

    def turn_a(slot, c, index):
        hi, lo = split(normal(raw_a, st_a, slot, band_of(c)).T)
        at_hi[index] = hi
        at_lo[index] = lo

    def take_b(slot, c):
        hi, lo = split(normal(raw_b, st_b, slot, band_of(c)))
        b_hi[...] = hi
        b_lo[...] = lo

    def take_halves(h, c):
        for slot in (1, 2):
            hi, lo = split(normal(raw_b, st_b, slot, band_of(c), halves[h]))
            b_hi[:, halves[slot - 1]] = hi
            b_lo[:, halves[slot - 1]] = lo

    def clear(t, carry):
        tiles[t] = jnp.zeros((width, width), F32)
        return carry

    lax.fori_loop(0, 4, clear, 0)

    def own_tile(c, carry):
        turn_a(0, c, c)
        take_b(0, c)
        add_tile(0, c)
        return carry

    def dest(q):
        return pl.multiple_of(mod(q, NZ) * chunk, chunk)

    whole = pl.ds(0, width)
    units = {"0": (0, whole), "3o": (3, whole), "3e": (3, whole)}
    for h in (0, 1):
        units["1%d" % h] = (1, halves[h])
        units["2%d" % h] = (2, halves[h])
    unit_sem = {"0": 0, "10": 1, "11": 2, "20": 3, "21": 4, "3o": 5, "3e": 5}

    def sum_send(unit, s):
        (t, cols), i = units[unit], unit_sem[unit]
        if s == 0:
            up = pl.ds(dest(z + HOPS), half)
            down = pl.ds(pl.multiple_of(dest(z + HOPS) + half, half), half)
            up_to, down_to = pl.ds(0, half), pl.ds(half, half)
        else:
            up, down = pl.ds(dest(z + HOPS - s), chunk), pl.ds(dest(z - HOPS + s), chunk)
            up_to = down_to = pl.ds(0, chunk)
        return (
            send(tiles.at[t, up, cols], rs_p.at[t, s, up_to, cols], rs_s.at[0, i, s], rs_r.at[0, i, s], above),
            send(tiles.at[t, down, cols], rs_m.at[t, s, down_to, cols], rs_s.at[1, i, s], rs_r.at[1, i, s], below),
        )

    def sum_start(unit, s):
        for copy in sum_send(unit, s):
            copy.start()

    def sum_take(unit, s):
        t, cols = units[unit]
        for copy in sum_send(unit, s):
            copy.wait_recv()
        for recv, q, low in ((rs_p, z + HOPS - 1 - s, 0), (rs_m, z - HOPS + 1 + s, half)):
            if s == 0:
                here = pl.ds(pl.multiple_of(dest(q) + low, half), half)
                tiles[t, here, cols] = tiles[t, here, cols] + recv[t, s, pl.ds(low, half), cols]
            else:
                here = pl.ds(dest(q), chunk)
                tiles[t, here, cols] = tiles[t, here, cols] + recv[t, s, :, cols]

    mine = pl.ds(dest(z), chunk)

    def y_copy(unit):
        (t, cols), i = units[unit], unit_sem[unit]
        return send(tiles.at[t, mine, cols], y_recv.at[t, :, cols], y_s.at[i], y_r.at[i], other_y)

    def sum_step(unit, s):
        if s > 0:
            sum_take(unit, s - 1)
        if s < HOPS:
            sum_start(unit, s)
        else:
            y_copy(unit).start()

    def sum_all(unit):
        t, cols = units[unit]
        y_copy(unit).wait_recv()
        return (tiles[t, mine, cols] + y_recv[t, :, cols]) * (1.0 / total)

    def hand(u, h=0):
        if u in (4, 5):
            src = cfull.at[u - 3, mine, halves[h]]
            dst = cfull.at[u, mine, halves[h]]
            device = neighbour(2) if u == 4 else ahead_crossed
        else:
            src, dst = fin, cfull.at[u, mine]
            device = neighbour(-1 if u == 3 else 2)
        return send(src, dst, hand_s.at[u, h], hand_r.at[u, h], device)

    def finish_sum(unit):
        value = sum_all(unit)
        t, cols = units[unit]
        if t < 3:
            cfull[t, mine, cols] = value
            if t > 0:
                hand(t + 3, int(unit[1])).start()
        else:
            fin[...] = value
            hand(3).start()
            if unit == "3o":
                cfull[6, mine, :] = value
            else:
                hand(6).start()

    def gather_part(s, mover):
        up, down = z - s - mover, z + s + mover
        if s < HOPS - 1:
            return pl.ds(dest(up), chunk), pl.ds(dest(down), chunk)
        return pl.ds(dest(up), half), pl.ds(pl.multiple_of(dest(down) + half, half), half)

    lanes = {"0": (0, 0, whole), "E": (1, 6, whole), "L": (2, 6 - 3 * core, whole)}
    for h in (0, 1):
        lanes["A%d" % h] = (3 + h, 1 + y_lo, halves[h])
        lanes["C%d" % h] = (5 + h, 4, halves[h])
        lanes["D%d" % h] = (7 + h, 5, halves[h])

    def gather_send(lane, s):
        i, u, cols = lanes[lane]
        up, down = gather_part(s, 0)
        return (
            send(cfull.at[u, up, cols], cfull.at[u, up, cols], ag_s.at[0, i, s], ag_r.at[0, i, s], above),
            send(cfull.at[u, down, cols], cfull.at[u, down, cols], ag_s.at[1, i, s], ag_r.at[1, i, s], below),
        )

    def across(lane, s, i):
        _, u, cols = lanes[lane]
        p = gather_part(s, 1)[i]
        if lane == "E":
            return send(cfull.at[6, p], cfull.at[3, p], ae_s.at[i, s], ae_r.at[i, s], other_core)
        h = int(lane[1])
        return send(
            cfull.at[u, p, cols], cfull.at[u, p, cols], ay_s.at[i, h, s], ay_r.at[i, h, s], other_y
        )

    def gather(lane, s):
        i, u, cols = lanes[lane]
        if s > 0:
            for d, p in enumerate(gather_part(s - 1, 1)):
                landed(cfull.at[u, p, cols], ag_r.at[d, i, s - 1], ag_s.at[d, i, s - 1])
                if lane[0] in "AE":
                    across(lane, s - 1, d).start()
        elif lane[0] in "CD":
            hand({"C": 4, "D": 5}[lane[0]], int(lane[1])).wait_recv()
        elif lane == "L":
            when(even, lambda: hand(6).wait_recv())
            when(odd, lambda: hand(3).wait_recv())
        if s < HOPS:
            for copy in gather_send(lane, s):
                copy.start()

    def gather_other(lane, u, cols):
        for s in range(HOPS):
            for i, p in enumerate(gather_part(s, 1)):
                if lane == "E":
                    landed(cfull.at[3, p], ae_r.at[i, s], ae_s.at[i, s])
                else:
                    h = int(lane[1])
                    landed(cfull.at[u, p, cols], ay_r.at[i, h, s], ay_s.at[i, h, s])

    def forward(view, j):
        raw = raws[view]
        return send(
            raw.at[1, *piece(view, j)], raw.at[2, *piece(view, j)], fwd_s.at[view, j], fwd_r.at[view, j],
            other_core,
        )

    def piece_take(j):
        for view in (1, 0):
            direct(view, j).wait_recv()
            forward(view, j).start()
        if j + AHEAD < PARTS:
            piece_start(j + AHEAD)

    def pass_on(r):
        for view in (1, 0):
            @pl.when(enters[view])
            def _():
                landed(relays[view].at[r], rel_r.at[view, r], rel_s.at[view, r])
                from_relay(view, r).start()

    def pass_far(r):
        for view, side in ((1, even), (0, odd)):
            @pl.when(jnp.logical_and(enters[view], side))
            def _():
                landed(relay_far.at[r], rel_far_r.at[r], rel_far_s.at[r])
                far_from_relay(view, r).start()

    def far_start(j):
        for view, side in ((1, even), (0, odd)):
            if j % 2 == 0:
                when(side, lambda: far(view, j).start())
            else:
                when(jnp.logical_and(side, leaves[view]), lambda: far_to_relay(view, j).start())
                when(
                    jnp.logical_and(side, jnp.logical_not(leaves[view])), lambda: far(view, j).start()
                )

    def far_take(view):
        for j in range(BANDS):
            far(view, j).wait_recv()

    def halves_step(h, c):
        forward(1, h * BANDS + c).wait_recv()
        take_halves(h, c)
        add_halves(h, c)

    def third_step(c):
        for j in (2 * c, 2 * c + 1):
            forward(0, j).wait_recv()

        @pl.when(even)
        def _():
            turn_a(2, c, BANDS)
            take_b(1, c)
            add_tile(3, BANDS)

    def fourth_tile():
        far_take(0)

        def body(c, carry):
            turn_a(3, c, BANDS)
            take_b(0, c)
            add_tile(3, BANDS)
            return carry

        lax.fori_loop(0, BANDS, body, 0)

    def grow(view, slot, u):
        g, raw, st = ((g_a, raw_b, st_b), (g_b, raw_a, st_a))[view]
        c = cfull[u]
        hi, lo = split(c)
        c_hi[...] = hi
        c_lo[...] = lo
        if view == 0:
            acc = squares[...]
            for j in range(width // 128):
                part_j = c[:, j * 128:(j + 1) * 128]
                acc = acc + part_j * part_j
            squares[...] = acc
        else:
            columns[...] = columns[...] + jnp.sum((c * c).reshape(width // 8, 8, width), axis=0)

        def body(i, carry):
            here = band_of(i)
            n = split(normal(raw, st, slot, here))
            g[here, :] = g[here, :] + dot3(n, (c_hi[...], c_lo[...]), view == 0)
            return carry

        lax.fori_loop(0, BANDS, body, 0)
        m = split(jnp.broadcast_to(st[slot, pl.ds(2, 1), :], (16, width)))
        means[view] = means[view] + dot3(m, (c_hi[...], c_lo[...]), view == 0)

    def grow_early():
        @pl.when(even)
        def _():
            far_take(1)
            hand(3).wait_recv()
            gather_other("E", 3, whole)
            grow(0, 3, 3)

        when(odd, grow, 1, 3, 6)

    def grow_late():
        @pl.when(odd)
        def _():
            far_take(1)
            grow(0, 3, 3)

        @pl.when(even)
        def _():
            far_take(0)
            grow(1, 3, 6)

    def grow_other():
        for h in (0, 1):
            gather_other("A%d" % h, 2 - y_lo, halves[h])
        grow(0, 2 - y_lo, 2 - y_lo)

    grows = {
        "a0": lambda: grow(0, 0, 0), "b0": lambda: grow(1, 0, 0),
        "A": lambda: grow(0, 1 + y_lo, 1 + y_lo), "O": grow_other,
        "C": lambda: grow(1, 1, 4), "D": lambda: grow(1, 2, 5),
        "E": grow_early, "L": grow_late,
    }

    def loss_part():
        value = jnp.zeros((8, 128), F32)
        for t in range(4):
            c = fin[...] if t == 3 else cfull[t, mine, :]
            terms = off_weight * c * c
            if t == 0:
                shape = (chunk, width)
                on = lax.broadcasted_iota(jnp.int32, shape, 1) == (
                    lax.broadcasted_iota(jnp.int32, shape, 0) + z * chunk
                )
                terms = jnp.where(on, (1.0 - c) * (1.0 - c), terms)
            terms = jnp.sum(terms.reshape(chunk // 8, 8, width), axis=0)
            for j in range(width // 128):
                value = value + terms[:, j * 128:(j + 1) * 128]
        l_z[z] = value

    def loss_z(d):
        return send(l_z.at[z], l_z.at[z], lz_s.at[d], lz_r.at[d], at_z(mod(z + d, NZ)))

    def loss_copy(r):
        return send(l_send.at[r], l_recv.at[r], loss_s.at[r], loss_r.at[r], crossed(1 << r))

    def loss_step(r):
        if r == 0:
            loss_part()
            for d in range(1, NZ):
                loss_z(d).start()
        elif r == 1:
            for d in range(1, NZ):
                landed(l_z.at[mod(z - d, NZ)], lz_r.at[d], lz_s.at[d])
            value = l_z[0]
            for i in range(1, NZ):
                value = value + l_z[i]
            l_send[0] = value
            loss_copy(0).start()
        else:
            loss_copy(r - 2).wait_recv()
            l_send[r - 1] = l_send[r - 2] + l_recv[r - 2]
            if r < 5:
                loss_copy(r - 1).start()

    squares[...] = jnp.zeros_like(squares)
    columns[...] = jnp.zeros_like(columns)
    means[...] = jnp.zeros_like(means)

    def clear_g(i, carry):
        g_a[band_of(i), :] = jnp.zeros((band, width), F32)
        g_b[band_of(i), :] = jnp.zeros((band, width), F32)
        return carry

    lax.fori_loop(0, BANDS, clear_g, 0)

    def step(name):
        kind, rest = name[0], name[1:]
        if name == "OWN":
            lax.fori_loop(0, BANDS, own_tile, 0)
            for slot in (3, 1, 2):
                for view, st in ((1, st_b), (0, st_a)):
                    landed(st.at[slot], stf_r.at[view, slot], stf_s.at[view, slot])
        elif name == "T3O":
            when(odd, fourth_tile)
        elif kind == "S":
            unit, s = rest.split("_")
            if unit[0] == "3":
                when(odd if unit == "3o" else even, sum_step, unit, int(s))
            else:
                sum_step(unit, int(s))
        elif kind == "F":
            if rest[0] == "3":
                when(odd if rest == "3o" else even, finish_sum, rest)
            else:
                finish_sum(rest)
        elif kind == "G":
            lane, s = rest.split("_")
            if lane == "E":
                when(odd, gather, lane, int(s))
            else:
                gather(lane, int(s))
        elif kind == "P":
            piece_take(int(rest))
        elif kind == "R":
            (pass_far if rest[0] == "L" else pass_on)(int(rest[-1]))
        elif kind == "C":
            if rest[0] == "3":
                third_step(int(rest[1]))
            else:
                halves_step(int(rest[0]), int(rest[1]))
        elif kind == "L":
            far_start(int(rest[1]))
        elif kind == "W":
            grows[rest]()
        elif kind == "X":
            loss_step(int(rest))

    for name in ORDER:
        step(name)

    loss_ref[0, 0] = jnp.sum(l_send[4]) * (1.0 / features)

    diagonal = []
    one_block = (
        lax.broadcasted_iota(jnp.int32, (128, 128), 0) == lax.broadcasted_iota(jnp.int32, (128, 128), 1)
    )
    for j in range(width // 128):
        block = cfull[0, j * 128:(j + 1) * 128, j * 128:(j + 1) * 128]
        diagonal.append(jnp.sum(jnp.where(one_block, block, 0.0), axis=0, keepdims=True))
    diagonal = jnp.concatenate(diagonal, axis=1)
    change = -(1.0 - diagonal) - off_weight * diagonal
    row_squares = jnp.sum(squares[...].T, axis=0, keepdims=True)
    column_squares = jnp.sum(columns[...], axis=0, keepdims=True)
    back_a = off_weight * row_squares + change * diagonal
    back_b = off_weight * column_squares + change * diagonal
    mean_a = off_weight * means[0, pl.ds(0, 1), :] + st_b[0, pl.ds(2, 1), :] * change
    mean_b = off_weight * means[1, pl.ds(0, 1), :] + st_a[0, pl.ds(2, 1), :] * change

    def out_copy(view, i):
        src, dst = ((g_a, ga_hbm), (g_b, gb_hbm))[view]
        return pltpu.make_async_copy(src.at[band_of(i)], dst.at[band_of(i)], out_sem.at[view, i])

    def finish(i, carry):
        here = band_of(i)
        n_a = normal(raw_a, st_a, 0, here)
        n_b = normal(raw_b, st_b, 0, here)
        g_a[here, :] = (off_weight * g_a[here, :] + n_b * change - mean_a - n_a * back_a) * st_a[0, pl.ds(1, 1), :]
        out_copy(0, i).start()
        g_b[here, :] = (off_weight * g_b[here, :] + n_a * change - mean_b - n_b * back_b) * st_b[0, pl.ds(1, 1), :]
        out_copy(1, i).start()
        return carry

    lax.fori_loop(0, BANDS, finish, 0)

    for view in (0, 1):
        for j in range(PARTS):
            direct(view, j).wait_send()
            forward(view, j).wait_send()
        for j in range(BANDS):
            far(view, j).wait_send()

        @pl.when(enters[view])
        def _():
            for r in range(PARTS // 2):
                from_relay(view, r).wait_send()

        @pl.when(jnp.logical_and(enters[view], (odd, even)[view]))
        def _():
            for r in range(BANDS // 2):
                far_from_relay(view, r).wait_send()

    for d in range(1, NZ):
        stat_z(d).wait_send()
        loss_z(d).wait_send()
    stat_y.wait_send()
    for k in (1, 2, 3):
        for view in (0, 1):
            stat_f(view, k).wait_send()
    for unit in ("0", "10", "11", "20", "21", "3o"):
        for s in range(HOPS):
            for copy in sum_send(unit, s):
                copy.wait_send()
        y_copy(unit).wait_send()
    for h in (0, 1):
        hand(4, h).wait_send()
        hand(5, h).wait_send()
    hand(3).wait_send()
    when(even, lambda: hand(6).wait_send())
    for lane in lanes:
        def sent(lane):
            for s in range(HOPS):
                for copy in gather_send(lane, s):
                    copy.wait_send()
                if lane[0] in "AE":
                    for i in (0, 1):
                        across(lane, s, i).wait_send()
        if lane == "E":
            when(odd, sent, lane)
        else:
            sent(lane)
    for r in range(4):
        loss_copy(r).wait_send()
    for view in (0, 1):
        for i in range(BANDS):
            out_copy(view, i).wait()


def local(view_a, view_b):
    rows, width = view_a.shape
    part = rows // PARTS
    band = rows // BANDS
    chunk = width // NZ
    dma = pltpu.SemaphoreType.DMA
    anywhere = pl.BlockSpec(memory_space=pl.ANY)
    grad_a, grad_b, loss = pl.pallas_call(
        kernel,
        out_shape=(
            jax.ShapeDtypeStruct((rows, width), F32),
            jax.ShapeDtypeStruct((rows, width), F32),
            jax.ShapeDtypeStruct((1, 1), F32),
        ),
        in_specs=[anywhere, anywhere],
        out_specs=(anywhere, anywhere, pl.BlockSpec(memory_space=pltpu.SMEM)),
        scratch_shapes=[
            pltpu.VMEM((4, rows, width), F32),
            pltpu.VMEM((4, rows, width), F32),
            pltpu.VMEM((BANDS + 1, width, band), BF16),
            pltpu.VMEM((BANDS + 1, width, band), BF16),
            pltpu.VMEM((band, width), BF16),
            pltpu.VMEM((band, width), BF16),
            pltpu.VMEM((4, width, width), F32),
            pltpu.VMEM((4, HOPS, chunk, width), F32),
            pltpu.VMEM((4, HOPS, chunk, width), F32),
            pltpu.VMEM((4, chunk, width), F32),
            pltpu.VMEM((chunk, width), F32),
            pltpu.VMEM((7, width, width), F32),
            pltpu.VMEM((width, width), BF16),
            pltpu.VMEM((width, width), BF16),
            pltpu.VMEM((rows, width), F32),
            pltpu.VMEM((rows, width), F32),
            pltpu.VMEM((PARTS // 2, part, width), F32),
            pltpu.VMEM((PARTS // 2, band, width // 2), F32),
            pltpu.VMEM((BANDS // 2, band, width), F32),
            pltpu.VMEM((NZ, 8, width), F32),
            pltpu.VMEM((2, 8, width), F32),
            pltpu.VMEM((4, 8, width), F32),
            pltpu.VMEM((4, 8, width), F32),
            pltpu.VMEM((width, 128), F32),
            pltpu.VMEM((8, width), F32),
            pltpu.VMEM((2, 16, width), F32),
            pltpu.VMEM((NZ, 8, 128), F32),
            pltpu.VMEM((5, 8, 128), F32),
            pltpu.VMEM((4, 8, 128), F32),
            dma((2,)),
            dma((2, BANDS)),
            dma((2, PARTS)), dma((2, PARTS)),
            dma((2, PARTS)), dma((2, PARTS)),
            dma((2, BANDS)), dma((2, BANDS)),
            dma((2, PARTS // 2)), dma((2, PARTS // 2)),
            dma((BANDS // 2,)), dma((BANDS // 2,)),
            dma((NZ,)), dma((NZ,)),
            dma(()), dma(()),
            dma((2, 4)), dma((2, 4)),
            dma((2, 6, HOPS)), dma((2, 6, HOPS)),
            dma((6,)), dma((6,)),
            dma((7, 2)), dma((7, 2)),
            dma((2, 9, HOPS)), dma((2, 9, HOPS)),
            dma((2, 2, HOPS)), dma((2, 2, HOPS)),
            dma((2, HOPS)), dma((2, HOPS)),
            dma((NZ,)), dma((NZ,)),
            dma((4,)), dma((4,)),
        ],
        compiler_params=pltpu.CompilerParams(
            collective_id=0, has_side_effects=True, vmem_limit_bytes=60 * 1024 * 1024
        ),
        cost_estimate=pl.CostEstimate(
            flops=2 * 3 * 12 * rows * width * width, bytes_accessed=16 * rows * width, transcendentals=0
        ),
    )(view_a, view_b)
    return grad_a, grad_b, loss[0, 0]


def solution(mesh):
    spec = P("batch", "feat")
    return jax.shard_map(
        local, mesh=mesh, in_specs=(spec, spec), out_specs=(spec, spec, P()), check_vma=False
    )
```

```python
import functools

import jax
import jax.numpy as jnp
from jax import lax
from jax.experimental import pallas as pl
from jax.experimental.pallas import tpu as pltpu
from jax.sharding import PartitionSpec as P

MESH = pl.DeviceIdType.MESH
F32 = jnp.float32
BF16 = jnp.bfloat16

eps = 1e-05
off_weight = 0.25

NZ = 8
NX = 4
NY = 4
NF = 16
PARTS = 4
BANDS = 4
SLABS = 2
HOPS = 4
AHEAD = 3

ORDER = (
    "OWN", "R0", "S0_0", "T3O", "S3o_0", "S0_1", "P0", "S3o_1", "S0_2", "P1", "S3o_2", "C00",
    "S0_3", "S3o_3", "C01", "SH0_0", "S0_4", "R1", "S3o_4", "SH0_1", "P2", "SH0_2", "F0", "G0_0",
    "F3o", "GE_0", "C10", "P3", "LT0", "LT1", "SH0_3", "G0_1", "GE_1", "C11", "SH1_0", "C30",
    "SH1_1", "GE_2", "C31", "SH1_2", "S3e_0", "GE_3", "SH0_4", "RL0", "G0_2", "SH1_3", "S3e_1",
    "GE_4", "FH0", "GQ0_0", "WE", "G0_3", "SH1_4", "S3e_2", "GQ0_1", "GR0_0", "G0_4", "Wa", "Wb",
    "FH1", "GQ1_0", "S3e_3", "GQ0_2", "GR0_1", "GQ1_1", "GR1_0", "S3e_4", "GQ0_3", "F3e", "X0",
    "GR0_2", "GQ1_2", "GL_0", "X1", "GR1_1", "GQ0_4", "WQ0", "X2", "GR0_3", "X3", "GQ1_3", "X4",
    "GL_1", "X5", "GR1_2", "GR0_4", "WR0", "GQ1_4", "WQ1", "GL_2", "GR1_3", "GL_3", "GR1_4", "WR1",
    "GL_4", "WL", "END",
)


def mod(value, n):
    return lax.rem(value + n, n)


def split(value):
    hi = value.astype(BF16)
    return hi, (value - hi.astype(F32)).astype(BF16)


def dot(left, right):
    return lax.dot_general(left, right, (((1,), (0,)), ((), ())), preferred_element_type=F32)


def dot3(left_hi, left_lo, right_hi, right_lo):
    return dot(left_hi, right_hi) + dot(left_hi, right_lo) + dot(left_lo, right_hi)


def kernel(
    a_hbm, b_hbm, ra_hbm, rb_hbm, ct_hi_hbm, ct_lo_hbm, cb_hi_hbm, cb_lo_hbm, st_a, st_b, vectors, loss_ref,
    raw_a, raw_b, left_hi, left_lo, right_hi, right_lo, tiles, rs_p, rs_m, y_recv, fin, cfull,
    ct_hi, ct_lo, cb_hi, cb_lo, relay_a, relay_b, relay_far, st_z, st_y, squares, columns, means, l_z, l_send, l_recv,
    in_sem, block_sem, out_sem, direct_s, direct_r, fwd_s, fwd_r, far_s, far_r, rel_s, rel_r, rel_far_s, rel_far_r,
    stz_s, stz_r, sty_s, sty_r, stf_s, stf_r, rs_s, rs_r, y_s, y_r, hand_s, hand_r,
    ag_s, ag_r, ae_s, ae_r, lz_s, lz_r, loss_s, loss_r,
):
    rows, width = a_hbm.shape
    part = rows // PARTS
    band = rows // BANDS
    slab = rows // SLABS
    mid = width // 2
    chunk = width // NZ
    half = chunk // 2
    total = float(rows * 2 * NZ)
    features = float(width * NF)

    batch = lax.axis_index("batch")
    feat = lax.axis_index("feat")
    z = lax.div(batch, 2)
    y_lo = lax.rem(batch, 2)
    y = lax.div(feat, 2 * NX) * 2 + y_lo
    x = lax.rem(lax.div(feat, 2), NX)
    core = lax.rem(feat, 2)
    even = core == 0
    odd = core == 1
    first_x = x == 0
    last_x = x == NX - 1
    seam = jnp.logical_or(first_x, last_x)

    def at_feat(f):
        return {"batch": batch, "feat": f}

    def at_z(z_other):
        return {"batch": z_other * 2 + y_lo, "feat": feat}

    def at_xy(x_other, y_other, core_other):
        f = lax.div(y_other, 2) * (2 * NX) + x_other * 2 + core_other
        return {"batch": z * 2 + lax.rem(y_other, 2), "feat": f}

    def neighbour(steps):
        return at_feat(mod(feat + steps, NF))

    def crossed(stride):
        return at_feat(feat + stride - 2 * stride * lax.rem(lax.div(feat, stride), 2))

    other_core = crossed(1)
    other_y = {"batch": batch + 1 - 2 * y_lo, "feat": feat}
    above = at_z(mod(z + 1, NZ))
    below = at_z(mod(z - 1, NZ))
    mirror_x = NX - 1 - x
    ahead_crossed = at_feat(mod(feat + 3 - 2 * core, NF))

    def send(src, dst, s_sem, r_sem, device):
        return pltpu.make_async_remote_copy(
            src_ref=src, dst_ref=dst, send_sem=s_sem, recv_sem=r_sem,
            device_id=device, device_id_type=MESH,
        )

    def landed(dst, r_sem):
        send(dst, dst, sty_s, r_sem, other_core).wait_recv()

    def left_here(src, s_sem):
        send(src, src, s_sem, sty_r, other_core).wait_send()

    load_b = pltpu.make_async_copy(b_hbm, raw_b.at[0], in_sem.at[0])
    load_a = pltpu.make_async_copy(a_hbm, raw_a.at[0], in_sem.at[1])
    load_b.start()
    load_a.start()

    barrier = pltpu.get_barrier_semaphore()
    friends = [neighbour(k) for k in (-3, -2, -1, 1, 2, 3)]
    friends += [crossed(k) for k in (2, 4, 8)]
    friends += [at_z(mod(z + d, NZ)) for d in range(1, NZ)]
    friends += [other_y]
    for friend in friends:
        pl.semaphore_signal(barrier, inc=1, device_id=friend, device_id_type=MESH)

    @pl.when(seam)
    def _():
        for friend in (
            at_xy(mirror_x, mod(y - 1, NY), core), at_xy(mirror_x, mod(y + 1, NY), core),
            at_xy(x, mod(y - 1, NY), core), at_xy(x, mod(y + 1, NY), core),
            at_xy(x, mod(y - 1, NY), 1 - core), at_xy(x, mod(y + 1, NY), 1 - core),
        ):
            pl.semaphore_signal(barrier, inc=1, device_id=friend, device_id_type=MESH)

    pl.semaphore_wait(barrier, jnp.where(seam, len(friends) + 6, len(friends)))


    def band_of(c):
        return pl.ds(pl.multiple_of(c * band, band), band)

    def span(i, size):
        return pl.ds(pl.multiple_of(i * size, size), size)

    halves = (pl.ds(0, mid), pl.ds(mid, mid))

    def piece(view, j):
        if view == 0:
            return span(j, part), pl.ds(0, width)
        return span(j % SLABS, slab), halves[j // SLABS]

    raws = (raw_a, raw_b)
    relays = (relay_a, relay_b)

    def direct(view, j):
        src, raw, steps = ((a_hbm, raw_a, 2), (b_hbm, raw_b, -2))[view]
        return send(
            src.at[piece(view, j)], raw.at[1, *piece(view, j)], direct_s.at[view, j], direct_r.at[view, j],
            neighbour(steps),
        )

    def to_relay(view, j):
        src = (a_hbm, b_hbm)[view]
        return send(
            src.at[piece(view, j)], relays[view].at[j // 2], direct_s.at[view, j], rel_r.at[view, j // 2],
            at_xy(mirror_x, mod(y - 1, NY), core),
        )

    def from_relay(view, r):
        j = 2 * r + 1
        return send(
            relays[view].at[r], raws[view].at[1, *piece(view, j)], rel_s.at[view, r], direct_r.at[view, j],
            at_xy(x, mod(y - 1, NY), core),
        )

    leaves = (last_x, first_x)
    enters = (first_x, last_x)

    def when(cond, f, *args):
        @pl.when(cond)
        def _():
            f(*args)

    def piece_start(j):
        for view in (1, 0):
            if j % 2 == 0:
                direct(view, j).start()
            else:
                @pl.when(leaves[view])
                def _():
                    to_relay(view, j).start()

                @pl.when(jnp.logical_not(leaves[view]))
                def _():
                    direct(view, j).start()

    for j in range(AHEAD):
        piece_start(j)

    def far(view, j, src=None):
        raw = raws[view]
        src = raw.at[1] if src is None else src
        return send(
            src.at[span(j, slab)], raw.at[3, span(j, slab)], far_s.at[view, j], far_r.at[view, j],
            neighbour(1 - 2 * view),
        )

    def far_to_relay(view, j):
        return send(
            raws[view].at[1, span(j, slab)], relay_far.at[j // 2], far_s.at[view, j], rel_far_r.at[j // 2],
            at_xy(mirror_x, mod(y - 1, NY), core),
        )

    def far_from_relay(view, r):
        j = 2 * r + 1
        return send(
            relay_far.at[r], raws[view].at[3, span(j, slab)], rel_far_s.at[r], far_r.at[view, j],
            at_xy(x, mod(y - 1, NY), 1 - core),
        )

    for j in range(SLABS):
        when(odd, lambda: far(1, j, b_hbm).start())
        when(even, lambda: far(0, j, a_hbm).start())

    load_b.wait()
    load_a.wait()
    strip = 128
    for view, raw in ((0, raw_a), (1, raw_b)):
        def add_up(i, acc):
            v = raw[0, pl.ds(pl.multiple_of(i * strip, strip), strip), :]
            return acc + jnp.sum(v.reshape(strip // 8, 8, width), axis=0)

        zeros = jnp.zeros((8, width), F32)
        acc = lax.fori_loop(0, rows // strip, add_up, zeros)
        mean = jnp.sum(acc, axis=0, keepdims=True) * (1.0 / rows)

        def add_up_squares(i, carry):
            rest, square = carry
            v = raw[0, pl.ds(pl.multiple_of(i * strip, strip), strip), :] - mean
            v = v.reshape(strip // 8, 8, width)
            return rest + jnp.sum(v, axis=0), square + jnp.sum(v * v, axis=0)

        rest, square = lax.fori_loop(0, rows // strip, add_up_squares, (zeros, zeros))
        st_z[z, pl.ds(3 * view, 1), :] = mean
        st_z[z, pl.ds(3 * view + 1, 1), :] = jnp.sum(square, axis=0, keepdims=True)
        st_z[z, pl.ds(3 * view + 2, 1), :] = jnp.sum(rest, axis=0, keepdims=True)

    def stat_z(d):
        return send(
            st_z.at[z], st_z.at[z], stz_s, stz_r, at_z(mod(z + d, NZ))
        )

    for d in range(1, NZ):
        stat_z(d).start()
    landed(st_z.at[pl.ds(0, NZ - 1)], stz_r)
    for view in (0, 1):
        means_z = [st_z[i, pl.ds(3 * view, 1), :] for i in range(NZ)]
        mean = sum(means_z[1:], means_z[0]) * (1.0 / NZ)
        square = jnp.zeros((1, width), F32)
        rest = jnp.zeros((1, width), F32)
        for i in range(NZ):
            off = means_z[i] - mean
            square = square + (st_z[i, pl.ds(3 * view + 1, 1), :] + float(rows) * off * off)
            rest = rest + (st_z[i, pl.ds(3 * view + 2, 1), :] + float(rows) * off)
        st_y[0, pl.ds(3 * view, 1), :] = mean
        st_y[0, pl.ds(3 * view + 1, 1), :] = square
        st_y[0, pl.ds(3 * view + 2, 1), :] = rest
    stat_y = send(st_y.at[0], st_y.at[1], sty_s, sty_r, other_y)
    stat_y.start()
    stat_y.wait_recv()
    rows_z = float(rows * NZ)
    for view, st in ((0, st_a), (1, st_b)):
        mean0, mean1 = (st_y[i, pl.ds(3 * view, 1), :] for i in (0, 1))
        mean = 0.5 * (mean0 + mean1)
        off0, off1 = mean0 - mean, mean1 - mean
        square = (
            st_y[0, pl.ds(3 * view + 1, 1), :] + st_y[1, pl.ds(3 * view + 1, 1), :]
            + rows_z * (off0 * off0 + off1 * off1)
        )
        rest = (
            st_y[0, pl.ds(3 * view + 2, 1), :] + st_y[1, pl.ds(3 * view + 2, 1), :]
            + rows_z * (off0 + off1)
        )
        inverse = 1.0 / jnp.sqrt(square * (1.0 / total) + eps)
        st[0, pl.ds(0, 1), :] = mean
        st[0, pl.ds(1, 1), :] = inverse
        st[0, pl.ds(2, 1), :] = rest * (1.0 / total) * inverse

    def stat_f(view, k):
        st = (st_a, st_b)[view]
        if k == 2:
            slot = 1
        elif (k == 1) == (view == 1):
            slot = 2 + core
        else:
            slot = 3 - core
        return send(
            st.at[0], st.at[slot], stf_s.at[view], stf_r.at[view],
            neighbour(-k if view == 1 else k),
        )

    for k in (2, 1, 3):
        for view in (1, 0):
            stat_f(view, k).start()

    def normal(raw, st, slot, rows_here, cols=slice(None)):
        return (raw[slot, rows_here, cols] - st[slot, pl.ds(0, 1), cols]) * st[slot, pl.ds(1, 1), cols]

    strips = 128

    def turn_a(slot, c, index):
        def body(i, carry):
            here = pl.ds(pl.multiple_of(c * slab + i * strips, strips), strips)
            hi, lo = split(normal(raw_a, st_a, slot, here).T)
            cols = pl.ds(pl.multiple_of(i * strips, strips), strips)
            left_hi[index, :, cols] = hi
            left_lo[index, :, cols] = lo
            return carry
        lax.fori_loop(0, slab // strips, body, 0)

    def take_b(slot, c):
        def body(i, carry):
            here = pl.ds(pl.multiple_of(c * slab + i * strips, strips), strips)
            right_hi[span(i, strips), :], right_lo[span(i, strips), :] = split(normal(raw_b, st_b, slot, here))
            return carry
        lax.fori_loop(0, slab // strips, body, 0)

    def take_halves(h, c):
        def body(i, carry):
            here = pl.ds(pl.multiple_of(c * slab + i * strips, strips), strips)
            for slot in (1, 2):
                hi, lo = split(normal(raw_b, st_b, slot, here, halves[h]))
                right_hi[span(i, strips), halves[slot - 1]] = hi
                right_lo[span(i, strips), halves[slot - 1]] = lo
            return carry
        lax.fori_loop(0, slab // strips, body, 0)

    def add_tile(t, c, first):
        def body(i, carry):
            here = span(i, mid)
            out = dot3(left_hi[c, here, :], left_lo[c, here, :], right_hi[...], right_lo[...])
            tiles[t, here, :] = out if first else tiles[t, here, :] + out
            return carry
        lax.fori_loop(0, 2, body, 0)

    def own_tile():
        for c in range(SLABS):
            turn_a(0, c, c)
            take_b(0, c)
            add_tile(0, c, c == 0)

    def dest(q):
        return pl.multiple_of(mod(q, NZ) * chunk, chunk)

    units = {"0": 0, "H0": 1, "H1": 2, "3o": 3, "3e": 3}

    def sum_send(unit, s):
        t = units[unit]
        if s == 0:
            up = pl.ds(dest(z + HOPS), half)
            down = pl.ds(pl.multiple_of(dest(z + HOPS) + half, half), half)
            up_to, down_to = pl.ds(0, half), pl.ds(half, half)
        else:
            up, down = pl.ds(dest(z + HOPS - s), chunk), pl.ds(dest(z - HOPS + s), chunk)
            up_to = down_to = pl.ds(0, chunk)
        return (
            send(tiles.at[t, up], rs_p.at[t, s, up_to], rs_s.at[t], rs_r.at[t, s], above),
            send(tiles.at[t, down], rs_m.at[t, s, down_to], rs_s.at[t], rs_r.at[t, s], below),
        )

    def sum_start(unit, s):
        for copy in sum_send(unit, s):
            copy.start()

    def sum_take(unit, s):
        t = units[unit]
        landed(tiles.at[t, pl.ds(0, chunk if s == 0 else 2 * chunk)], rs_r.at[t, s])
        for recv, q, low in ((rs_p, z + HOPS - 1 - s, 0), (rs_m, z - HOPS + 1 + s, half)):
            if s == 0:
                here = pl.ds(pl.multiple_of(dest(q) + low, half), half)
                tiles[t, here, :] = tiles[t, here, :] + recv[t, s, pl.ds(low, half), :]
            else:
                here = pl.ds(dest(q), chunk)
                tiles[t, here, :] = tiles[t, here, :] + recv[t, s]

    mine = pl.ds(dest(z), chunk)

    def y_copy(unit):
        t = units[unit]
        return send(tiles.at[t, mine], y_recv.at[t], y_s.at[t], y_r.at[t], other_y)

    def sum_step(unit, s):
        if s > 0:
            sum_take(unit, s - 1)
        if s < HOPS:
            sum_start(unit, s)
        else:
            y_copy(unit).start()

    def sum_all(unit):
        t = units[unit]
        y_copy(unit).wait_recv()
        return (tiles[t, mine, :] + y_recv[t]) * (1.0 / total)

    def hand(u, h=0):
        if u in (4, 5):
            src = cfull.at[1 + h, mine, halves[u - 4]]
            dst = cfull.at[4 + h, mine, halves[u - 4]]
            device = neighbour(2) if u == 4 else ahead_crossed
        else:
            src, dst = fin, cfull.at[u, mine]
            device = neighbour(-1 if u == 3 else 2)
        return send(src, dst, hand_s.at[u, h], hand_r.at[u, h], device)

    def finish_sum(unit):
        value = sum_all(unit)
        t = units[unit]
        if t < 3:
            cfull[t, mine, :] = value
            if t > 0:
                hand(4, t - 1).start()
                hand(5, t - 1).start()
        else:
            fin[...] = value
            hand(3).start()
            if unit == "3o":
                cfull[6, mine, :] = value
            else:
                hand(6).start()

    def gather_part(s, mover):
        up, down = z - s - mover, z + s + mover
        if s < HOPS - 1:
            return pl.ds(dest(up), chunk), pl.ds(dest(down), chunk)
        return pl.ds(dest(up), half), pl.ds(pl.multiple_of(dest(down) + half, half), half)

    lanes = {
        "0": (0, 0), "E": (1, 6), "L": (2, 6 - 3 * core),
        "Q0": (3, 1), "Q1": (4, 2), "R0": (5, 4), "R1": (6, 5),
    }

    def gather_send(lane, s):
        i, u = lanes[lane]
        return [
            send(cfull.at[u, p], cfull.at[u, p], ag_s.at[i], ag_r.at[i, s], device)
            for p, device in zip(gather_part(s, 0), (above, below))
        ]

    def across(s):
        return [
            send(cfull.at[6, p], cfull.at[3, p], ae_s, ae_r, other_core) for p in gather_part(s, 1)
        ]

    def gather(lane, s):
        i, u = lanes[lane]
        if s > 0:
            landed(cfull.at[u, pl.ds(0, 2 * chunk if s < HOPS else chunk)], ag_r.at[i, s - 1])
        elif lane[0] == "R":
            hand(4, int(lane[1])).wait_recv()
            hand(5, int(lane[1])).wait_recv()
        elif lane == "L":
            when(even, lambda: hand(6).wait_recv())
            when(odd, lambda: hand(3).wait_recv())
        if s < HOPS:
            for copy in gather_send(lane, s):
                copy.start()
        if s > 0 and lane == "E":
            for copy in across(s - 1):
                copy.start()

    def forward(view, j):
        raw = raws[view]
        return send(
            raw.at[1, *piece(view, j)], raw.at[2, *piece(view, j)], fwd_s.at[view, j], fwd_r.at[view, j],
            other_core,
        )

    def piece_take(j):
        for view in (1, 0):
            direct(view, j).wait_recv()
            forward(view, j).start()
        if j + AHEAD < PARTS:
            piece_start(j + AHEAD)

    def pass_on(r):
        for view in (1, 0):
            @pl.when(enters[view])
            def _():
                landed(relays[view].at[r], rel_r.at[view, r])
                from_relay(view, r).start()

    def pass_far(r):
        for view, side in ((1, even), (0, odd)):
            @pl.when(jnp.logical_and(enters[view], side))
            def _():
                landed(relay_far.at[r], rel_far_r.at[r])
                far_from_relay(view, r).start()

    def far_start(j):
        for view, side in ((1, even), (0, odd)):
            if j % 2 == 0:
                when(side, lambda: far(view, j).start())
            else:
                when(jnp.logical_and(side, leaves[view]), lambda: far_to_relay(view, j).start())
                when(
                    jnp.logical_and(side, jnp.logical_not(leaves[view])), lambda: far(view, j).start()
                )

    def far_take(view):
        for j in range(SLABS):
            far(view, j).wait_recv()

    def halves_step(h, c):
        forward(1, h * SLABS + c).wait_recv()
        take_halves(h, c)
        add_tile(1 + h, c, c == 0)

    def third_step(c):
        for j in range(c * SLABS, c * SLABS + SLABS):
            forward(0, j).wait_recv()

        @pl.when(even)
        def _():
            turn_a(2, c, SLABS)
            take_b(1, c)
            add_tile(3, SLABS, c == 0)

    def fourth_tile():
        far_take(0)
        for c in range(SLABS):
            turn_a(3, c, SLABS)
            take_b(0, c)
            add_tile(3, SLABS, c == 0)

    def block_out(view, slot):
        raw, dst = ((raw_a, ra_hbm), (raw_b, rb_hbm))[view]
        return pltpu.make_async_copy(raw.at[slot], dst.at[slot - 1], block_sem.at[view, slot - 1])

    def tile_out(view, k, cols=slice(None), count=1, i=0):
        here = pl.ds(k * width, count * width)
        pairs = (((ct_hi, ct_hi_hbm), (ct_lo, ct_lo_hbm)), ((cb_hi, cb_hi_hbm), (cb_lo, cb_lo_hbm)))[view]
        return [
            pltpu.make_async_copy(src.at[here, cols], dst.at[here, cols], out_sem.at[view, k + i, j])
            for j, (src, dst) in enumerate(pairs)
        ]

    def keep(view, st, slot, at, to, cols, value):
        sums, hi_ref, lo_ref = ((squares, ct_hi, ct_lo), (columns, cb_hi, cb_lo))[view]
        sums[:, cols] = sums[:, cols] + jnp.sum((value * value).reshape(strips // 8, 8, -1), axis=0)
        factor = st[slot, :, pl.ds(at, strips)].T[:, 2:3]
        means[view, :, cols] = means[view, :, cols] + jnp.sum(
            (value * factor).reshape(strips // 8, 8, -1), axis=0
        )
        hi, lo = split(value)
        hi_ref[pl.ds(to, strips), cols] = hi
        lo_ref[pl.ds(to, strips), cols] = lo

    everything = slice(None)

    def keep_a(u, k, slots):
        for i in range(width // strips):
            value = cfull[u, :, pl.ds(i * strips, strips)].T
            slot, at = slots(i)
            keep(0, st_b, slot, at, k * width + i * strips, everything, value)
        for copy in tile_out(0, k):
            copy.start()

    def keep_b(u, k, slot):
        for i in range(width // strips):
            value = cfull[u, pl.ds(i * strips, strips), :]
            keep(1, st_a, slot, i * strips, k * width + i * strips, everything, value)
        for copy in tile_out(1, k):
            copy.start()

    def keep_a_half(h):
        per = mid // strips
        keep_a(1 + h, 1 + h, lambda i: (1 + i // per, h * mid + (i % per) * strips))

    def keep_b_half(h):
        for k in (1, 2):
            for i in range(width // strips):
                value = cfull[4 + h, pl.ds(i * strips, strips), halves[k - 1]]
                keep(1, st_a, k, i * strips, k * width + i * strips, halves[h], value)
        for copy in tile_out(1, 1, halves[h], 2, h):
            copy.start()

    def keep_early():
        @pl.when(even)
        def _():
            hand(3).wait_recv()
            landed(cfull.at[3, pl.ds(0, width - chunk)], ae_r)
            keep_a(3, 3, lambda i: (3, i * strips))

        when(odd, keep_b, 6, 3, 3)

    def keep_late():
        @pl.when(odd)
        def _():
            far_take(1)
            block_out(1, 3).start()
            keep_a(3, 3, lambda i: (3, i * strips))

        @pl.when(even)
        def _():
            far_take(0)
            block_out(0, 3).start()
            keep_b(6, 3, 3)

    keeps = {
        "a": lambda: keep_a(0, 0, lambda i: (0, i * strips)), "b": lambda: keep_b(0, 0, 0),
        "Q0": lambda: keep_a_half(0), "Q1": lambda: keep_a_half(1),
        "R0": lambda: keep_b_half(0), "R1": lambda: keep_b_half(1),
        "E": keep_early, "L": keep_late,
    }

    def blocks_out():
        for view in (0, 1):
            for slot in (1, 2):
                block_out(view, slot).start()

        @pl.when(even)
        def _():
            far_take(1)
            block_out(1, 3).start()

        when(odd, lambda: block_out(0, 3).start())

    def loss_part():
        value = jnp.zeros((8, 128), F32)
        for t in range(4):
            c = fin[...] if t == 3 else cfull[t, mine, :]
            terms = off_weight * c * c
            if t == 0:
                shape = (chunk, width)
                on = lax.broadcasted_iota(jnp.int32, shape, 1) == (
                    lax.broadcasted_iota(jnp.int32, shape, 0) + z * chunk
                )
                terms = jnp.where(on, (1.0 - c) * (1.0 - c), terms)
            terms = jnp.sum(terms.reshape(chunk // 8, 8, width), axis=0)
            for j in range(width // 128):
                value = value + terms[:, j * 128:(j + 1) * 128]
        l_z[z] = value

    def loss_z(d):
        return send(l_z.at[z], l_z.at[z], lz_s, lz_r, at_z(mod(z + d, NZ)))

    def loss_copy(r):
        return send(l_send.at[r], l_recv.at[r], loss_s.at[r], loss_r.at[r], crossed(1 << r))

    def loss_step(r):
        if r == 0:
            blocks_out()
            loss_part()
            for d in range(1, NZ):
                loss_z(d).start()
        elif r == 1:
            landed(l_z.at[pl.ds(0, NZ - 1)], lz_r)
            value = l_z[0]
            for i in range(1, NZ):
                value = value + l_z[i]
            l_send[0] = value
            loss_copy(0).start()
        else:
            loss_copy(r - 2).wait_recv()
            l_send[r - 1] = l_send[r - 2] + l_recv[r - 2]
            if r < 5:
                loss_copy(r - 1).start()

    squares[...] = jnp.zeros_like(squares)
    columns[...] = jnp.zeros_like(columns)
    means[...] = jnp.zeros_like(means)

    def step(name):
        kind, rest = name[0], name[1:]
        if name == "OWN":
            own_tile()
            for view, st in ((1, st_b), (0, st_a)):
                landed(st.at[pl.ds(1, 3)], stf_r.at[view])
        elif name == "T3O":
            when(odd, fourth_tile)
        elif kind == "S":
            unit, s = rest.split("_")
            if unit[0] == "3":
                when(odd if unit == "3o" else even, sum_step, unit, int(s))
            else:
                sum_step(unit, int(s))
        elif kind == "F":
            if rest[0] == "3":
                when(odd if rest == "3o" else even, finish_sum, rest)
            else:
                finish_sum(rest)
        elif kind == "G":
            lane, s = rest.split("_")
            if lane == "E":
                when(odd, gather, lane, int(s))
            else:
                gather(lane, int(s))
        elif kind == "P":
            piece_take(int(rest))
        elif kind == "R":
            (pass_far if rest[0] == "L" else pass_on)(int(rest[-1]))
        elif kind == "C":
            if rest[0] == "3":
                third_step(int(rest[1]))
            else:
                halves_step(int(rest[0]), int(rest[1]))
        elif kind == "L":
            far_start(int(rest[1]))
        elif kind == "W":
            keeps[rest]()
        elif kind == "X":
            loss_step(int(rest))

    for name in ORDER:
        step(name)

    loss_ref[0, 0] = jnp.sum(l_send[4]) * (1.0 / features)

    diagonal = []
    one_block = (
        lax.broadcasted_iota(jnp.int32, (128, 128), 0) == lax.broadcasted_iota(jnp.int32, (128, 128), 1)
    )
    for j in range(width // 128):
        block = cfull[0, j * 128:(j + 1) * 128, j * 128:(j + 1) * 128]
        diagonal.append(jnp.sum(jnp.where(one_block, block, 0.0), axis=0, keepdims=True))
    diagonal = jnp.concatenate(diagonal, axis=1)
    change = -(1.0 - diagonal) - off_weight * diagonal
    row_squares = jnp.sum(squares[...], axis=0, keepdims=True)
    column_squares = jnp.sum(columns[...], axis=0, keepdims=True)
    back_a = off_weight * row_squares + change * diagonal
    back_b = off_weight * column_squares + change * diagonal
    mean_a = off_weight * jnp.sum(means[0], axis=0, keepdims=True) + st_b[0, pl.ds(2, 1), :] * change
    mean_b = off_weight * jnp.sum(means[1], axis=0, keepdims=True) + st_a[0, pl.ds(2, 1), :] * change
    for i, row in enumerate((change, back_a, back_b, mean_a, mean_b)):
        vectors[pl.ds(i, 1), :] = row

    for view in (0, 1):
        for j in range(PARTS):
            direct(view, j).wait_send()
            forward(view, j).wait_send()
        for j in range(SLABS):
            far(view, j).wait_send()

        @pl.when(enters[view])
        def _():
            for r in range(PARTS // 2):
                from_relay(view, r).wait_send()

        @pl.when(jnp.logical_and(enters[view], (odd, even)[view]))
        def _():
            for r in range(SLABS // 2):
                far_from_relay(view, r).wait_send()

    left_here(st_z.at[pl.ds(0, NZ - 1)], stz_s)
    left_here(l_z.at[pl.ds(0, NZ - 1)], lz_s)
    stat_y.wait_send()
    for view, st in ((1, st_b), (0, st_a)):
        left_here(st.at[pl.ds(1, 3)], stf_s.at[view])
    for unit in ("0", "H0", "H1", "3o"):
        left_here(tiles.at[units[unit], pl.ds(0, width - chunk)], rs_s.at[units[unit]])
        y_copy(unit).wait_send()
    for h in (0, 1):
        hand(4, h).wait_send()
        hand(5, h).wait_send()
    hand(3).wait_send()
    when(even, lambda: hand(6).wait_send())
    for lane in lanes:
        i, u = lanes[lane]
        if lane == "E":
            @pl.when(odd)
            def _():
                left_here(cfull.at[6, pl.ds(0, width - chunk)], ag_s.at[1])
                left_here(cfull.at[6, pl.ds(0, width - chunk)], ae_s)
        else:
            left_here(cfull.at[u, pl.ds(0, width - chunk)], ag_s.at[i])
    for r in range(4):
        loss_copy(r).wait_send()
    for view in (0, 1):
        for slot in (1, 2, 3):
            block_out(view, slot).wait()
    for k in range(4):
        for copy in tile_out(0, k):
            copy.wait()
    for k in (0, 3):
        for copy in tile_out(1, k):
            copy.wait()
    for h in (0, 1):
        for copy in tile_out(1, 1, halves[h], 2, h):
            copy.wait()


def gradients(
    a_ref, b_ref, ra_ref, rb_ref, ct_hi, ct_lo, cb_hi, cb_lo, st_a, st_b, vectors, ga_ref, gb_ref, n_hi, n_lo
):
    width = a_ref.shape[1]
    mid = width // 2
    lower, upper = pl.ds(0, mid), pl.ds(mid, mid)

    def row(i):
        return vectors[pl.ds(i, 1), :]

    def normal(value, st, slot, cols=slice(None)):
        return (value - st[slot, pl.ds(0, 1), cols]) * st[slot, pl.ds(1, 1), cols]

    def put(at, value):
        hi, lo = split(value)
        n_hi[:, pl.ds(at, value.shape[1])] = hi
        n_lo[:, pl.ds(at, value.shape[1])] = lo

    change = row(0)
    norm_a = normal(a_ref[...], st_a, 0)
    norm_b = normal(b_ref[...], st_b, 0)
    put(0, norm_b)
    for h, cols in enumerate((lower, upper)):
        for slot in (1, 2):
            at = (1 + h) * width + (slot - 1) * mid
            put(at, normal(rb_ref[slot - 1, :, cols], st_b, slot, cols))
    put(3 * width, normal(rb_ref[2], st_b, 3))
    g = off_weight * dot3(n_hi[...], n_lo[...], ct_hi[...], ct_lo[...]) + norm_b * change
    ga_ref[...] = (g - row(3) - norm_a * row(1)) * st_a[0, pl.ds(1, 1), :]
    put(0, norm_a)
    for slot in (1, 2, 3):
        put(slot * width, normal(ra_ref[slot - 1], st_a, slot))
    g = off_weight * dot3(n_hi[...], n_lo[...], cb_hi[...], cb_lo[...]) + norm_a * change
    gb_ref[...] = (g - row(4) - norm_b * row(2)) * st_b[0, pl.ds(1, 1), :]


def local(view_a, view_b):
    rows, width = view_a.shape
    part = rows // PARTS
    band = rows // BANDS
    slab = rows // SLABS
    chunk = width // NZ
    dma = pltpu.SemaphoreType.DMA
    anywhere = pl.BlockSpec(memory_space=pl.ANY)
    in_vmem = pl.BlockSpec(memory_space=pltpu.VMEM)
    blocks = jax.ShapeDtypeStruct((3, rows, width), F32)
    sides = jax.ShapeDtypeStruct((BANDS * width, width), BF16)
    stats = jax.ShapeDtypeStruct((4, 8, width), F32)
    ra, rb, ct_hi, ct_lo, cb_hi, cb_lo, st_a, st_b, vectors, loss = pl.pallas_call(
        kernel,
        out_shape=(
            blocks, blocks, sides, sides, sides, sides, stats, stats,
            jax.ShapeDtypeStruct((8, width), F32), jax.ShapeDtypeStruct((1, 1), F32),
        ),
        in_specs=[anywhere, anywhere],
        out_specs=(anywhere,) * 6 + (in_vmem,) * 3 + (pl.BlockSpec(memory_space=pltpu.SMEM),),
        scratch_shapes=[
            pltpu.VMEM((4, rows, width), F32),
            pltpu.VMEM((4, rows, width), F32),
            pltpu.VMEM((SLABS + 1, width, slab), BF16),
            pltpu.VMEM((SLABS + 1, width, slab), BF16),
            pltpu.VMEM((slab, width), BF16),
            pltpu.VMEM((slab, width), BF16),
            pltpu.VMEM((4, width, width), F32),
            pltpu.VMEM((4, HOPS, chunk, width), F32),
            pltpu.VMEM((4, HOPS, chunk, width), F32),
            pltpu.VMEM((4, chunk, width), F32),
            pltpu.VMEM((chunk, width), F32),
            pltpu.VMEM((7, width, width), F32),
            pltpu.VMEM((4 * width, width), BF16),
            pltpu.VMEM((4 * width, width), BF16),
            pltpu.VMEM((4 * width, width), BF16),
            pltpu.VMEM((4 * width, width), BF16),
            pltpu.VMEM((PARTS // 2, part, width), F32),
            pltpu.VMEM((PARTS // 2, slab, width // 2), F32),
            pltpu.VMEM((SLABS // 2, slab, width), F32),
            pltpu.VMEM((NZ, 8, width), F32),
            pltpu.VMEM((2, 8, width), F32),
            pltpu.VMEM((8, width), F32),
            pltpu.VMEM((8, width), F32),
            pltpu.VMEM((2, 8, width), F32),
            pltpu.VMEM((NZ, 8, 128), F32),
            pltpu.VMEM((5, 8, 128), F32),
            pltpu.VMEM((4, 8, 128), F32),
            dma((2,)),
            dma((2, 3)),
            dma((2, 4, 2)),
            dma((2, PARTS)), dma((2, PARTS)),
            dma((2, PARTS)), dma((2, PARTS)),
            dma((2, SLABS)), dma((2, SLABS)),
            dma((2, PARTS // 2)), dma((2, PARTS // 2)),
            dma((SLABS // 2,)), dma((SLABS // 2,)),
            dma(()), dma(()),
            dma(()), dma(()),
            dma((2,)), dma((2,)),
            dma((4,)), dma((4, HOPS)),
            dma((4,)), dma((4,)),
            dma((7, 2)), dma((7, 2)),
            dma((7,)), dma((7, HOPS)),
            dma(()), dma(()),
            dma(()), dma(()),
            dma((4,)), dma((4,)),
        ],
        compiler_params=pltpu.CompilerParams(
            collective_id=0, has_side_effects=True, vmem_limit_bytes=60 * 1024 * 1024
        ),
        cost_estimate=pl.CostEstimate(
            flops=2 * 3 * 4 * rows * width * width, bytes_accessed=32 * rows * width, transcendentals=0
        ),
    )(view_a, view_b)

    def rows_of(*shape):
        return pl.BlockSpec(shape, lambda i: (0,) * (len(shape) - 2) + (i, 0))

    def once(*shape):
        return pl.BlockSpec(shape, lambda i: (0,) * len(shape), pipeline_mode=pl.Buffered(1))

    grad_a, grad_b = pl.pallas_call(
        gradients,
        grid=(BANDS,),
        out_shape=(jax.ShapeDtypeStruct((rows, width), F32),) * 2,
        in_specs=[rows_of(band, width)] * 2 + [rows_of(3, band, width)] * 2
        + [once(BANDS * width, width)] * 4 + [once(4, 8, width)] * 2 + [once(8, width)],
        out_specs=(rows_of(band, width),) * 2,
        scratch_shapes=[pltpu.VMEM((band, 4 * width), BF16), pltpu.VMEM((band, 4 * width), BF16)],
        compiler_params=pltpu.CompilerParams(vmem_limit_bytes=48 * 1024 * 1024),
        cost_estimate=pl.CostEstimate(
            flops=2 * 3 * 8 * rows * width * width, bytes_accessed=56 * rows * width, transcendentals=0
        ),
    )(view_a, view_b, ra, rb, ct_hi, ct_lo, cb_hi, cb_lo, st_a, st_b, vectors)
    return grad_a, grad_b, loss[0, 0]


def solution(mesh):
    spec = P("batch", "feat")
    return jax.shard_map(
        local, mesh=mesh, in_specs=(spec, spec), out_specs=(spec, spec, P()), check_vma=False
    )
```

```python
import functools

import jax
import jax.numpy as jnp
from jax import lax
from jax.experimental import pallas as pl
from jax.experimental.pallas import tpu as pltpu
from jax.sharding import PartitionSpec as P

MESH = pl.DeviceIdType.MESH
F32 = jnp.float32
BF16 = jnp.bfloat16

eps = 1e-05
off_weight = 0.25

NZ = 8
NX = 4
NY = 4
NF = 16
PARTS = 8
BANDS = 4
HOPS = 4


def mod(value, n):
    return lax.rem(value + n, n)


def split(value):
    hi = value.astype(BF16)
    return hi, (value - hi.astype(F32)).astype(BF16)


def dot3(left, right, transposed=False):
    dims = (((1,), (1 if transposed else 0,)), ((), ()))
    dot = functools.partial(lax.dot_general, dimension_numbers=dims, preferred_element_type=F32)
    return dot(left[0], right[0]) + dot(left[0], right[1]) + dot(left[1], right[0])


def kernel(
    a_hbm, b_hbm, ga_hbm, gb_hbm, loss_ref,
    raw_a, raw_b, at_hi, at_lo, b_hi, b_lo, tiles, rs_p, rs_m, y_recv, fin, cfull, c_hi, c_lo,
    g_a, g_b, relay, st_z, st_y, st_a, st_b, squares, columns, means, l_z, l_send, l_recv,
    in_sem, out_sem, direct_s, direct_r, fwd_s, fwd_r, far_s, far_r, rel_s, rel_r,
    stz_s, stz_r, sty_s, sty_r, stf_s, stf_r, rs_s, rs_r, y_s, y_r, hand_s, hand_r,
    ag_s, ag_r, ay_s, ay_r, lz_s, lz_r, loss_s, loss_r,
):
    rows, width = a_hbm.shape
    part = rows // PARTS
    band = rows // BANDS
    chunk = width // NZ
    half = chunk // 2
    total = float(rows * 2 * NZ)
    features = float(width * NF)

    batch = lax.axis_index("batch")
    feat = lax.axis_index("feat")
    z = lax.div(batch, 2)
    y_lo = lax.rem(batch, 2)
    y = lax.div(feat, 2 * NX) * 2 + y_lo
    x = lax.rem(lax.div(feat, 2), NX)
    core = lax.rem(feat, 2)
    even = core == 0
    odd = core == 1
    first_x = x == 0
    last_x = x == NX - 1
    seam = jnp.logical_or(first_x, last_x)

    def at_feat(f):
        return {"batch": batch, "feat": f}

    def at_z(z_other):
        return {"batch": z_other * 2 + y_lo, "feat": feat}

    def at_xy(x_other, y_other):
        f = lax.div(y_other, 2) * (2 * NX) + x_other * 2 + core
        return {"batch": z * 2 + lax.rem(y_other, 2), "feat": f}

    def neighbour(steps):
        return at_feat(mod(feat + steps, NF))

    def crossed(stride):
        return at_feat(feat + stride - 2 * stride * lax.rem(lax.div(feat, stride), 2))

    other_core = crossed(1)
    other_y = {"batch": batch + 1 - 2 * y_lo, "feat": feat}
    above = at_z(mod(z + 1, NZ))
    below = at_z(mod(z - 1, NZ))
    mirror_x = NX - 1 - x
    ahead_crossed = at_feat(mod(feat + 3 - 2 * core, NF))

    def send(src, dst, s_sem, r_sem, device):
        return pltpu.make_async_remote_copy(
            src_ref=src, dst_ref=dst, send_sem=s_sem, recv_sem=r_sem,
            device_id=device, device_id_type=MESH,
        )

    def landed(dst, r_sem, s_sem):
        send(dst, dst, s_sem, r_sem, other_core).wait_recv()

    load_b = pltpu.make_async_copy(b_hbm, raw_b.at[0], in_sem.at[0])
    load_a = pltpu.make_async_copy(a_hbm, raw_a.at[0], in_sem.at[1])
    load_b.start()
    load_a.start()

    barrier = pltpu.get_barrier_semaphore()
    friends = [neighbour(k) for k in (-3, -2, -1, 1, 2, 3)]
    friends += [crossed(k) for k in (2, 4, 8)]
    friends += [at_z(mod(z + d, NZ)) for d in range(1, NZ)]
    friends += [other_y]
    for friend in friends:
        pl.semaphore_signal(barrier, inc=1, device_id=friend, device_id_type=MESH)

    @pl.when(seam)
    def _():
        for friend in (
            at_xy(mirror_x, mod(y - 1, NY)), at_xy(mirror_x, mod(y + 1, NY)),
            at_xy(x, mod(y - 1, NY)), at_xy(x, mod(y + 1, NY)),
        ):
            pl.semaphore_signal(barrier, inc=1, device_id=friend, device_id_type=MESH)

    pl.semaphore_wait(barrier, jnp.where(seam, len(friends) + 4, len(friends)))


    def piece(c):
        return pl.ds(pl.multiple_of(c * part, part), part)

    def direct(view, c):
        src, raw, steps = ((a_hbm, raw_a, 2), (b_hbm, raw_b, -2))[view]
        return send(
            src.at[piece(c)], raw.at[1, piece(c)], direct_s.at[view, c], direct_r.at[view, c],
            neighbour(steps),
        )

    def to_relay(view, c):
        src = (a_hbm, b_hbm)[view]
        return send(
            src.at[piece(c)], relay.at[c - PARTS // 2], direct_s.at[view, c],
            rel_r.at[c - PARTS // 2], at_xy(mirror_x, mod(y - 1, NY)),
        )

    def from_relay(view, r):
        raw = (raw_a, raw_b)[view]
        c = r + PARTS // 2
        return send(
            relay.at[r], raw.at[1, piece(c)], rel_s.at[r], direct_r.at[view, c],
            at_xy(x, mod(y - 1, NY)),
        )

    for c in (0, 4, 1, 5, 2, 6, 3, 7):
        for view, edge in ((1, first_x), (0, last_x)):
            if c < PARTS // 2:
                direct(view, c).start()
            else:
                @pl.when(edge)
                def _():
                    to_relay(view, c).start()

                @pl.when(jnp.logical_not(edge))
                def _():
                    direct(view, c).start()

    raws = (raw_a, raw_b)

    def quarter(j):
        return pl.ds(j * band, band)

    def far(view, j, src=None):
        raw = raws[view]
        src = raw.at[1] if src is None else src
        return send(
            src.at[quarter(j)], raw.at[3, quarter(j)], far_s.at[view, j], far_r.at[view, j],
            neighbour(1 - 2 * view),
        )

    def far_take(view):
        for j in range(BANDS):
            far(view, j).wait_recv()

    @pl.when(even)
    def _():
        for j in range(BANDS):
            far(0, j, a_hbm).start()

    load_b.wait()
    load_a.wait()
    strip = 128
    for view, raw in ((0, raw_a), (1, raw_b)):
        def add_up(i, acc):
            v = raw[0, pl.ds(pl.multiple_of(i * strip, strip), strip), :]
            return acc + jnp.sum(v.reshape(strip // 8, 8, width), axis=0)

        zeros = jnp.zeros((8, width), F32)
        acc = lax.fori_loop(0, rows // strip, add_up, zeros)
        mean = jnp.sum(acc, axis=0, keepdims=True) * (1.0 / rows)

        def add_up_squares(i, carry):
            rest, square = carry
            v = raw[0, pl.ds(pl.multiple_of(i * strip, strip), strip), :] - mean
            v = v.reshape(strip // 8, 8, width)
            return rest + jnp.sum(v, axis=0), square + jnp.sum(v * v, axis=0)

        rest, square = lax.fori_loop(0, rows // strip, add_up_squares, (zeros, zeros))
        st_z[z, pl.ds(3 * view, 1), :] = mean
        st_z[z, pl.ds(3 * view + 1, 1), :] = jnp.sum(square, axis=0, keepdims=True)
        st_z[z, pl.ds(3 * view + 2, 1), :] = jnp.sum(rest, axis=0, keepdims=True)

    def stat_z(d):
        return send(
            st_z.at[z], st_z.at[z], stz_s.at[d], stz_r.at[d], at_z(mod(z + d, NZ))
        )

    for d in range(1, NZ):
        stat_z(d).start()
    for d in range(1, NZ):
        landed(st_z.at[mod(z - d, NZ)], stz_r.at[d], stz_s.at[d])
    for view in (0, 1):
        means_z = [st_z[i, pl.ds(3 * view, 1), :] for i in range(NZ)]
        mean = sum(means_z[1:], means_z[0]) * (1.0 / NZ)
        square = jnp.zeros((1, width), F32)
        rest = jnp.zeros((1, width), F32)
        for i in range(NZ):
            off = means_z[i] - mean
            square = square + (st_z[i, pl.ds(3 * view + 1, 1), :] + float(rows) * off * off)
            rest = rest + (st_z[i, pl.ds(3 * view + 2, 1), :] + float(rows) * off)
        st_y[0, pl.ds(3 * view, 1), :] = mean
        st_y[0, pl.ds(3 * view + 1, 1), :] = square
        st_y[0, pl.ds(3 * view + 2, 1), :] = rest
    stat_y = send(st_y.at[0], st_y.at[1], sty_s, sty_r, other_y)
    stat_y.start()
    stat_y.wait_recv()
    rows_z = float(rows * NZ)
    for view, st in ((0, st_a), (1, st_b)):
        mean0, mean1 = (st_y[i, pl.ds(3 * view, 1), :] for i in (0, 1))
        mean = 0.5 * (mean0 + mean1)
        off0, off1 = mean0 - mean, mean1 - mean
        square = (
            st_y[0, pl.ds(3 * view + 1, 1), :] + st_y[1, pl.ds(3 * view + 1, 1), :]
            + rows_z * (off0 * off0 + off1 * off1)
        )
        rest = (
            st_y[0, pl.ds(3 * view + 2, 1), :] + st_y[1, pl.ds(3 * view + 2, 1), :]
            + rows_z * (off0 + off1)
        )
        inverse = 1.0 / jnp.sqrt(square * (1.0 / total) + eps)
        st[0, pl.ds(0, 1), :] = mean
        st[0, pl.ds(1, 1), :] = inverse
        st[0, pl.ds(2, 1), :] = rest * (1.0 / total) * inverse

    def stat_f(view, k):
        st = (st_a, st_b)[view]
        if k == 2:
            slot = 1
        elif (k == 1) == (view == 1):
            slot = 2 + core
        else:
            slot = 3 - core
        return send(
            st.at[0], st.at[slot], stf_s.at[view, k], stf_r.at[view, slot],
            neighbour(-k if view == 1 else k),
        )

    for k in (2, 1, 3):
        for view in (1, 0):
            stat_f(view, k).start()

    def normal(raw, st, slot, rows_here):
        return (raw[slot, rows_here, :] - st[slot, pl.ds(0, 1), :]) * st[slot, pl.ds(1, 1), :]

    def add_tile(t, c, left_hi, left_lo, first):
        right = (b_hi[...], b_lo[...])
        def rows_of(i, carry):
            here = pl.ds(pl.multiple_of(i * (width // 2), width // 2), width // 2)
            out = dot3((left_hi[c, here, :], left_lo[c, here, :]), right)
            if first:
                tiles[t, here, :] = out
            else:
                tiles[t, here, :] = tiles[t, here, :] + out
            return carry
        lax.fori_loop(0, 2, rows_of, 0)

    def band_of(c):
        return pl.ds(pl.multiple_of(c * band, band), band)

    def turn_a(slot, c, index):
        hi, lo = split(normal(raw_a, st_a, slot, band_of(c)).T)
        at_hi[index] = hi
        at_lo[index] = lo

    def take_b(slot, c):
        hi, lo = split(normal(raw_b, st_b, slot, band_of(c)))
        b_hi[...] = hi
        b_lo[...] = lo

    def clear(t, carry):
        tiles[t] = jnp.zeros((width, width), F32)
        return carry

    lax.fori_loop(0, 4, clear, 0)

    def own_tile(c, carry):
        turn_a(0, c, c)
        take_b(0, c)
        add_tile(0, c, at_hi, at_lo, False)
        return carry

    lax.fori_loop(0, BANDS, own_tile, 0)

    def dest(q):
        return pl.multiple_of(mod(q, NZ) * chunk, chunk)

    def sum_send(t, s):
        if s == 0:
            up = pl.ds(dest(z + HOPS), half)
            down = pl.ds(pl.multiple_of(dest(z + HOPS) + half, half), half)
            up_to, down_to = pl.ds(0, half), pl.ds(half, half)
        else:
            up, down = pl.ds(dest(z + HOPS - s), chunk), pl.ds(dest(z - HOPS + s), chunk)
            up_to = down_to = pl.ds(0, chunk)
        return (
            send(tiles.at[t, up], rs_p.at[t, s, up_to], rs_s.at[0, t, s], rs_r.at[0, t, s], above),
            send(tiles.at[t, down], rs_m.at[t, s, down_to], rs_s.at[1, t, s], rs_r.at[1, t, s], below),
        )

    def sum_start(t, s):
        for copy in sum_send(t, s):
            copy.start()

    def sum_take(t, s):
        for copy in sum_send(t, s):
            copy.wait_recv()
        for recv, q, low in ((rs_p, z + HOPS - 1 - s, 0), (rs_m, z - HOPS + 1 + s, half)):
            if s == 0:
                here = pl.ds(pl.multiple_of(dest(q) + low, half), half)
                tiles[t, here, :] = tiles[t, here, :] + recv[t, s, pl.ds(low, half), :]
            else:
                here = pl.ds(dest(q), chunk)
                tiles[t, here, :] = tiles[t, here, :] + recv[t, s]

    mine = pl.ds(dest(z), chunk)

    def y_copy(t):
        return send(tiles.at[t, mine], y_recv.at[t], y_s.at[t], y_r.at[t], other_y)

    def sum_end(t):
        sum_take(t, HOPS - 1)
        y_copy(t).start()

    def sum_all(t):
        y_copy(t).wait_recv()
        return (tiles[t, mine, :] + y_recv[t]) * (1.0 / total)

    def gather_part(s, mover):
        up, down = z - s - mover, z + s + mover
        if s < HOPS - 1:
            return pl.ds(dest(up), chunk), pl.ds(dest(down), chunk)
        return pl.ds(dest(up), half), pl.ds(pl.multiple_of(dest(down) + half, half), half)

    def gather_send(lane, u, s):
        up, down = gather_part(s, 0)
        return (
            send(cfull.at[u, up], cfull.at[u, up], ag_s.at[0, lane, s], ag_r.at[0, lane, s], above),
            send(cfull.at[u, down], cfull.at[u, down], ag_s.at[1, lane, s], ag_r.at[1, lane, s], below),
        )

    def gather_start(lane, u, s):
        for copy in gather_send(lane, u, s):
            copy.start()

    def across(lane, u, s, i):
        p = gather_part(s, 1)[i]
        return send(cfull.at[u, p], cfull.at[u, p], ay_s.at[i, lane, s], ay_r.at[i, lane, s], other_y)

    def gather_take(lane, u, s):
        for i, p in enumerate(gather_part(s, 1)):
            landed(cfull.at[u, p], ag_r.at[i, lane, s], ag_s.at[i, lane, s])
            if lane < 2:
                across(lane, u, s, i).start()
        if s < HOPS - 1:
            gather_start(lane, u, s + 1)

    def gather_other(lane, u):
        for s in range(HOPS):
            for i in (0, 1):
                across(lane, u, s, i).wait_recv()

    lane_tile = (1 + y_lo, 4 + y_lo, 0, 3 + 3 * core, 6 - 3 * core)
    other_tile = (2 - y_lo, 5 - y_lo)

    def gather(lane, s):
        if s < 0:
            gather_start(lane, lane_tile[lane], 0)
        else:
            gather_take(lane, lane_tile[lane], s)

    hand1 = send(cfull.at[1, mine], cfull.at[4, mine], hand_s.at[0], hand_r.at[4], neighbour(2))
    hand2 = send(cfull.at[2, mine], cfull.at[5, mine], hand_s.at[1], hand_r.at[5], ahead_crossed)
    hand3 = send(fin, cfull.at[3, mine], hand_s.at[2], hand_r.at[3], neighbour(-1))
    hand6 = send(fin, cfull.at[6, mine], hand_s.at[3], hand_r.at[6], neighbour(2))

    def hand_take(u):
        landed(cfull.at[u, mine], hand_r.at[u], hand_s.at[0])

    def when(cond, f, *args):
        @pl.when(cond)
        def _():
            f(*args)

    def sum_step(t, s):
        if s < HOPS - 1:
            sum_take(t, s)
            sum_start(t, s + 1)
        else:
            sum_end(t)

    def end_0():
        cfull[0, mine, :] = sum_all(0)

    def end_1():
        cfull[1, mine, :] = sum_all(1)
        hand1.start()

    def end_2():
        cfull[2, mine, :] = sum_all(2)
        hand2.start()

    def end_3_odd():
        last = sum_all(3)
        fin[...] = last
        hand3.start()
        cfull[6, mine, :] = last

    def end_3_even():
        fin[...] = sum_all(3)
        hand3.start()
        hand6.start()

    def forward(view, c):
        raw = (raw_a, raw_b)[view]
        return send(
            raw.at[1, piece(c)], raw.at[2, piece(c)], fwd_s.at[view, c], fwd_r.at[view, c],
            other_core,
        )

    sum_start(0, 0)
    for slot in (3, 1, 2):
        for view, st in ((1, st_b), (0, st_a)):
            landed(st.at[slot], stf_r.at[view, slot], stf_s.at[view, slot])

    def fourth():
        far_take(0)

        def fourth_tile(c, carry):
            turn_a(3, c, BANDS)
            take_b(0, c)
            add_tile(3, BANDS, at_hi, at_lo, False)
            return carry

        lax.fori_loop(0, BANDS, fourth_tile, 0)
        sum_start(3, 0)

    def early(j):
        if j < HOPS:
            sum_step(0, j)
        else:
            when(odd, sum_step, 3, j - HOPS)
            if j == HOPS:
                end_0()
            gather(2, j - HOPS - 1)

    for c in range(BANDS):
        for j in (2 * c, 2 * c + 1):
            if j < PARTS // 2:
                for view, edge in ((1, last_x), (0, first_x)):
                    @pl.when(edge)
                    def _():
                        landed(relay.at[j], rel_r.at[j], rel_s.at[j])
                        from_relay(view, j).start()

            direct(1, j).wait_recv()
            forward(1, j).start()
            direct(0, j).wait_recv()
            when(odd, lambda: forward(0, j).start())
            early(j)
        take_b(1, c)
        add_tile(1, c, at_hi, at_lo, False)

        @pl.when(even)
        def _():
            for j in (2 * c, 2 * c + 1):
                forward(0, j).wait_recv()
            turn_a(2, c, BANDS)
            add_tile(3, BANDS, at_hi, at_lo, False)

        for j in (2 * c, 2 * c + 1):
            forward(1, j).wait_recv()
        take_b(2, c)
        add_tile(2, c, at_hi, at_lo, False)
        if c == 1:
            when(odd, fourth)

    @pl.when(even)
    def _():
        for j in range(PARTS):
            forward(0, j).start()

    @pl.when(odd)
    def _():
        for j in range(BANDS):
            far(1, j, b_hbm).start()

    def late_start(j):
        when(even, lambda: far(1, j).start())
        when(odd, lambda: far(0, j).start())

    for t in (1, 2):
        sum_start(t, 0)
    when(even, sum_start, 3, 0)

    squares[...] = jnp.zeros_like(squares)
    columns[...] = jnp.zeros_like(columns)
    means[...] = jnp.zeros_like(means)

    def clear_g(i, carry):
        g_a[band_of(i), :] = jnp.zeros((band, width), F32)
        g_b[band_of(i), :] = jnp.zeros((band, width), F32)
        return carry

    lax.fori_loop(0, BANDS, clear_g, 0)

    def grow(view, slot, u):
        g, raw, st = ((g_a, raw_b, st_b), (g_b, raw_a, st_a))[view]
        c = cfull[u]
        hi, lo = split(c)
        c_hi[...] = hi
        c_lo[...] = lo
        if view == 0:
            acc = squares[...]
            for j in range(width // 128):
                part_j = c[:, j * 128:(j + 1) * 128]
                acc = acc + part_j * part_j
            squares[...] = acc
        else:
            columns[...] = columns[...] + jnp.sum((c * c).reshape(width // 8, 8, width), axis=0)

        def body(i, carry):
            here = band_of(i)
            n = split(normal(raw, st, slot, here))
            g[here, :] = g[here, :] + dot3(n, (c_hi[...], c_lo[...]), view == 0)
            return carry

        lax.fori_loop(0, BANDS, body, 0)
        m = split(jnp.broadcast_to(st[slot, pl.ds(2, 1), :], (16, width)))
        means[view] = means[view] + dot3(m, (c_hi[...], c_lo[...]), view == 0)

    def loss_part():
        value = jnp.zeros((8, 128), F32)
        for t in range(4):
            c = fin[...] if t == 3 else cfull[t, mine, :]
            terms = off_weight * c * c
            if t == 0:
                shape = (chunk, width)
                on = lax.broadcasted_iota(jnp.int32, shape, 1) == (
                    lax.broadcasted_iota(jnp.int32, shape, 0) + z * chunk
                )
                terms = jnp.where(on, (1.0 - c) * (1.0 - c), terms)
            terms = jnp.sum(terms.reshape(chunk // 8, 8, width), axis=0)
            for j in range(width // 128):
                value = value + terms[:, j * 128:(j + 1) * 128]
        l_z[z] = value

    def loss_z(d):
        return send(l_z.at[z], l_z.at[z], lz_s.at[d], lz_r.at[d], at_z(mod(z + d, NZ)))

    def loss_copy(r):
        return send(l_send.at[r], l_recv.at[r], loss_s.at[r], loss_r.at[r], crossed(1 << r))

    def loss_start():
        for d in range(1, NZ):
            landed(l_z.at[mod(z - d, NZ)], lz_r.at[d], lz_s.at[d])
        value = l_z[0]
        for i in range(1, NZ):
            value = value + l_z[i]
        l_send[0] = value
        loss_copy(0).start()

    def loss_step(r):
        loss_copy(r).wait_recv()
        l_send[r + 1] = l_send[r] + l_recv[r]
        if r < 3:
            loss_copy(r + 1).start()

    def sum_round(s):
        for t in (1, 2):
            sum_step(t, s)
        when(even, sum_step, 3, s)
        late_start(s)

    when(odd, end_3_odd)
    gather(2, 3)
    grow(0, 0, 0)
    sum_round(0)
    when(even, hand_take, 3)
    gather(3, -1)
    grow(1, 0, 0)
    sum_round(1)
    gather(3, 0)
    sum_round(2)
    gather(3, 1)
    sum_round(3)
    gather(3, 2)
    end_1()
    end_2()
    gather(0, -1)
    gather(3, 3)
    when(even, end_3_even)
    loss_part()
    for d in range(1, NZ):
        loss_z(d).start()
    hand_take(4)
    hand_take(5)
    gather(1, -1)
    gather(0, 0)
    when(even, hand_take, 6)
    when(odd, hand_take, 3)
    gather(4, -1)
    gather(1, 0)
    gather(0, 1)
    gather(4, 0)
    gather(1, 1)
    gather(0, 2)
    loss_start()
    gather(4, 1)
    gather(1, 2)

    @pl.when(even)
    def _():
        far_take(1)
        grow(0, 3, 3)

    when(odd, grow, 1, 3, 6)
    gather(0, 3)
    grow(0, 1 + y_lo, lane_tile[0])
    loss_step(0)
    gather(4, 2)
    gather(1, 3)

    @pl.when(odd)
    def _():
        for j in range(PARTS):
            forward(0, j).wait_recv()

    grow(1, 1 + y_lo, lane_tile[1])
    loss_step(1)
    gather(4, 3)
    gather_other(0, other_tile[0])
    grow(0, 2 - y_lo, other_tile[0])
    loss_step(2)
    gather_other(1, other_tile[1])
    grow(1, 2 - y_lo, other_tile[1])
    loss_step(3)

    @pl.when(odd)
    def _():
        far_take(1)
        grow(0, 3, 3)

    @pl.when(even)
    def _():
        far_take(0)
        grow(1, 3, 6)

    loss_ref[0, 0] = jnp.sum(l_send[4]) * (1.0 / features)

    diagonal = []
    one_block = (
        lax.broadcasted_iota(jnp.int32, (128, 128), 0) == lax.broadcasted_iota(jnp.int32, (128, 128), 1)
    )
    for j in range(width // 128):
        block = cfull[0, j * 128:(j + 1) * 128, j * 128:(j + 1) * 128]
        diagonal.append(jnp.sum(jnp.where(one_block, block, 0.0), axis=0, keepdims=True))
    diagonal = jnp.concatenate(diagonal, axis=1)
    change = -(1.0 - diagonal) - off_weight * diagonal
    row_squares = jnp.sum(squares[...].T, axis=0, keepdims=True)
    column_squares = jnp.sum(columns[...], axis=0, keepdims=True)
    back_a = off_weight * row_squares + change * diagonal
    back_b = off_weight * column_squares + change * diagonal
    mean_a = off_weight * means[0, pl.ds(0, 1), :] + st_b[0, pl.ds(2, 1), :] * change
    mean_b = off_weight * means[1, pl.ds(0, 1), :] + st_a[0, pl.ds(2, 1), :] * change

    def out_copy(view, i):
        src, dst = ((g_a, ga_hbm), (g_b, gb_hbm))[view]
        return pltpu.make_async_copy(src.at[band_of(i)], dst.at[band_of(i)], out_sem.at[view, i])

    def finish(i, carry):
        here = band_of(i)
        n_a = normal(raw_a, st_a, 0, here)
        n_b = normal(raw_b, st_b, 0, here)
        g_a[here, :] = (off_weight * g_a[here, :] + n_b * change - mean_a - n_a * back_a) * st_a[0, pl.ds(1, 1), :]
        out_copy(0, i).start()
        g_b[here, :] = (off_weight * g_b[here, :] + n_a * change - mean_b - n_b * back_b) * st_b[0, pl.ds(1, 1), :]
        out_copy(1, i).start()
        return carry

    lax.fori_loop(0, BANDS, finish, 0)

    for view, edge in ((1, first_x), (0, last_x)):
        for c in range(PARTS):
            direct(view, c).wait_send()
            forward(view, c).wait_send()
    for view in (0, 1):
        for j in range(BANDS):
            far(view, j).wait_send()

    @pl.when(seam)
    def _():
        for r in range(PARTS // 2):
            from_relay(0, r).wait_send()

    for d in range(1, NZ):
        stat_z(d).wait_send()
    stat_y.wait_send()
    for k in (1, 2, 3):
        for view in (0, 1):
            stat_f(view, k).wait_send()
    for t in range(4):
        for s in range(HOPS):
            for copy in sum_send(t, s):
                copy.wait_send()
        y_copy(t).wait_send()
    hand1.wait_send()
    hand2.wait_send()
    hand3.wait_send()

    @pl.when(even)
    def _():
        hand6.wait_send()

    for lane in range(5):
        for s in range(HOPS):
            for copy in gather_send(lane, lane_tile[lane], s):
                copy.wait_send()
            if lane < 2:
                for i in (0, 1):
                    across(lane, lane_tile[lane], s, i).wait_send()
    for d in range(1, NZ):
        loss_z(d).wait_send()
    for r in range(4):
        loss_copy(r).wait_send()
    for view in (0, 1):
        for i in range(BANDS):
            out_copy(view, i).wait()


def local(view_a, view_b):
    rows, width = view_a.shape
    part = rows // PARTS
    band = rows // BANDS
    chunk = width // NZ
    dma = pltpu.SemaphoreType.DMA
    anywhere = pl.BlockSpec(memory_space=pl.ANY)
    grad_a, grad_b, loss = pl.pallas_call(
        kernel,
        out_shape=(
            jax.ShapeDtypeStruct((rows, width), F32),
            jax.ShapeDtypeStruct((rows, width), F32),
            jax.ShapeDtypeStruct((1, 1), F32),
        ),
        in_specs=[anywhere, anywhere],
        out_specs=(anywhere, anywhere, pl.BlockSpec(memory_space=pltpu.SMEM)),
        scratch_shapes=[
            pltpu.VMEM((4, rows, width), F32),
            pltpu.VMEM((4, rows, width), F32),
            pltpu.VMEM((BANDS + 1, width, band), BF16),
            pltpu.VMEM((BANDS + 1, width, band), BF16),
            pltpu.VMEM((band, width), BF16),
            pltpu.VMEM((band, width), BF16),
            pltpu.VMEM((4, width, width), F32),
            pltpu.VMEM((4, HOPS, chunk, width), F32),
            pltpu.VMEM((4, HOPS, chunk, width), F32),
            pltpu.VMEM((4, chunk, width), F32),
            pltpu.VMEM((chunk, width), F32),
            pltpu.VMEM((7, width, width), F32),
            pltpu.VMEM((width, width), BF16),
            pltpu.VMEM((width, width), BF16),
            pltpu.VMEM((rows, width), F32),
            pltpu.VMEM((rows, width), F32),
            pltpu.VMEM((PARTS // 2, part, width), F32),
            pltpu.VMEM((NZ, 8, width), F32),
            pltpu.VMEM((2, 8, width), F32),
            pltpu.VMEM((4, 8, width), F32),
            pltpu.VMEM((4, 8, width), F32),
            pltpu.VMEM((width, 128), F32),
            pltpu.VMEM((8, width), F32),
            pltpu.VMEM((2, 16, width), F32),
            pltpu.VMEM((NZ, 8, 128), F32),
            pltpu.VMEM((5, 8, 128), F32),
            pltpu.VMEM((4, 8, 128), F32),
            dma((2,)),
            dma((2, BANDS)),
            dma((2, PARTS)), dma((2, PARTS)),
            dma((2, PARTS)), dma((2, PARTS)),
            dma((2, BANDS)), dma((2, BANDS)),
            dma((PARTS // 2,)), dma((PARTS // 2,)),
            dma((NZ,)), dma((NZ,)),
            dma(()), dma(()),
            dma((2, 4)), dma((2, 4)),
            dma((2, 4, HOPS)), dma((2, 4, HOPS)),
            dma((4,)), dma((4,)),
            dma((4,)), dma((7,)),
            dma((2, 5, HOPS)), dma((2, 5, HOPS)),
            dma((2, 2, HOPS)), dma((2, 2, HOPS)),
            dma((NZ,)), dma((NZ,)),
            dma((4,)), dma((4,)),
        ],
        compiler_params=pltpu.CompilerParams(
            collective_id=0, has_side_effects=True, vmem_limit_bytes=60 * 1024 * 1024
        ),
        cost_estimate=pl.CostEstimate(
            flops=2 * 3 * 12 * rows * width * width, bytes_accessed=16 * rows * width, transcendentals=0
        ),
    )(view_a, view_b)
    return grad_a, grad_b, loss[0, 0]


def solution(mesh):
    spec = P("batch", "feat")
    return jax.shard_map(
        local, mesh=mesh, in_specs=(spec, spec), out_specs=(spec, spec, P()), check_vma=False
    )
```

```python
import functools

import jax
import jax.numpy as jnp
from jax import lax
from jax.experimental import pallas as pl
from jax.experimental.pallas import tpu as pltpu
from jax.sharding import PartitionSpec as P

MESH = pl.DeviceIdType.MESH
F32 = jnp.float32
BF16 = jnp.bfloat16

eps = 1e-05
off_weight = 0.25

NZ = 8
NX = 4
NY = 4
NF = 16
PARTS = 8
BANDS = 4
HOPS = 4


def mod(value, n):
    return lax.rem(value + n, n)


def split(value):
    hi = value.astype(BF16)
    return hi, (value - hi.astype(F32)).astype(BF16)


def dot3(left, right, transposed=False):
    dims = (((1,), (1 if transposed else 0,)), ((), ()))
    dot = functools.partial(lax.dot_general, dimension_numbers=dims, preferred_element_type=F32)
    return dot(left[0], right[0]) + dot(left[0], right[1]) + dot(left[1], right[0])


def kernel(
    a_hbm, b_hbm, ga_hbm, gb_hbm, loss_ref,
    raw_a, raw_b, at_hi, at_lo, b_hi, b_lo, tiles, rs_p, rs_m, y_recv, fin, cfull, c_hi, c_lo,
    g_a, g_b, relay, st_z, st_y, st_a, st_b, squares, columns, means, l_z, l_send, l_recv,
    in_sem, out_sem, direct_s, direct_r, fwd_s, fwd_r, far_s, far_r, rel_s, rel_r,
    stz_s, stz_r, sty_s, sty_r, stf_s, stf_r, rs_s, rs_r, y_s, y_r, hand_s, hand_r,
    ag_s, ag_r, ay_s, ay_r, lz_s, lz_r, loss_s, loss_r,
):
    rows, width = a_hbm.shape
    part = rows // PARTS
    band = rows // BANDS
    chunk = width // NZ
    half = chunk // 2
    total = float(rows * 2 * NZ)
    features = float(width * NF)

    batch = lax.axis_index("batch")
    feat = lax.axis_index("feat")
    z = lax.div(batch, 2)
    y_lo = lax.rem(batch, 2)
    y = lax.div(feat, 2 * NX) * 2 + y_lo
    x = lax.rem(lax.div(feat, 2), NX)
    core = lax.rem(feat, 2)
    even = core == 0
    odd = core == 1
    first_x = x == 0
    last_x = x == NX - 1
    seam = jnp.logical_or(first_x, last_x)

    def at_feat(f):
        return {"batch": batch, "feat": f}

    def at_z(z_other):
        return {"batch": z_other * 2 + y_lo, "feat": feat}

    def at_xy(x_other, y_other):
        f = lax.div(y_other, 2) * (2 * NX) + x_other * 2 + core
        return {"batch": z * 2 + lax.rem(y_other, 2), "feat": f}

    def neighbour(steps):
        return at_feat(mod(feat + steps, NF))

    def crossed(stride):
        return at_feat(feat + stride - 2 * stride * lax.rem(lax.div(feat, stride), 2))

    other_core = crossed(1)
    other_y = {"batch": batch + 1 - 2 * y_lo, "feat": feat}
    above = at_z(mod(z + 1, NZ))
    below = at_z(mod(z - 1, NZ))
    mirror_x = NX - 1 - x
    ahead_crossed = at_feat(mod(feat + 3 - 2 * core, NF))

    def send(src, dst, s_sem, r_sem, device):
        return pltpu.make_async_remote_copy(
            src_ref=src, dst_ref=dst, send_sem=s_sem, recv_sem=r_sem,
            device_id=device, device_id_type=MESH,
        )

    def landed(dst, r_sem, s_sem):
        send(dst, dst, s_sem, r_sem, other_core).wait_recv()

    load_b = pltpu.make_async_copy(b_hbm, raw_b.at[0], in_sem.at[0])
    load_a = pltpu.make_async_copy(a_hbm, raw_a.at[0], in_sem.at[1])
    load_b.start()
    load_a.start()

    barrier = pltpu.get_barrier_semaphore()
    friends = [neighbour(k) for k in (-3, -2, -1, 1, 2, 3)]
    friends += [crossed(k) for k in (2, 4, 8)]
    friends += [at_z(mod(z + d, NZ)) for d in range(1, NZ)]
    friends += [other_y]
    for friend in friends:
        pl.semaphore_signal(barrier, inc=1, device_id=friend, device_id_type=MESH)

    @pl.when(seam)
    def _():
        for friend in (
            at_xy(mirror_x, mod(y - 1, NY)), at_xy(mirror_x, mod(y + 1, NY)),
            at_xy(x, mod(y - 1, NY)), at_xy(x, mod(y + 1, NY)),
        ):
            pl.semaphore_signal(barrier, inc=1, device_id=friend, device_id_type=MESH)

    pl.semaphore_wait(barrier, jnp.where(seam, len(friends) + 4, len(friends)))


    def piece(c):
        return pl.ds(pl.multiple_of(c * part, part), part)

    def direct(view, c):
        src, raw, steps = ((a_hbm, raw_a, 2), (b_hbm, raw_b, -2))[view]
        return send(
            src.at[piece(c)], raw.at[1, piece(c)], direct_s.at[view, c], direct_r.at[view, c],
            neighbour(steps),
        )

    def to_relay(view, c):
        src = (a_hbm, b_hbm)[view]
        return send(
            src.at[piece(c)], relay.at[c - PARTS // 2], direct_s.at[view, c],
            rel_r.at[c - PARTS // 2], at_xy(mirror_x, mod(y - 1, NY)),
        )

    def from_relay(view, r):
        raw = (raw_a, raw_b)[view]
        c = r + PARTS // 2
        return send(
            relay.at[r], raw.at[1, piece(c)], rel_s.at[r], direct_r.at[view, c],
            at_xy(x, mod(y - 1, NY)),
        )

    for c in (0, 4, 1, 5, 2, 6, 3, 7):
        for view, edge in ((1, first_x), (0, last_x)):
            if c < PARTS // 2:
                direct(view, c).start()
            else:
                @pl.when(edge)
                def _():
                    to_relay(view, c).start()

                @pl.when(jnp.logical_not(edge))
                def _():
                    direct(view, c).start()

    raws = (raw_a, raw_b)

    def quarter(j):
        return pl.ds(j * band, band)

    def far(view, j, src=None):
        raw = raws[view]
        src = raw.at[1] if src is None else src
        return send(
            src.at[quarter(j)], raw.at[3, quarter(j)], far_s.at[view, j], far_r.at[view, j],
            neighbour(1 - 2 * view),
        )

    def far_take(view):
        for j in range(BANDS):
            far(view, j).wait_recv()

    @pl.when(even)
    def _():
        for j in range(BANDS):
            far(0, j, a_hbm).start()

    load_b.wait()
    load_a.wait()
    strip = 128
    for view, raw in ((0, raw_a), (1, raw_b)):
        def add_up(i, acc):
            v = raw[0, pl.ds(pl.multiple_of(i * strip, strip), strip), :]
            return acc + jnp.sum(v.reshape(strip // 8, 8, width), axis=0)

        zeros = jnp.zeros((8, width), F32)
        acc = lax.fori_loop(0, rows // strip, add_up, zeros)
        mean = jnp.sum(acc, axis=0, keepdims=True) * (1.0 / rows)

        def add_up_squares(i, carry):
            rest, square = carry
            v = raw[0, pl.ds(pl.multiple_of(i * strip, strip), strip), :] - mean
            v = v.reshape(strip // 8, 8, width)
            return rest + jnp.sum(v, axis=0), square + jnp.sum(v * v, axis=0)

        rest, square = lax.fori_loop(0, rows // strip, add_up_squares, (zeros, zeros))
        st_z[z, pl.ds(3 * view, 1), :] = mean
        st_z[z, pl.ds(3 * view + 1, 1), :] = jnp.sum(square, axis=0, keepdims=True)
        st_z[z, pl.ds(3 * view + 2, 1), :] = jnp.sum(rest, axis=0, keepdims=True)

    def stat_z(d):
        return send(
            st_z.at[z], st_z.at[z], stz_s.at[d], stz_r.at[d], at_z(mod(z + d, NZ))
        )

    for d in range(1, NZ):
        stat_z(d).start()
    for d in range(1, NZ):
        landed(st_z.at[mod(z - d, NZ)], stz_r.at[d], stz_s.at[d])
    for view in (0, 1):
        means_z = [st_z[i, pl.ds(3 * view, 1), :] for i in range(NZ)]
        mean = sum(means_z[1:], means_z[0]) * (1.0 / NZ)
        square = jnp.zeros((1, width), F32)
        rest = jnp.zeros((1, width), F32)
        for i in range(NZ):
            off = means_z[i] - mean
            square = square + (st_z[i, pl.ds(3 * view + 1, 1), :] + float(rows) * off * off)
            rest = rest + (st_z[i, pl.ds(3 * view + 2, 1), :] + float(rows) * off)
        st_y[0, pl.ds(3 * view, 1), :] = mean
        st_y[0, pl.ds(3 * view + 1, 1), :] = square
        st_y[0, pl.ds(3 * view + 2, 1), :] = rest
    stat_y = send(st_y.at[0], st_y.at[1], sty_s, sty_r, other_y)
    stat_y.start()
    stat_y.wait_recv()
    rows_z = float(rows * NZ)
    for view, st in ((0, st_a), (1, st_b)):
        mean0, mean1 = (st_y[i, pl.ds(3 * view, 1), :] for i in (0, 1))
        mean = 0.5 * (mean0 + mean1)
        off0, off1 = mean0 - mean, mean1 - mean
        square = (
            st_y[0, pl.ds(3 * view + 1, 1), :] + st_y[1, pl.ds(3 * view + 1, 1), :]
            + rows_z * (off0 * off0 + off1 * off1)
        )
        rest = (
            st_y[0, pl.ds(3 * view + 2, 1), :] + st_y[1, pl.ds(3 * view + 2, 1), :]
            + rows_z * (off0 + off1)
        )
        inverse = 1.0 / jnp.sqrt(square * (1.0 / total) + eps)
        st[0, pl.ds(0, 1), :] = mean
        st[0, pl.ds(1, 1), :] = inverse
        st[0, pl.ds(2, 1), :] = rest * (1.0 / total) * inverse

    def stat_f(view, k):
        st = (st_a, st_b)[view]
        if k == 2:
            slot = 1
        elif (k == 1) == (view == 1):
            slot = 2 + core
        else:
            slot = 3 - core
        return send(
            st.at[0], st.at[slot], stf_s.at[view, k], stf_r.at[view, slot],
            neighbour(-k if view == 1 else k),
        )

    for k in (2, 1, 3):
        for view in (1, 0):
            stat_f(view, k).start()

    def normal(raw, st, slot, rows_here):
        return (raw[slot, rows_here, :] - st[slot, pl.ds(0, 1), :]) * st[slot, pl.ds(1, 1), :]

    def add_tile(t, c, left_hi, left_lo, first):
        right = (b_hi[...], b_lo[...])
        def rows_of(i, carry):
            here = pl.ds(pl.multiple_of(i * (width // 2), width // 2), width // 2)
            out = dot3((left_hi[c, here, :], left_lo[c, here, :]), right)
            if first:
                tiles[t, here, :] = out
            else:
                tiles[t, here, :] = tiles[t, here, :] + out
            return carry
        lax.fori_loop(0, 2, rows_of, 0)

    def band_of(c):
        return pl.ds(pl.multiple_of(c * band, band), band)

    def turn_a(slot, c, index):
        hi, lo = split(normal(raw_a, st_a, slot, band_of(c)).T)
        at_hi[index] = hi
        at_lo[index] = lo

    def take_b(slot, c):
        hi, lo = split(normal(raw_b, st_b, slot, band_of(c)))
        b_hi[...] = hi
        b_lo[...] = lo

    def clear(t, carry):
        tiles[t] = jnp.zeros((width, width), F32)
        return carry

    lax.fori_loop(0, 4, clear, 0)

    def own_tile(c, carry):
        turn_a(0, c, c)
        take_b(0, c)
        add_tile(0, c, at_hi, at_lo, False)
        return carry

    lax.fori_loop(0, BANDS, own_tile, 0)

    def dest(q):
        return pl.multiple_of(mod(q, NZ) * chunk, chunk)

    def sum_send(t, s):
        if s == 0:
            up = pl.ds(dest(z + HOPS), half)
            down = pl.ds(pl.multiple_of(dest(z + HOPS) + half, half), half)
            up_to, down_to = pl.ds(0, half), pl.ds(half, half)
        else:
            up, down = pl.ds(dest(z + HOPS - s), chunk), pl.ds(dest(z - HOPS + s), chunk)
            up_to = down_to = pl.ds(0, chunk)
        return (
            send(tiles.at[t, up], rs_p.at[t, s, up_to], rs_s.at[0, t, s], rs_r.at[0, t, s], above),
            send(tiles.at[t, down], rs_m.at[t, s, down_to], rs_s.at[1, t, s], rs_r.at[1, t, s], below),
        )

    def sum_start(t, s):
        for copy in sum_send(t, s):
            copy.start()

    def sum_take(t, s):
        for copy in sum_send(t, s):
            copy.wait_recv()
        for recv, q, low in ((rs_p, z + HOPS - 1 - s, 0), (rs_m, z - HOPS + 1 + s, half)):
            if s == 0:
                here = pl.ds(pl.multiple_of(dest(q) + low, half), half)
                tiles[t, here, :] = tiles[t, here, :] + recv[t, s, pl.ds(low, half), :]
            else:
                here = pl.ds(dest(q), chunk)
                tiles[t, here, :] = tiles[t, here, :] + recv[t, s]

    mine = pl.ds(dest(z), chunk)

    def y_copy(t):
        return send(tiles.at[t, mine], y_recv.at[t], y_s.at[t], y_r.at[t], other_y)

    def sum_end(t):
        sum_take(t, HOPS - 1)
        y_copy(t).start()

    def sum_all(t):
        y_copy(t).wait_recv()
        return (tiles[t, mine, :] + y_recv[t]) * (1.0 / total)

    def gather_part(s, mover):
        up, down = z - s - mover, z + s + mover
        if s < HOPS - 1:
            return pl.ds(dest(up), chunk), pl.ds(dest(down), chunk)
        return pl.ds(dest(up), half), pl.ds(pl.multiple_of(dest(down) + half, half), half)

    def gather_send(lane, u, s):
        up, down = gather_part(s, 0)
        return (
            send(cfull.at[u, up], cfull.at[u, up], ag_s.at[0, lane, s], ag_r.at[0, lane, s], above),
            send(cfull.at[u, down], cfull.at[u, down], ag_s.at[1, lane, s], ag_r.at[1, lane, s], below),
        )

    def gather_start(lane, u, s):
        for copy in gather_send(lane, u, s):
            copy.start()

    def across(lane, u, s, i):
        p = gather_part(s, 1)[i]
        return send(cfull.at[u, p], cfull.at[u, p], ay_s.at[i, lane, s], ay_r.at[i, lane, s], other_y)

    def gather_take(lane, u, s):
        for i, p in enumerate(gather_part(s, 1)):
            landed(cfull.at[u, p], ag_r.at[i, lane, s], ag_s.at[i, lane, s])
            if lane < 2:
                across(lane, u, s, i).start()
        if s < HOPS - 1:
            gather_start(lane, u, s + 1)

    def gather_other(lane, u):
        for s in range(HOPS):
            for i in (0, 1):
                across(lane, u, s, i).wait_recv()

    lane_tile = (1 + y_lo, 4 + y_lo, 0, 3 + 3 * core, 6 - 3 * core)
    other_tile = (2 - y_lo, 5 - y_lo)

    def gather(lane, s):
        if s < 0:
            gather_start(lane, lane_tile[lane], 0)
        else:
            gather_take(lane, lane_tile[lane], s)

    hand1 = send(cfull.at[1, mine], cfull.at[4, mine], hand_s.at[0], hand_r.at[4], neighbour(2))
    hand2 = send(cfull.at[2, mine], cfull.at[5, mine], hand_s.at[1], hand_r.at[5], ahead_crossed)
    hand3 = send(fin, cfull.at[3, mine], hand_s.at[2], hand_r.at[3], neighbour(-1))
    hand6 = send(fin, cfull.at[6, mine], hand_s.at[3], hand_r.at[6], neighbour(2))

    def hand_take(u):
        landed(cfull.at[u, mine], hand_r.at[u], hand_s.at[0])

    def when(cond, f, *args):
        @pl.when(cond)
        def _():
            f(*args)

    def sum_step(t, s):
        if s < HOPS - 1:
            sum_take(t, s)
            sum_start(t, s + 1)
        else:
            sum_end(t)

    def end_0():
        cfull[0, mine, :] = sum_all(0)

    def end_1():
        cfull[1, mine, :] = sum_all(1)
        hand1.start()

    def end_2():
        cfull[2, mine, :] = sum_all(2)
        hand2.start()

    def end_3_odd():
        last = sum_all(3)
        fin[...] = last
        hand3.start()
        cfull[6, mine, :] = last

    def end_3_even():
        fin[...] = sum_all(3)
        hand3.start()
        hand6.start()

    def forward(view, c):
        raw = (raw_a, raw_b)[view]
        return send(
            raw.at[1, piece(c)], raw.at[2, piece(c)], fwd_s.at[view, c], fwd_r.at[view, c],
            other_core,
        )

    sum_start(0, 0)
    for slot in (3, 1, 2):
        for view, st in ((1, st_b), (0, st_a)):
            landed(st.at[slot], stf_r.at[view, slot], stf_s.at[view, slot])

    def fourth():
        far_take(0)

        def fourth_tile(c, carry):
            turn_a(3, c, BANDS)
            take_b(0, c)
            add_tile(3, BANDS, at_hi, at_lo, False)
            return carry

        lax.fori_loop(0, BANDS, fourth_tile, 0)
        sum_start(3, 0)

    when(odd, fourth)

    def early(j):
        if j < HOPS:
            sum_step(0, j)
            when(odd, sum_step, 3, j)
        elif j == 4:
            end_0()
            gather(2, -1)
            when(odd, end_3_odd)
        elif j == 5:
            gather(2, 0)
            when(even, hand_take, 3)
            gather(3, -1)
        else:
            gather(2, j - 5)
            gather(3, j - 6)

    for c in range(BANDS):
        for j in (2 * c, 2 * c + 1):
            if j < PARTS // 2:
                for view, edge in ((1, last_x), (0, first_x)):
                    @pl.when(edge)
                    def _():
                        landed(relay.at[j], rel_r.at[j], rel_s.at[j])
                        from_relay(view, j).start()

            direct(1, j).wait_recv()
            forward(1, j).start()
            direct(0, j).wait_recv()
            when(odd, lambda: forward(0, j).start())
            if j >= BANDS:
                when(odd, lambda: far(1, j - BANDS, b_hbm).start())
            early(j)
        take_b(1, c)
        add_tile(1, c, at_hi, at_lo, False)

        @pl.when(even)
        def _():
            for j in (2 * c, 2 * c + 1):
                forward(0, j).wait_recv()
            turn_a(2, c, BANDS)
            add_tile(3, BANDS, at_hi, at_lo, False)

        for j in (2 * c, 2 * c + 1):
            forward(1, j).wait_recv()
        take_b(2, c)
        add_tile(2, c, at_hi, at_lo, False)

    @pl.when(even)
    def _():
        for j in range(PARTS):
            forward(0, j).start()

    def late_start(j):
        when(even, lambda: far(1, j).start())
        when(odd, lambda: far(0, j).start())

    for t in (1, 2):
        sum_start(t, 0)
    when(even, sum_start, 3, 0)

    squares[...] = jnp.zeros_like(squares)
    columns[...] = jnp.zeros_like(columns)
    means[...] = jnp.zeros_like(means)

    def clear_g(i, carry):
        g_a[band_of(i), :] = jnp.zeros((band, width), F32)
        g_b[band_of(i), :] = jnp.zeros((band, width), F32)
        return carry

    lax.fori_loop(0, BANDS, clear_g, 0)

    def grow(view, slot, u):
        g, raw, st = ((g_a, raw_b, st_b), (g_b, raw_a, st_a))[view]
        c = cfull[u]
        hi, lo = split(c)
        c_hi[...] = hi
        c_lo[...] = lo
        if view == 0:
            acc = squares[...]
            for j in range(width // 128):
                part_j = c[:, j * 128:(j + 1) * 128]
                acc = acc + part_j * part_j
            squares[...] = acc
        else:
            columns[...] = columns[...] + jnp.sum((c * c).reshape(width // 8, 8, width), axis=0)

        def body(i, carry):
            here = band_of(i)
            n = split(normal(raw, st, slot, here))
            g[here, :] = g[here, :] + dot3(n, (c_hi[...], c_lo[...]), view == 0)
            return carry

        lax.fori_loop(0, BANDS, body, 0)
        m = split(jnp.broadcast_to(st[slot, pl.ds(2, 1), :], (16, width)))
        means[view] = means[view] + dot3(m, (c_hi[...], c_lo[...]), view == 0)

    def loss_part():
        value = jnp.zeros((8, 128), F32)
        for t in range(4):
            c = fin[...] if t == 3 else cfull[t, mine, :]
            terms = off_weight * c * c
            if t == 0:
                shape = (chunk, width)
                on = lax.broadcasted_iota(jnp.int32, shape, 1) == (
                    lax.broadcasted_iota(jnp.int32, shape, 0) + z * chunk
                )
                terms = jnp.where(on, (1.0 - c) * (1.0 - c), terms)
            terms = jnp.sum(terms.reshape(chunk // 8, 8, width), axis=0)
            for j in range(width // 128):
                value = value + terms[:, j * 128:(j + 1) * 128]
        l_z[z] = value

    def loss_z(d):
        return send(l_z.at[z], l_z.at[z], lz_s.at[d], lz_r.at[d], at_z(mod(z + d, NZ)))

    def loss_copy(r):
        return send(l_send.at[r], l_recv.at[r], loss_s.at[r], loss_r.at[r], crossed(1 << r))

    def loss_start():
        for d in range(1, NZ):
            landed(l_z.at[mod(z - d, NZ)], lz_r.at[d], lz_s.at[d])
        value = l_z[0]
        for i in range(1, NZ):
            value = value + l_z[i]
        l_send[0] = value
        loss_copy(0).start()

    def loss_step(r):
        loss_copy(r).wait_recv()
        l_send[r + 1] = l_send[r] + l_recv[r]
        if r < 3:
            loss_copy(r + 1).start()

    def sum_round(s):
        for t in (1, 2):
            sum_step(t, s)
        when(even, sum_step, 3, s)
        late_start(s)

    gather(2, 3)
    gather(3, 2)
    grow(0, 0, 0)
    gather(3, 3)
    sum_round(0)
    grow(1, 0, 0)
    sum_round(1)

    @pl.when(even)
    def _():
        far_take(1)
        grow(0, 3, 3)

    when(odd, grow, 1, 3, 6)
    sum_round(2)
    sum_round(3)
    end_1()
    end_2()
    gather(0, -1)
    when(even, end_3_even)
    loss_part()
    for d in range(1, NZ):
        loss_z(d).start()
    hand_take(4)
    hand_take(5)
    gather(1, -1)
    gather(0, 0)
    when(even, hand_take, 6)
    when(odd, hand_take, 3)
    gather(4, -1)
    gather(1, 0)
    gather(0, 1)
    gather(4, 0)
    gather(1, 1)
    gather(0, 2)
    loss_start()
    gather(4, 1)
    gather(1, 2)
    gather(0, 3)
    grow(0, 1 + y_lo, lane_tile[0])
    loss_step(0)
    gather(4, 2)
    gather(1, 3)

    @pl.when(odd)
    def _():
        for j in range(PARTS):
            forward(0, j).wait_recv()

    grow(1, 1 + y_lo, lane_tile[1])
    loss_step(1)
    gather(4, 3)
    gather_other(0, other_tile[0])
    grow(0, 2 - y_lo, other_tile[0])
    loss_step(2)
    gather_other(1, other_tile[1])
    grow(1, 2 - y_lo, other_tile[1])
    loss_step(3)

    @pl.when(odd)
    def _():
        far_take(1)
        grow(0, 3, 3)

    @pl.when(even)
    def _():
        far_take(0)
        grow(1, 3, 6)

    loss_ref[0, 0] = jnp.sum(l_send[4]) * (1.0 / features)

    diagonal = []
    one_block = (
        lax.broadcasted_iota(jnp.int32, (128, 128), 0) == lax.broadcasted_iota(jnp.int32, (128, 128), 1)
    )
    for j in range(width // 128):
        block = cfull[0, j * 128:(j + 1) * 128, j * 128:(j + 1) * 128]
        diagonal.append(jnp.sum(jnp.where(one_block, block, 0.0), axis=0, keepdims=True))
    diagonal = jnp.concatenate(diagonal, axis=1)
    change = -(1.0 - diagonal) - off_weight * diagonal
    row_squares = jnp.sum(squares[...].T, axis=0, keepdims=True)
    column_squares = jnp.sum(columns[...], axis=0, keepdims=True)
    back_a = off_weight * row_squares + change * diagonal
    back_b = off_weight * column_squares + change * diagonal
    mean_a = off_weight * means[0, pl.ds(0, 1), :] + st_b[0, pl.ds(2, 1), :] * change
    mean_b = off_weight * means[1, pl.ds(0, 1), :] + st_a[0, pl.ds(2, 1), :] * change

    def out_copy(view, i):
        src, dst = ((g_a, ga_hbm), (g_b, gb_hbm))[view]
        return pltpu.make_async_copy(src.at[band_of(i)], dst.at[band_of(i)], out_sem.at[view, i])

    def finish(i, carry):
        here = band_of(i)
        n_a = normal(raw_a, st_a, 0, here)
        n_b = normal(raw_b, st_b, 0, here)
        g_a[here, :] = (off_weight * g_a[here, :] + n_b * change - mean_a - n_a * back_a) * st_a[0, pl.ds(1, 1), :]
        out_copy(0, i).start()
        g_b[here, :] = (off_weight * g_b[here, :] + n_a * change - mean_b - n_b * back_b) * st_b[0, pl.ds(1, 1), :]
        out_copy(1, i).start()
        return carry

    lax.fori_loop(0, BANDS, finish, 0)

    for view, edge in ((1, first_x), (0, last_x)):
        for c in range(PARTS):
            direct(view, c).wait_send()
            forward(view, c).wait_send()
    for view in (0, 1):
        for j in range(BANDS):
            far(view, j).wait_send()

    @pl.when(seam)
    def _():
        for r in range(PARTS // 2):
            from_relay(0, r).wait_send()

    for d in range(1, NZ):
        stat_z(d).wait_send()
    stat_y.wait_send()
    for k in (1, 2, 3):
        for view in (0, 1):
            stat_f(view, k).wait_send()
    for t in range(4):
        for s in range(HOPS):
            for copy in sum_send(t, s):
                copy.wait_send()
        y_copy(t).wait_send()
    hand1.wait_send()
    hand2.wait_send()
    hand3.wait_send()

    @pl.when(even)
    def _():
        hand6.wait_send()

    for lane in range(5):
        for s in range(HOPS):
            for copy in gather_send(lane, lane_tile[lane], s):
                copy.wait_send()
            if lane < 2:
                for i in (0, 1):
                    across(lane, lane_tile[lane], s, i).wait_send()
    for d in range(1, NZ):
        loss_z(d).wait_send()
    for r in range(4):
        loss_copy(r).wait_send()
    for view in (0, 1):
        for i in range(BANDS):
            out_copy(view, i).wait()


def local(view_a, view_b):
    rows, width = view_a.shape
    part = rows // PARTS
    band = rows // BANDS
    chunk = width // NZ
    dma = pltpu.SemaphoreType.DMA
    anywhere = pl.BlockSpec(memory_space=pl.ANY)
    grad_a, grad_b, loss = pl.pallas_call(
        kernel,
        out_shape=(
            jax.ShapeDtypeStruct((rows, width), F32),
            jax.ShapeDtypeStruct((rows, width), F32),
            jax.ShapeDtypeStruct((1, 1), F32),
        ),
        in_specs=[anywhere, anywhere],
        out_specs=(anywhere, anywhere, pl.BlockSpec(memory_space=pltpu.SMEM)),
        scratch_shapes=[
            pltpu.VMEM((4, rows, width), F32),
            pltpu.VMEM((4, rows, width), F32),
            pltpu.VMEM((BANDS + 1, width, band), BF16),
            pltpu.VMEM((BANDS + 1, width, band), BF16),
            pltpu.VMEM((band, width), BF16),
            pltpu.VMEM((band, width), BF16),
            pltpu.VMEM((4, width, width), F32),
            pltpu.VMEM((4, HOPS, chunk, width), F32),
            pltpu.VMEM((4, HOPS, chunk, width), F32),
            pltpu.VMEM((4, chunk, width), F32),
            pltpu.VMEM((chunk, width), F32),
            pltpu.VMEM((7, width, width), F32),
            pltpu.VMEM((width, width), BF16),
            pltpu.VMEM((width, width), BF16),
            pltpu.VMEM((rows, width), F32),
            pltpu.VMEM((rows, width), F32),
            pltpu.VMEM((PARTS // 2, part, width), F32),
            pltpu.VMEM((NZ, 8, width), F32),
            pltpu.VMEM((2, 8, width), F32),
            pltpu.VMEM((4, 8, width), F32),
            pltpu.VMEM((4, 8, width), F32),
            pltpu.VMEM((width, 128), F32),
            pltpu.VMEM((8, width), F32),
            pltpu.VMEM((2, 16, width), F32),
            pltpu.VMEM((NZ, 8, 128), F32),
            pltpu.VMEM((5, 8, 128), F32),
            pltpu.VMEM((4, 8, 128), F32),
            dma((2,)),
            dma((2, BANDS)),
            dma((2, PARTS)), dma((2, PARTS)),
            dma((2, PARTS)), dma((2, PARTS)),
            dma((2, BANDS)), dma((2, BANDS)),
            dma((PARTS // 2,)), dma((PARTS // 2,)),
            dma((NZ,)), dma((NZ,)),
            dma(()), dma(()),
            dma((2, 4)), dma((2, 4)),
            dma((2, 4, HOPS)), dma((2, 4, HOPS)),
            dma((4,)), dma((4,)),
            dma((4,)), dma((7,)),
            dma((2, 5, HOPS)), dma((2, 5, HOPS)),
            dma((2, 2, HOPS)), dma((2, 2, HOPS)),
            dma((NZ,)), dma((NZ,)),
            dma((4,)), dma((4,)),
        ],
        compiler_params=pltpu.CompilerParams(
            collective_id=0, has_side_effects=True, vmem_limit_bytes=60 * 1024 * 1024
        ),
        cost_estimate=pl.CostEstimate(
            flops=2 * 3 * 12 * rows * width * width, bytes_accessed=16 * rows * width, transcendentals=0
        ),
    )(view_a, view_b)
    return grad_a, grad_b, loss[0, 0]


def solution(mesh):
    spec = P("batch", "feat")
    return jax.shard_map(
        local, mesh=mesh, in_specs=(spec, spec), out_specs=(spec, spec, P()), check_vma=False
    )
```

```python
import functools

import jax
import jax.numpy as jnp
from jax import lax
from jax.experimental import pallas as pl
from jax.experimental.pallas import tpu as pltpu
from jax.sharding import PartitionSpec as P

MESH = pl.DeviceIdType.MESH
F32 = jnp.float32
BF16 = jnp.bfloat16

eps = 1e-05
off_weight = 0.25

NZ = 8
NX = 4
NY = 4
NF = 16
PARTS = 8
BANDS = 4
HOPS = 4


def mod(value, n):
    return lax.rem(value + n, n)


def split(value):
    hi = value.astype(BF16)
    return hi, (value - hi.astype(F32)).astype(BF16)


def dot3(left, right, transposed=False):
    dims = (((1,), (1 if transposed else 0,)), ((), ()))
    dot = functools.partial(lax.dot_general, dimension_numbers=dims, preferred_element_type=F32)
    return dot(left[0], right[0]) + dot(left[0], right[1]) + dot(left[1], right[0])


def kernel(
    a_hbm, b_hbm, ga_hbm, gb_hbm, loss_ref,
    raw_a, raw_b, at_hi, at_lo, b_hi, b_lo, tiles, rs_p, rs_m, y_recv, fin, cfull, c_hi, c_lo,
    g_a, g_b, relay, relay_far, st_z, st_y, st_a, st_b, squares, columns, means, l_z, l_send, l_recv,
    in_sem, out_sem, direct_s, direct_r, fwd_s, fwd_r, far_s, far_r, rel_s, rel_r, rel_far_s, rel_far_r,
    stz_s, stz_r, sty_s, sty_r, stf_s, stf_r, rs_s, rs_r, y_s, y_r, hand_s, hand_r,
    ag_s, ag_r, ay_s, ay_r, lz_s, lz_r, loss_s, loss_r,
):
    rows, width = a_hbm.shape
    part = rows // PARTS
    band = rows // BANDS
    chunk = width // NZ
    half = chunk // 2
    total = float(rows * 2 * NZ)
    features = float(width * NF)

    batch = lax.axis_index("batch")
    feat = lax.axis_index("feat")
    z = lax.div(batch, 2)
    y_lo = lax.rem(batch, 2)
    y = lax.div(feat, 2 * NX) * 2 + y_lo
    x = lax.rem(lax.div(feat, 2), NX)
    core = lax.rem(feat, 2)
    even = core == 0
    odd = core == 1
    first_x = x == 0
    last_x = x == NX - 1
    seam = jnp.logical_or(first_x, last_x)

    def at_feat(f):
        return {"batch": batch, "feat": f}

    def at_z(z_other):
        return {"batch": z_other * 2 + y_lo, "feat": feat}

    def at_xy(x_other, y_other, core_other):
        f = lax.div(y_other, 2) * (2 * NX) + x_other * 2 + core_other
        return {"batch": z * 2 + lax.rem(y_other, 2), "feat": f}

    def neighbour(steps):
        return at_feat(mod(feat + steps, NF))

    def crossed(stride):
        return at_feat(feat + stride - 2 * stride * lax.rem(lax.div(feat, stride), 2))

    other_core = crossed(1)
    other_y = {"batch": batch + 1 - 2 * y_lo, "feat": feat}
    above = at_z(mod(z + 1, NZ))
    below = at_z(mod(z - 1, NZ))
    mirror_x = NX - 1 - x
    ahead_crossed = at_feat(mod(feat + 3 - 2 * core, NF))

    def send(src, dst, s_sem, r_sem, device):
        return pltpu.make_async_remote_copy(
            src_ref=src, dst_ref=dst, send_sem=s_sem, recv_sem=r_sem,
            device_id=device, device_id_type=MESH,
        )

    def landed(dst, r_sem, s_sem):
        send(dst, dst, s_sem, r_sem, other_core).wait_recv()

    load_b = pltpu.make_async_copy(b_hbm, raw_b.at[0], in_sem.at[0])
    load_a = pltpu.make_async_copy(a_hbm, raw_a.at[0], in_sem.at[1])
    load_b.start()
    load_a.start()

    barrier = pltpu.get_barrier_semaphore()
    friends = [neighbour(k) for k in (-3, -2, -1, 1, 2, 3)]
    friends += [crossed(k) for k in (2, 4, 8)]
    friends += [at_z(mod(z + d, NZ)) for d in range(1, NZ)]
    friends += [other_y]
    for friend in friends:
        pl.semaphore_signal(barrier, inc=1, device_id=friend, device_id_type=MESH)

    @pl.when(seam)
    def _():
        for friend in (
            at_xy(mirror_x, mod(y - 1, NY), core), at_xy(mirror_x, mod(y + 1, NY), core),
            at_xy(x, mod(y - 1, NY), core), at_xy(x, mod(y + 1, NY), core),
            at_xy(x, mod(y - 1, NY), 1 - core), at_xy(x, mod(y + 1, NY), 1 - core),
        ):
            pl.semaphore_signal(barrier, inc=1, device_id=friend, device_id_type=MESH)

    pl.semaphore_wait(barrier, jnp.where(seam, len(friends) + 6, len(friends)))


    def piece(c):
        return pl.ds(pl.multiple_of(c * part, part), part)

    def direct(view, c):
        src, raw, steps = ((a_hbm, raw_a, 2), (b_hbm, raw_b, -2))[view]
        return send(
            src.at[piece(c)], raw.at[1, piece(c)], direct_s.at[view, c], direct_r.at[view, c],
            neighbour(steps),
        )

    def to_relay(view, c):
        src = (a_hbm, b_hbm)[view]
        return send(
            src.at[piece(c)], relay.at[c - PARTS // 2], direct_s.at[view, c],
            rel_r.at[c - PARTS // 2], at_xy(mirror_x, mod(y - 1, NY), core),
        )

    def from_relay(view, r):
        raw = (raw_a, raw_b)[view]
        c = r + PARTS // 2
        return send(
            relay.at[r], raw.at[1, piece(c)], rel_s.at[r], direct_r.at[view, c],
            at_xy(x, mod(y - 1, NY), core),
        )

    for c in (0, 4, 1, 5, 2, 6, 3, 7):
        for view, edge in ((1, first_x), (0, last_x)):
            if c < PARTS // 2:
                direct(view, c).start()
            else:
                @pl.when(edge)
                def _():
                    to_relay(view, c).start()

                @pl.when(jnp.logical_not(edge))
                def _():
                    direct(view, c).start()

    raws = (raw_a, raw_b)
    late = ((0, odd, last_x, first_x), (1, even, first_x, last_x))

    def far(view, src, here):
        raw = raws[view]
        return send(
            src.at[here], raw.at[3, here], far_s.at[view], far_r.at[view], neighbour(1 - 2 * view)
        )

    def left_here(src, s_sem):
        send(src, src, s_sem, sty_r, other_core).wait_send()

    def far_take(view):
        landed(raws[view].at[3], far_r.at[view], far_s.at[view])

    def late_start(view, side, leaves, j):
        raw = raws[view]
        if j < PARTS // 2:
            @pl.when(side)
            def _():
                far(view, raw.at[1], piece(j)).start()
        else:
            @pl.when(jnp.logical_and(side, leaves))
            def _():
                send(
                    raw.at[1, piece(j)], relay_far.at[j - PARTS // 2], far_s.at[view],
                    rel_far_r.at[j - PARTS // 2], at_xy(mirror_x, mod(y - 1, NY), core),
                ).start()

            @pl.when(jnp.logical_and(side, jnp.logical_not(leaves)))
            def _():
                far(view, raw.at[1], piece(j)).start()

    def late_out(view, r):
        return send(
            relay_far.at[r], raws[view].at[3, piece(r + PARTS // 2)], rel_far_s.at[r], far_r.at[view],
            at_xy(x, mod(y - 1, NY), 1 - core),
        )

    def late_pass(r):
        for view, side, leaves, enters in late:
            @pl.when(jnp.logical_and(side, enters))
            def _():
                landed(relay_far.at[r], rel_far_r.at[r], rel_far_s.at[r])
                late_out(view, r).start()

    @pl.when(odd)
    def _():
        far(1, b_hbm, pl.ds(0, rows)).start()

    @pl.when(even)
    def _():
        far(0, a_hbm, pl.ds(0, rows)).start()

    load_b.wait()
    load_a.wait()
    strip = 128
    for view, raw in ((0, raw_a), (1, raw_b)):
        def add_up(i, acc):
            v = raw[0, pl.ds(pl.multiple_of(i * strip, strip), strip), :]
            return acc + jnp.sum(v.reshape(strip // 8, 8, width), axis=0)

        zeros = jnp.zeros((8, width), F32)
        acc = lax.fori_loop(0, rows // strip, add_up, zeros)
        mean = jnp.sum(acc, axis=0, keepdims=True) * (1.0 / rows)

        def add_up_squares(i, carry):
            rest, square = carry
            v = raw[0, pl.ds(pl.multiple_of(i * strip, strip), strip), :] - mean
            v = v.reshape(strip // 8, 8, width)
            return rest + jnp.sum(v, axis=0), square + jnp.sum(v * v, axis=0)

        rest, square = lax.fori_loop(0, rows // strip, add_up_squares, (zeros, zeros))
        st_z[z, pl.ds(3 * view, 1), :] = mean
        st_z[z, pl.ds(3 * view + 1, 1), :] = jnp.sum(square, axis=0, keepdims=True)
        st_z[z, pl.ds(3 * view + 2, 1), :] = jnp.sum(rest, axis=0, keepdims=True)

    def stat_z(d):
        return send(
            st_z.at[z], st_z.at[z], stz_s.at[d], stz_r.at[d], at_z(mod(z + d, NZ))
        )

    for d in range(1, NZ):
        stat_z(d).start()
    for d in range(1, NZ):
        landed(st_z.at[mod(z - d, NZ)], stz_r.at[d], stz_s.at[d])
    for view in (0, 1):
        means_z = [st_z[i, pl.ds(3 * view, 1), :] for i in range(NZ)]
        mean = sum(means_z[1:], means_z[0]) * (1.0 / NZ)
        square = jnp.zeros((1, width), F32)
        rest = jnp.zeros((1, width), F32)
        for i in range(NZ):
            off = means_z[i] - mean
            square = square + (st_z[i, pl.ds(3 * view + 1, 1), :] + float(rows) * off * off)
            rest = rest + (st_z[i, pl.ds(3 * view + 2, 1), :] + float(rows) * off)
        st_y[0, pl.ds(3 * view, 1), :] = mean
        st_y[0, pl.ds(3 * view + 1, 1), :] = square
        st_y[0, pl.ds(3 * view + 2, 1), :] = rest
    stat_y = send(st_y.at[0], st_y.at[1], sty_s, sty_r, other_y)
    stat_y.start()
    stat_y.wait_recv()
    rows_z = float(rows * NZ)
    for view, st in ((0, st_a), (1, st_b)):
        mean0, mean1 = (st_y[i, pl.ds(3 * view, 1), :] for i in (0, 1))
        mean = 0.5 * (mean0 + mean1)
        off0, off1 = mean0 - mean, mean1 - mean
        square = (
            st_y[0, pl.ds(3 * view + 1, 1), :] + st_y[1, pl.ds(3 * view + 1, 1), :]
            + rows_z * (off0 * off0 + off1 * off1)
        )
        rest = (
            st_y[0, pl.ds(3 * view + 2, 1), :] + st_y[1, pl.ds(3 * view + 2, 1), :]
            + rows_z * (off0 + off1)
        )
        inverse = 1.0 / jnp.sqrt(square * (1.0 / total) + eps)
        st[0, pl.ds(0, 1), :] = mean
        st[0, pl.ds(1, 1), :] = inverse
        st[0, pl.ds(2, 1), :] = rest * (1.0 / total) * inverse

    def stat_f(view, k):
        st = (st_a, st_b)[view]
        if k == 2:
            slot = 1
        elif (k == 1) == (view == 1):
            slot = 2 + core
        else:
            slot = 3 - core
        return send(
            st.at[0], st.at[slot], stf_s.at[view, k], stf_r.at[view, slot],
            neighbour(-k if view == 1 else k),
        )

    for k in (2, 1, 3):
        for view in (1, 0):
            stat_f(view, k).start()

    def normal(raw, st, slot, rows_here):
        return (raw[slot, rows_here, :] - st[slot, pl.ds(0, 1), :]) * st[slot, pl.ds(1, 1), :]

    def add_tile(t, c, left_hi, left_lo, first):
        right = (b_hi[...], b_lo[...])
        def rows_of(i, carry):
            here = pl.ds(pl.multiple_of(i * (width // 2), width // 2), width // 2)
            out = dot3((left_hi[c, here, :], left_lo[c, here, :]), right)
            if first:
                tiles[t, here, :] = out
            else:
                tiles[t, here, :] = tiles[t, here, :] + out
            return carry
        lax.fori_loop(0, 2, rows_of, 0)

    def band_of(c):
        return pl.ds(pl.multiple_of(c * band, band), band)

    def turn_a(slot, c, index):
        hi, lo = split(normal(raw_a, st_a, slot, band_of(c)).T)
        at_hi[index] = hi
        at_lo[index] = lo

    def take_b(slot, c):
        hi, lo = split(normal(raw_b, st_b, slot, band_of(c)))
        b_hi[...] = hi
        b_lo[...] = lo

    def clear(t, carry):
        tiles[t] = jnp.zeros((width, width), F32)
        return carry

    lax.fori_loop(0, 4, clear, 0)

    def own_tile(c, carry):
        turn_a(0, c, c)
        take_b(0, c)
        add_tile(0, c, at_hi, at_lo, False)
        return carry

    lax.fori_loop(0, BANDS, own_tile, 0)

    def dest(q):
        return pl.multiple_of(mod(q, NZ) * chunk, chunk)

    def sum_send(t, s):
        if s == 0:
            up = pl.ds(dest(z + HOPS), half)
            down = pl.ds(pl.multiple_of(dest(z + HOPS) + half, half), half)
            up_to, down_to = pl.ds(0, half), pl.ds(half, half)
        else:
            up, down = pl.ds(dest(z + HOPS - s), chunk), pl.ds(dest(z - HOPS + s), chunk)
            up_to = down_to = pl.ds(0, chunk)
        return (
            send(tiles.at[t, up], rs_p.at[t, s, up_to], rs_s.at[0, t, s], rs_r.at[0, t, s], above),
            send(tiles.at[t, down], rs_m.at[t, s, down_to], rs_s.at[1, t, s], rs_r.at[1, t, s], below),
        )

    def sum_start(t, s):
        for copy in sum_send(t, s):
            copy.start()

    def sum_take(t, s):
        for copy in sum_send(t, s):
            copy.wait_recv()
        for recv, q, low in ((rs_p, z + HOPS - 1 - s, 0), (rs_m, z - HOPS + 1 + s, half)):
            if s == 0:
                here = pl.ds(pl.multiple_of(dest(q) + low, half), half)
                tiles[t, here, :] = tiles[t, here, :] + recv[t, s, pl.ds(low, half), :]
            else:
                here = pl.ds(dest(q), chunk)
                tiles[t, here, :] = tiles[t, here, :] + recv[t, s]

    mine = pl.ds(dest(z), chunk)

    def y_copy(t):
        return send(tiles.at[t, mine], y_recv.at[t], y_s.at[t], y_r.at[t], other_y)

    def sum_end(t):
        sum_take(t, HOPS - 1)
        y_copy(t).start()

    def sum_all(t):
        y_copy(t).wait_recv()
        return (tiles[t, mine, :] + y_recv[t]) * (1.0 / total)

    def gather_part(s, mover):
        up, down = z - s - mover, z + s + mover
        if s < HOPS - 1:
            return pl.ds(dest(up), chunk), pl.ds(dest(down), chunk)
        return pl.ds(dest(up), half), pl.ds(pl.multiple_of(dest(down) + half, half), half)

    def gather_send(lane, u, s):
        up, down = gather_part(s, 0)
        return (
            send(cfull.at[u, up], cfull.at[u, up], ag_s.at[0, lane, s], ag_r.at[0, lane, s], above),
            send(cfull.at[u, down], cfull.at[u, down], ag_s.at[1, lane, s], ag_r.at[1, lane, s], below),
        )

    def gather_start(lane, u, s):
        for copy in gather_send(lane, u, s):
            copy.start()

    def across(lane, u, s, i):
        p = gather_part(s, 1)[i]
        return send(cfull.at[u, p], cfull.at[u, p], ay_s.at[i, lane, s], ay_r.at[i, lane, s], other_y)

    def gather_take(lane, u, s):
        for i, p in enumerate(gather_part(s, 1)):
            landed(cfull.at[u, p], ag_r.at[i, lane, s], ag_s.at[i, lane, s])
            if lane < 2:
                across(lane, u, s, i).start()
        if s < HOPS - 1:
            gather_start(lane, u, s + 1)

    def gather_other(lane, u):
        for s in range(HOPS):
            for i in (0, 1):
                across(lane, u, s, i).wait_recv()

    lane_tile = (1 + y_lo, 4 + y_lo, 0, 3 + 3 * core, 6 - 3 * core)
    other_tile = (2 - y_lo, 5 - y_lo)

    def gather(lane, s):
        if s < 0:
            gather_start(lane, lane_tile[lane], 0)
        else:
            gather_take(lane, lane_tile[lane], s)

    hand1 = send(cfull.at[1, mine], cfull.at[4, mine], hand_s.at[0], hand_r.at[4], neighbour(2))
    hand2 = send(cfull.at[2, mine], cfull.at[5, mine], hand_s.at[1], hand_r.at[5], ahead_crossed)
    hand3 = send(fin, cfull.at[3, mine], hand_s.at[2], hand_r.at[3], neighbour(-1))
    hand6 = send(fin, cfull.at[6, mine], hand_s.at[3], hand_r.at[6], neighbour(2))

    def hand_take(u):
        landed(cfull.at[u, mine], hand_r.at[u], hand_s.at[0])

    def when(cond, f, *args):
        @pl.when(cond)
        def _():
            f(*args)

    def sum_step(t, s):
        if s < HOPS - 1:
            sum_take(t, s)
            sum_start(t, s + 1)
        else:
            sum_end(t)

    def end_0():
        cfull[0, mine, :] = sum_all(0)

    def end_1():
        cfull[1, mine, :] = sum_all(1)
        hand1.start()

    def end_2():
        cfull[2, mine, :] = sum_all(2)
        hand2.start()

    def end_3_odd():
        last = sum_all(3)
        fin[...] = last
        hand3.start()
        cfull[6, mine, :] = last

    def end_3_even():
        fin[...] = sum_all(3)
        hand3.start()
        hand6.start()

    def forward(view, c):
        raw = (raw_a, raw_b)[view]
        return send(
            raw.at[1, piece(c)], raw.at[2, piece(c)], fwd_s.at[view, c], fwd_r.at[view, c],
            other_core,
        )

    sum_start(0, 0)
    for slot in (3, 1, 2):
        for view, st in ((1, st_b), (0, st_a)):
            landed(st.at[slot], stf_r.at[view, slot], stf_s.at[view, slot])

    @pl.when(odd)
    def _():
        far_take(0)

        def fourth_tile(c, carry):
            turn_a(3, c, BANDS)
            take_b(0, c)
            add_tile(3, BANDS, at_hi, at_lo, False)
            return carry

        lax.fori_loop(0, BANDS, fourth_tile, 0)
        sum_start(3, 0)

    def early(j):
        if j < HOPS:
            sum_step(0, j)
            when(odd, sum_step, 3, j)
        elif j == 4:
            end_0()
            gather(2, -1)
            when(odd, end_3_odd)
        elif j == 5:
            gather(2, 0)
            when(even, hand_take, 3)
            gather(3, -1)
        else:
            gather(2, j - 5)
            gather(3, j - 6)

    for c in range(BANDS):
        for j in (2 * c, 2 * c + 1):
            if j < PARTS // 2:
                for view, edge in ((1, last_x), (0, first_x)):
                    @pl.when(edge)
                    def _():
                        landed(relay.at[j], rel_r.at[j], rel_s.at[j])
                        from_relay(view, j).start()

            for view in (1, 0):
                direct(view, j).wait_recv()
                forward(view, j).start()
                _, side, leaves, _ = late[view]
                late_start(view, side, leaves, j)
            early(j)
        take_b(1, c)
        add_tile(1, c, at_hi, at_lo, False)

        @pl.when(even)
        def _():
            for j in (2 * c, 2 * c + 1):
                forward(0, j).wait_recv()
            turn_a(2, c, BANDS)
            add_tile(3, BANDS, at_hi, at_lo, False)

        for j in (2 * c, 2 * c + 1):
            forward(1, j).wait_recv()
        take_b(2, c)
        add_tile(2, c, at_hi, at_lo, False)

    @pl.when(odd)
    def _():
        for j in range(PARTS):
            forward(0, j).wait_recv()

    for t in (1, 2):
        sum_start(t, 0)
    when(even, sum_start, 3, 0)

    squares[...] = jnp.zeros_like(squares)
    columns[...] = jnp.zeros_like(columns)
    means[...] = jnp.zeros_like(means)

    def clear_g(i, carry):
        g_a[band_of(i), :] = jnp.zeros((band, width), F32)
        g_b[band_of(i), :] = jnp.zeros((band, width), F32)
        return carry

    lax.fori_loop(0, BANDS, clear_g, 0)

    def grow(view, slot, u):
        g, raw, st = ((g_a, raw_b, st_b), (g_b, raw_a, st_a))[view]
        c = cfull[u]
        hi, lo = split(c)
        c_hi[...] = hi
        c_lo[...] = lo
        if view == 0:
            acc = squares[...]
            for j in range(width // 128):
                part_j = c[:, j * 128:(j + 1) * 128]
                acc = acc + part_j * part_j
            squares[...] = acc
        else:
            columns[...] = columns[...] + jnp.sum((c * c).reshape(width // 8, 8, width), axis=0)

        def body(i, carry):
            here = band_of(i)
            n = split(normal(raw, st, slot, here))
            g[here, :] = g[here, :] + dot3(n, (c_hi[...], c_lo[...]), view == 0)
            return carry

        lax.fori_loop(0, BANDS, body, 0)
        m = split(jnp.broadcast_to(st[slot, pl.ds(2, 1), :], (16, width)))
        means[view] = means[view] + dot3(m, (c_hi[...], c_lo[...]), view == 0)

    def loss_part():
        value = jnp.zeros((8, 128), F32)
        for t in range(4):
            c = fin[...] if t == 3 else cfull[t, mine, :]
            terms = off_weight * c * c
            if t == 0:
                shape = (chunk, width)
                on = lax.broadcasted_iota(jnp.int32, shape, 1) == (
                    lax.broadcasted_iota(jnp.int32, shape, 0) + z * chunk
                )
                terms = jnp.where(on, (1.0 - c) * (1.0 - c), terms)
            terms = jnp.sum(terms.reshape(chunk // 8, 8, width), axis=0)
            for j in range(width // 128):
                value = value + terms[:, j * 128:(j + 1) * 128]
        l_z[z] = value

    def loss_z(d):
        return send(l_z.at[z], l_z.at[z], lz_s.at[d], lz_r.at[d], at_z(mod(z + d, NZ)))

    def loss_copy(r):
        return send(l_send.at[r], l_recv.at[r], loss_s.at[r], loss_r.at[r], crossed(1 << r))

    def loss_start():
        for d in range(1, NZ):
            landed(l_z.at[mod(z - d, NZ)], lz_r.at[d], lz_s.at[d])
        value = l_z[0]
        for i in range(1, NZ):
            value = value + l_z[i]
        l_send[0] = value
        loss_copy(0).start()

    def loss_step(r):
        loss_copy(r).wait_recv()
        l_send[r + 1] = l_send[r] + l_recv[r]
        if r < 3:
            loss_copy(r + 1).start()

    gather(2, 3)
    gather(3, 2)
    grow(0, 0, 0)
    gather(3, 3)
    for t in (1, 2):
        sum_step(t, 0)
    when(even, sum_step, 3, 0)
    late_pass(0)
    late_pass(1)
    grow(1, 0, 0)
    for t in (1, 2):
        sum_step(t, 1)
    when(even, sum_step, 3, 1)
    late_pass(2)
    late_pass(3)

    @pl.when(even)
    def _():
        far_take(1)
        grow(0, 3, 3)

    when(odd, grow, 1, 3, 6)
    for s in (2, 3):
        for t in (1, 2):
            sum_step(t, s)
        when(even, sum_step, 3, s)
    end_1()
    end_2()
    gather(0, -1)
    when(even, end_3_even)
    loss_part()
    for d in range(1, NZ):
        loss_z(d).start()
    hand_take(4)
    hand_take(5)
    gather(1, -1)
    gather(0, 0)
    when(even, hand_take, 6)
    when(odd, hand_take, 3)
    gather(4, -1)
    gather(1, 0)
    gather(0, 1)
    gather(4, 0)
    gather(1, 1)
    gather(0, 2)
    loss_start()
    gather(4, 1)
    gather(1, 2)
    gather(0, 3)
    grow(0, 1 + y_lo, lane_tile[0])
    loss_step(0)
    gather(4, 2)
    gather(1, 3)
    grow(1, 1 + y_lo, lane_tile[1])
    loss_step(1)
    gather(4, 3)
    gather_other(0, other_tile[0])
    grow(0, 2 - y_lo, other_tile[0])
    loss_step(2)
    gather_other(1, other_tile[1])
    grow(1, 2 - y_lo, other_tile[1])
    loss_step(3)

    @pl.when(odd)
    def _():
        far_take(1)
        grow(0, 3, 3)

    @pl.when(even)
    def _():
        far_take(0)
        grow(1, 3, 6)

    loss_ref[0, 0] = jnp.sum(l_send[4]) * (1.0 / features)

    diagonal = []
    one_block = (
        lax.broadcasted_iota(jnp.int32, (128, 128), 0) == lax.broadcasted_iota(jnp.int32, (128, 128), 1)
    )
    for j in range(width // 128):
        block = cfull[0, j * 128:(j + 1) * 128, j * 128:(j + 1) * 128]
        diagonal.append(jnp.sum(jnp.where(one_block, block, 0.0), axis=0, keepdims=True))
    diagonal = jnp.concatenate(diagonal, axis=1)
    change = -(1.0 - diagonal) - off_weight * diagonal
    row_squares = jnp.sum(squares[...].T, axis=0, keepdims=True)
    column_squares = jnp.sum(columns[...], axis=0, keepdims=True)
    back_a = off_weight * row_squares + change * diagonal
    back_b = off_weight * column_squares + change * diagonal
    mean_a = off_weight * means[0, pl.ds(0, 1), :] + st_b[0, pl.ds(2, 1), :] * change
    mean_b = off_weight * means[1, pl.ds(0, 1), :] + st_a[0, pl.ds(2, 1), :] * change

    def out_copy(view, i):
        src, dst = ((g_a, ga_hbm), (g_b, gb_hbm))[view]
        return pltpu.make_async_copy(src.at[band_of(i)], dst.at[band_of(i)], out_sem.at[view, i])

    def finish(i, carry):
        here = band_of(i)
        n_a = normal(raw_a, st_a, 0, here)
        n_b = normal(raw_b, st_b, 0, here)
        g_a[here, :] = (off_weight * g_a[here, :] + n_b * change - mean_a - n_a * back_a) * st_a[0, pl.ds(1, 1), :]
        out_copy(0, i).start()
        g_b[here, :] = (off_weight * g_b[here, :] + n_a * change - mean_b - n_b * back_b) * st_b[0, pl.ds(1, 1), :]
        out_copy(1, i).start()
        return carry

    lax.fori_loop(0, BANDS, finish, 0)

    for view, edge in ((1, first_x), (0, last_x)):
        for c in range(PARTS):
            direct(view, c).wait_send()
            forward(view, c).wait_send()
    for view, side, leaves, enters in late:
        left_here(raws[view].at[3], far_s.at[view])

        @pl.when(jnp.logical_and(side, enters))
        def _():
            for r in range(PARTS // 2):
                late_out(view, r).wait_send()

    @pl.when(seam)
    def _():
        for r in range(PARTS // 2):
            from_relay(0, r).wait_send()

    for d in range(1, NZ):
        stat_z(d).wait_send()
    stat_y.wait_send()
    for k in (1, 2, 3):
        for view in (0, 1):
            stat_f(view, k).wait_send()
    for t in range(4):
        for s in range(HOPS):
            for copy in sum_send(t, s):
                copy.wait_send()
        y_copy(t).wait_send()
    hand1.wait_send()
    hand2.wait_send()
    hand3.wait_send()

    @pl.when(even)
    def _():
        hand6.wait_send()

    for lane in range(5):
        for s in range(HOPS):
            for copy in gather_send(lane, lane_tile[lane], s):
                copy.wait_send()
            if lane < 2:
                for i in (0, 1):
                    across(lane, lane_tile[lane], s, i).wait_send()
    for d in range(1, NZ):
        loss_z(d).wait_send()
    for r in range(4):
        loss_copy(r).wait_send()
    for view in (0, 1):
        for i in range(BANDS):
            out_copy(view, i).wait()


def local(view_a, view_b):
    rows, width = view_a.shape
    part = rows // PARTS
    band = rows // BANDS
    chunk = width // NZ
    dma = pltpu.SemaphoreType.DMA
    anywhere = pl.BlockSpec(memory_space=pl.ANY)
    grad_a, grad_b, loss = pl.pallas_call(
        kernel,
        out_shape=(
            jax.ShapeDtypeStruct((rows, width), F32),
            jax.ShapeDtypeStruct((rows, width), F32),
            jax.ShapeDtypeStruct((1, 1), F32),
        ),
        in_specs=[anywhere, anywhere],
        out_specs=(anywhere, anywhere, pl.BlockSpec(memory_space=pltpu.SMEM)),
        scratch_shapes=[
            pltpu.VMEM((4, rows, width), F32),
            pltpu.VMEM((4, rows, width), F32),
            pltpu.VMEM((BANDS + 1, width, band), BF16),
            pltpu.VMEM((BANDS + 1, width, band), BF16),
            pltpu.VMEM((band, width), BF16),
            pltpu.VMEM((band, width), BF16),
            pltpu.VMEM((4, width, width), F32),
            pltpu.VMEM((4, HOPS, chunk, width), F32),
            pltpu.VMEM((4, HOPS, chunk, width), F32),
            pltpu.VMEM((4, chunk, width), F32),
            pltpu.VMEM((chunk, width), F32),
            pltpu.VMEM((7, width, width), F32),
            pltpu.VMEM((width, width), BF16),
            pltpu.VMEM((width, width), BF16),
            pltpu.VMEM((rows, width), F32),
            pltpu.VMEM((rows, width), F32),
            pltpu.VMEM((PARTS // 2, part, width), F32),
            pltpu.VMEM((PARTS // 2, part, width), F32),
            pltpu.VMEM((NZ, 8, width), F32),
            pltpu.VMEM((2, 8, width), F32),
            pltpu.VMEM((4, 8, width), F32),
            pltpu.VMEM((4, 8, width), F32),
            pltpu.VMEM((width, 128), F32),
            pltpu.VMEM((8, width), F32),
            pltpu.VMEM((2, 16, width), F32),
            pltpu.VMEM((NZ, 8, 128), F32),
            pltpu.VMEM((5, 8, 128), F32),
            pltpu.VMEM((4, 8, 128), F32),
            dma((2,)),
            dma((2, BANDS)),
            dma((2, PARTS)), dma((2, PARTS)),
            dma((2, PARTS)), dma((2, PARTS)),
            dma((2,)), dma((2,)),
            dma((PARTS // 2,)), dma((PARTS // 2,)),
            dma((PARTS // 2,)), dma((PARTS // 2,)),
            dma((NZ,)), dma((NZ,)),
            dma(()), dma(()),
            dma((2, 4)), dma((2, 4)),
            dma((2, 4, HOPS)), dma((2, 4, HOPS)),
            dma((4,)), dma((4,)),
            dma((4,)), dma((7,)),
            dma((2, 5, HOPS)), dma((2, 5, HOPS)),
            dma((2, 2, HOPS)), dma((2, 2, HOPS)),
            dma((NZ,)), dma((NZ,)),
            dma((4,)), dma((4,)),
        ],
        compiler_params=pltpu.CompilerParams(
            collective_id=0, has_side_effects=True, vmem_limit_bytes=60 * 1024 * 1024
        ),
        cost_estimate=pl.CostEstimate(
            flops=2 * 3 * 12 * rows * width * width, bytes_accessed=16 * rows * width, transcendentals=0
        ),
    )(view_a, view_b)
    return grad_a, grad_b, loss[0, 0]


def solution(mesh):
    spec = P("batch", "feat")
    return jax.shard_map(
        local, mesh=mesh, in_specs=(spec, spec), out_specs=(spec, spec, P()), check_vma=False
    )
```

```python
import functools

import jax
import jax.numpy as jnp
from jax import lax
from jax.experimental import pallas as pl
from jax.experimental.pallas import tpu as pltpu
from jax.sharding import PartitionSpec as P

MESH = pl.DeviceIdType.MESH
F32 = jnp.float32
BF16 = jnp.bfloat16

eps = 1e-05
off_weight = 0.25

NZ = 8
NX = 4
NY = 4
NF = 16
PARTS = 8
AHEAD = 3
BANDS = 4
HOPS = 4


def mod(value, n):
    return lax.rem(value + n, n)


def split(value):
    hi = value.astype(BF16)
    return hi, (value - hi.astype(F32)).astype(BF16)


def dot3(left, right, transposed=False):
    dims = (((1,), (1 if transposed else 0,)), ((), ()))
    dot = functools.partial(lax.dot_general, dimension_numbers=dims, preferred_element_type=F32)
    return dot(left[0], right[0]) + dot(left[0], right[1]) + dot(left[1], right[0])


def kernel(
    a_hbm, b_hbm, ga_hbm, gb_hbm, loss_ref,
    raw_a, raw_b, at_hi, at_lo, b_hi, b_lo, tiles, rs_p, rs_m, y_recv, fin, cfull, c_hi, c_lo,
    g_a, g_b, relay, st_z, st_y, st_a, st_b, squares, columns, means, l_z, l_send, l_recv,
    in_sem, out_sem, direct_s, direct_r, fwd_s, fwd_r, far_s, far_r, rel_s, rel_r,
    stz_s, stz_r, sty_s, sty_r, stf_s, stf_r, rs_s, rs_r, y_s, y_r, hand_s, hand_r,
    ag_s, ag_r, ay_s, ay_r, lz_s, lz_r, loss_s, loss_r,
):
    rows, width = a_hbm.shape
    part = rows // PARTS
    band = rows // BANDS
    chunk = width // NZ
    half = chunk // 2
    total = float(rows * 2 * NZ)
    features = float(width * NF)

    batch = lax.axis_index("batch")
    feat = lax.axis_index("feat")
    z = lax.div(batch, 2)
    y_lo = lax.rem(batch, 2)
    y = lax.div(feat, 2 * NX) * 2 + y_lo
    x = lax.rem(lax.div(feat, 2), NX)
    core = lax.rem(feat, 2)
    even = core == 0
    odd = core == 1
    first_x = x == 0
    last_x = x == NX - 1
    seam = jnp.logical_or(first_x, last_x)

    def at_feat(f):
        return {"batch": batch, "feat": f}

    def at_z(z_other):
        return {"batch": z_other * 2 + y_lo, "feat": feat}

    def at_xy(x_other, y_other):
        f = lax.div(y_other, 2) * (2 * NX) + x_other * 2 + core
        return {"batch": z * 2 + lax.rem(y_other, 2), "feat": f}

    def neighbour(steps):
        return at_feat(mod(feat + steps, NF))

    def crossed(stride):
        return at_feat(feat + stride - 2 * stride * lax.rem(lax.div(feat, stride), 2))

    other_core = crossed(1)
    other_y = {"batch": batch + 1 - 2 * y_lo, "feat": feat}
    above = at_z(mod(z + 1, NZ))
    below = at_z(mod(z - 1, NZ))
    mirror_x = NX - 1 - x
    ahead_crossed = at_feat(mod(feat + 3 - 2 * core, NF))

    def send(src, dst, s_sem, r_sem, device):
        return pltpu.make_async_remote_copy(
            src_ref=src, dst_ref=dst, send_sem=s_sem, recv_sem=r_sem,
            device_id=device, device_id_type=MESH,
        )

    def landed(dst, r_sem, s_sem):
        send(dst, dst, s_sem, r_sem, other_core).wait_recv()

    load_b = pltpu.make_async_copy(b_hbm, raw_b.at[0], in_sem.at[0])
    load_a = pltpu.make_async_copy(a_hbm, raw_a.at[0], in_sem.at[1])
    load_b.start()
    load_a.start()

    barrier = pltpu.get_barrier_semaphore()
    friends = [neighbour(k) for k in (-3, -2, -1, 1, 2, 3)]
    friends += [crossed(k) for k in (2, 4, 8)]
    friends += [at_z(mod(z + d, NZ)) for d in range(1, NZ)]
    friends += [other_y]
    for friend in friends:
        pl.semaphore_signal(barrier, inc=1, device_id=friend, device_id_type=MESH)

    @pl.when(seam)
    def _():
        for friend in (
            at_xy(mirror_x, mod(y - 1, NY)), at_xy(mirror_x, mod(y + 1, NY)),
            at_xy(x, mod(y - 1, NY)), at_xy(x, mod(y + 1, NY)),
        ):
            pl.semaphore_signal(barrier, inc=1, device_id=friend, device_id_type=MESH)

    pl.semaphore_wait(barrier, jnp.where(seam, len(friends) + 4, len(friends)))


    def piece(c):
        return pl.ds(pl.multiple_of(c * part, part), part)

    def direct(view, c):
        src, raw, steps = ((a_hbm, raw_a, 2), (b_hbm, raw_b, -2))[view]
        return send(
            src.at[piece(c)], raw.at[1, piece(c)], direct_s.at[view, c], direct_r.at[view, c],
            neighbour(steps),
        )

    def to_relay(view, c):
        src = (a_hbm, b_hbm)[view]
        return send(
            src.at[piece(c)], relay.at[c - PARTS // 2], direct_s.at[view, c],
            rel_r.at[c - PARTS // 2], at_xy(mirror_x, mod(y - 1, NY)),
        )

    def from_relay(view, r):
        raw = (raw_a, raw_b)[view]
        c = r + PARTS // 2
        return send(
            relay.at[r], raw.at[1, piece(c)], rel_s.at[r], direct_r.at[view, c],
            at_xy(x, mod(y - 1, NY)),
        )

    def piece_start(c):
        for view, edge in ((1, first_x), (0, last_x)):
            if c < PARTS // 2:
                direct(view, c).start()
            else:
                @pl.when(edge)
                def _():
                    to_relay(view, c).start()

                @pl.when(jnp.logical_not(edge))
                def _():
                    direct(view, c).start()

    for c in range(AHEAD):
        piece_start(c)

    def far_b(src):
        return send(src, raw_b.at[3], far_s.at[1], far_r.at[1], neighbour(-1))

    def far_a(src):
        return send(src, raw_a.at[3], far_s.at[0], far_r.at[0], neighbour(1))

    @pl.when(odd)
    def _():
        far_b(b_hbm).start()

    @pl.when(even)
    def _():
        far_a(a_hbm).start()

    load_b.wait()
    load_a.wait()
    strip = 128
    for view, raw in ((0, raw_a), (1, raw_b)):
        def add_up(i, acc):
            v = raw[0, pl.ds(pl.multiple_of(i * strip, strip), strip), :]
            return acc + jnp.sum(v.reshape(strip // 8, 8, width), axis=0)

        zeros = jnp.zeros((8, width), F32)
        acc = lax.fori_loop(0, rows // strip, add_up, zeros)
        mean = jnp.sum(acc, axis=0, keepdims=True) * (1.0 / rows)

        def add_up_squares(i, carry):
            rest, square = carry
            v = raw[0, pl.ds(pl.multiple_of(i * strip, strip), strip), :] - mean
            v = v.reshape(strip // 8, 8, width)
            return rest + jnp.sum(v, axis=0), square + jnp.sum(v * v, axis=0)

        rest, square = lax.fori_loop(0, rows // strip, add_up_squares, (zeros, zeros))
        st_z[z, pl.ds(3 * view, 1), :] = mean
        st_z[z, pl.ds(3 * view + 1, 1), :] = jnp.sum(square, axis=0, keepdims=True)
        st_z[z, pl.ds(3 * view + 2, 1), :] = jnp.sum(rest, axis=0, keepdims=True)

    def stat_z(d):
        return send(
            st_z.at[z], st_z.at[z], stz_s.at[d], stz_r.at[d], at_z(mod(z + d, NZ))
        )

    for d in range(1, NZ):
        stat_z(d).start()
    for d in range(1, NZ):
        landed(st_z.at[mod(z - d, NZ)], stz_r.at[d], stz_s.at[d])
    for view in (0, 1):
        means_z = [st_z[i, pl.ds(3 * view, 1), :] for i in range(NZ)]
        mean = sum(means_z[1:], means_z[0]) * (1.0 / NZ)
        square = jnp.zeros((1, width), F32)
        rest = jnp.zeros((1, width), F32)
        for i in range(NZ):
            off = means_z[i] - mean
            square = square + (st_z[i, pl.ds(3 * view + 1, 1), :] + float(rows) * off * off)
            rest = rest + (st_z[i, pl.ds(3 * view + 2, 1), :] + float(rows) * off)
        st_y[0, pl.ds(3 * view, 1), :] = mean
        st_y[0, pl.ds(3 * view + 1, 1), :] = square
        st_y[0, pl.ds(3 * view + 2, 1), :] = rest
    stat_y = send(st_y.at[0], st_y.at[1], sty_s, sty_r, other_y)
    stat_y.start()
    stat_y.wait_recv()
    rows_z = float(rows * NZ)
    for view, st in ((0, st_a), (1, st_b)):
        mean0, mean1 = (st_y[i, pl.ds(3 * view, 1), :] for i in (0, 1))
        mean = 0.5 * (mean0 + mean1)
        off0, off1 = mean0 - mean, mean1 - mean
        square = (
            st_y[0, pl.ds(3 * view + 1, 1), :] + st_y[1, pl.ds(3 * view + 1, 1), :]
            + rows_z * (off0 * off0 + off1 * off1)
        )
        rest = (
            st_y[0, pl.ds(3 * view + 2, 1), :] + st_y[1, pl.ds(3 * view + 2, 1), :]
            + rows_z * (off0 + off1)
        )
        inverse = 1.0 / jnp.sqrt(square * (1.0 / total) + eps)
        st[0, pl.ds(0, 1), :] = mean
        st[0, pl.ds(1, 1), :] = inverse
        st[0, pl.ds(2, 1), :] = rest * (1.0 / total) * inverse

    def stat_f(view, k):
        st = (st_a, st_b)[view]
        if k == 2:
            slot = 1
        elif (k == 1) == (view == 1):
            slot = 2 + core
        else:
            slot = 3 - core
        return send(
            st.at[0], st.at[slot], stf_s.at[view, k], stf_r.at[view, slot],
            neighbour(-k if view == 1 else k),
        )

    for k in (2, 1, 3):
        for view in (1, 0):
            stat_f(view, k).start()

    def normal(raw, st, slot, rows_here):
        return (raw[slot, rows_here, :] - st[slot, pl.ds(0, 1), :]) * st[slot, pl.ds(1, 1), :]

    def add_tile(t, c, left_hi, left_lo, first):
        right = (b_hi[...], b_lo[...])
        def rows_of(i, carry):
            here = pl.ds(pl.multiple_of(i * (width // 2), width // 2), width // 2)
            out = dot3((left_hi[c, here, :], left_lo[c, here, :]), right)
            if first:
                tiles[t, here, :] = out
            else:
                tiles[t, here, :] = tiles[t, here, :] + out
            return carry
        lax.fori_loop(0, 2, rows_of, 0)

    def band_of(c):
        return pl.ds(pl.multiple_of(c * band, band), band)

    def turn_a(slot, c, index):
        hi, lo = split(normal(raw_a, st_a, slot, band_of(c)).T)
        at_hi[index] = hi
        at_lo[index] = lo

    def take_b(slot, c):
        hi, lo = split(normal(raw_b, st_b, slot, band_of(c)))
        b_hi[...] = hi
        b_lo[...] = lo

    def clear(t, carry):
        tiles[t] = jnp.zeros((width, width), F32)
        return carry

    lax.fori_loop(0, 4, clear, 0)

    def own_tile(c, carry):
        turn_a(0, c, c)
        take_b(0, c)
        add_tile(0, c, at_hi, at_lo, False)
        return carry

    lax.fori_loop(0, BANDS, own_tile, 0)

    def dest(q):
        return pl.multiple_of(mod(q, NZ) * chunk, chunk)

    def sum_send(t, s):
        if s == 0:
            up = pl.ds(dest(z + HOPS), half)
            down = pl.ds(pl.multiple_of(dest(z + HOPS) + half, half), half)
            up_to, down_to = pl.ds(0, half), pl.ds(half, half)
        else:
            up, down = pl.ds(dest(z + HOPS - s), chunk), pl.ds(dest(z - HOPS + s), chunk)
            up_to = down_to = pl.ds(0, chunk)
        return (
            send(tiles.at[t, up], rs_p.at[t, s, up_to], rs_s.at[0, t, s], rs_r.at[0, t, s], above),
            send(tiles.at[t, down], rs_m.at[t, s, down_to], rs_s.at[1, t, s], rs_r.at[1, t, s], below),
        )

    def sum_start(t, s):
        for copy in sum_send(t, s):
            copy.start()

    def sum_take(t, s):
        for copy in sum_send(t, s):
            copy.wait_recv()
        for recv, q, low in ((rs_p, z + HOPS - 1 - s, 0), (rs_m, z - HOPS + 1 + s, half)):
            if s == 0:
                here = pl.ds(pl.multiple_of(dest(q) + low, half), half)
                tiles[t, here, :] = tiles[t, here, :] + recv[t, s, pl.ds(low, half), :]
            else:
                here = pl.ds(dest(q), chunk)
                tiles[t, here, :] = tiles[t, here, :] + recv[t, s]

    mine = pl.ds(dest(z), chunk)

    def y_copy(t):
        return send(tiles.at[t, mine], y_recv.at[t], y_s.at[t], y_r.at[t], other_y)

    def sum_end(t):
        sum_take(t, HOPS - 1)
        y_copy(t).start()

    def sum_all(t):
        y_copy(t).wait_recv()
        return (tiles[t, mine, :] + y_recv[t]) * (1.0 / total)

    def gather_part(s, mover):
        up, down = z - s - mover, z + s + mover
        if s < HOPS - 1:
            return pl.ds(dest(up), chunk), pl.ds(dest(down), chunk)
        return pl.ds(dest(up), half), pl.ds(pl.multiple_of(dest(down) + half, half), half)

    def gather_send(lane, u, s):
        up, down = gather_part(s, 0)
        return (
            send(cfull.at[u, up], cfull.at[u, up], ag_s.at[0, lane, s], ag_r.at[0, lane, s], above),
            send(cfull.at[u, down], cfull.at[u, down], ag_s.at[1, lane, s], ag_r.at[1, lane, s], below),
        )

    def gather_start(lane, u, s):
        for copy in gather_send(lane, u, s):
            copy.start()

    def across(lane, u, s, i):
        p = gather_part(s, 1)[i]
        return send(cfull.at[u, p], cfull.at[u, p], ay_s.at[i, lane, s], ay_r.at[i, lane, s], other_y)

    def gather_take(lane, u, s):
        for i, p in enumerate(gather_part(s, 1)):
            landed(cfull.at[u, p], ag_r.at[i, lane, s], ag_s.at[i, lane, s])
            if lane < 2:
                across(lane, u, s, i).start()
        if s < HOPS - 1:
            gather_start(lane, u, s + 1)

    def gather_other(lane, u):
        for s in range(HOPS):
            for i in (0, 1):
                across(lane, u, s, i).wait_recv()

    lane_tile = (1 + y_lo, 4 + y_lo, 0, 3 + 3 * core, 6 - 3 * core)
    other_tile = (2 - y_lo, 5 - y_lo)

    def gather(lane, s):
        if s < 0:
            gather_start(lane, lane_tile[lane], 0)
        else:
            gather_take(lane, lane_tile[lane], s)

    hand1 = send(cfull.at[1, mine], cfull.at[4, mine], hand_s.at[0], hand_r.at[4], neighbour(2))
    hand2 = send(cfull.at[2, mine], cfull.at[5, mine], hand_s.at[1], hand_r.at[5], ahead_crossed)
    hand3 = send(fin, cfull.at[3, mine], hand_s.at[2], hand_r.at[3], neighbour(-1))
    hand6 = send(fin, cfull.at[6, mine], hand_s.at[3], hand_r.at[6], neighbour(2))

    def hand_take(u):
        landed(cfull.at[u, mine], hand_r.at[u], hand_s.at[0])

    def when(cond, f, *args):
        @pl.when(cond)
        def _():
            f(*args)

    def sum_step(t, s):
        if s < HOPS - 1:
            sum_take(t, s)
            sum_start(t, s + 1)
        else:
            sum_end(t)

    def end_0():
        cfull[0, mine, :] = sum_all(0)

    def end_1():
        cfull[1, mine, :] = sum_all(1)
        hand1.start()

    def end_2():
        cfull[2, mine, :] = sum_all(2)
        hand2.start()

    def end_3_odd():
        last = sum_all(3)
        fin[...] = last
        hand3.start()
        cfull[6, mine, :] = last

    def end_3_even():
        fin[...] = sum_all(3)
        hand3.start()
        hand6.start()

    def forward(view, c):
        raw = (raw_a, raw_b)[view]
        return send(
            raw.at[1, piece(c)], raw.at[2, piece(c)], fwd_s.at[view, c], fwd_r.at[view, c],
            other_core,
        )

    sum_start(0, 0)
    for slot in (3, 1, 2):
        for view, st in ((1, st_b), (0, st_a)):
            landed(st.at[slot], stf_r.at[view, slot], stf_s.at[view, slot])

    @pl.when(odd)
    def _():
        far_a(a_hbm).wait_recv()

        def fourth_tile(c, carry):
            turn_a(3, c, BANDS)
            take_b(0, c)
            add_tile(3, BANDS, at_hi, at_lo, False)
            return carry

        lax.fori_loop(0, BANDS, fourth_tile, 0)
        sum_start(3, 0)

    def early(j):
        if j < HOPS:
            sum_step(0, j)
            when(odd, sum_step, 3, j)
        elif j == 4:
            end_0()
            gather(2, -1)
            when(odd, end_3_odd)
        elif j == 5:
            gather(2, 0)
            when(even, hand_take, 3)
            gather(3, -1)
        else:
            gather(2, j - 5)
            gather(3, j - 6)

    for c in range(BANDS):
        for j in (2 * c, 2 * c + 1):
            r = j - AHEAD
            if 0 <= r < PARTS // 2:
                for view, edge in ((1, last_x), (0, first_x)):
                    @pl.when(edge)
                    def _():
                        landed(relay.at[r], rel_r.at[r], rel_s.at[r])
                        from_relay(view, r).start()

            for view in (1, 0):
                direct(view, j).wait_recv()
                forward(view, j).start()
            if j + AHEAD < PARTS:
                piece_start(j + AHEAD)
            early(j)
        take_b(1, c)
        add_tile(1, c, at_hi, at_lo, False)

        @pl.when(even)
        def _():
            for j in (2 * c, 2 * c + 1):
                forward(0, j).wait_recv()
            turn_a(2, c, BANDS)
            add_tile(3, BANDS, at_hi, at_lo, False)

        for j in (2 * c, 2 * c + 1):
            forward(1, j).wait_recv()
        take_b(2, c)
        add_tile(2, c, at_hi, at_lo, False)

    @pl.when(odd)
    def _():
        for j in range(PARTS):
            forward(0, j).wait_recv()

    for t in (1, 2):
        sum_start(t, 0)
    when(even, sum_start, 3, 0)
    when(even, far_b(raw_b.at[1]).start)
    when(odd, far_a(raw_a.at[1]).start)

    squares[...] = jnp.zeros_like(squares)
    columns[...] = jnp.zeros_like(columns)
    means[...] = jnp.zeros_like(means)

    def clear_g(i, carry):
        g_a[band_of(i), :] = jnp.zeros((band, width), F32)
        g_b[band_of(i), :] = jnp.zeros((band, width), F32)
        return carry

    lax.fori_loop(0, BANDS, clear_g, 0)

    def grow(view, slot, u):
        g, raw, st = ((g_a, raw_b, st_b), (g_b, raw_a, st_a))[view]
        c = cfull[u]
        hi, lo = split(c)
        c_hi[...] = hi
        c_lo[...] = lo
        if view == 0:
            acc = squares[...]
            for j in range(width // 128):
                part_j = c[:, j * 128:(j + 1) * 128]
                acc = acc + part_j * part_j
            squares[...] = acc
        else:
            columns[...] = columns[...] + jnp.sum((c * c).reshape(width // 8, 8, width), axis=0)

        def body(i, carry):
            here = band_of(i)
            n = split(normal(raw, st, slot, here))
            g[here, :] = g[here, :] + dot3(n, (c_hi[...], c_lo[...]), view == 0)
            return carry

        lax.fori_loop(0, BANDS, body, 0)
        m = split(jnp.broadcast_to(st[slot, pl.ds(2, 1), :], (16, width)))
        means[view] = means[view] + dot3(m, (c_hi[...], c_lo[...]), view == 0)

    def loss_part():
        value = jnp.zeros((8, 128), F32)
        for t in range(4):
            c = fin[...] if t == 3 else cfull[t, mine, :]
            terms = off_weight * c * c
            if t == 0:
                shape = (chunk, width)
                on = lax.broadcasted_iota(jnp.int32, shape, 1) == (
                    lax.broadcasted_iota(jnp.int32, shape, 0) + z * chunk
                )
                terms = jnp.where(on, (1.0 - c) * (1.0 - c), terms)
            terms = jnp.sum(terms.reshape(chunk // 8, 8, width), axis=0)
            for j in range(width // 128):
                value = value + terms[:, j * 128:(j + 1) * 128]
        l_z[z] = value

    def loss_z(d):
        return send(l_z.at[z], l_z.at[z], lz_s.at[d], lz_r.at[d], at_z(mod(z + d, NZ)))

    def loss_copy(r):
        return send(l_send.at[r], l_recv.at[r], loss_s.at[r], loss_r.at[r], crossed(1 << r))

    def loss_start():
        for d in range(1, NZ):
            landed(l_z.at[mod(z - d, NZ)], lz_r.at[d], lz_s.at[d])
        value = l_z[0]
        for i in range(1, NZ):
            value = value + l_z[i]
        l_send[0] = value
        loss_copy(0).start()

    def loss_step(r):
        loss_copy(r).wait_recv()
        l_send[r + 1] = l_send[r] + l_recv[r]
        if r < 3:
            loss_copy(r + 1).start()

    gather(2, 3)
    gather(3, 2)
    grow(0, 0, 0)
    gather(3, 3)
    for t in (1, 2):
        sum_step(t, 0)
    when(even, sum_step, 3, 0)
    grow(1, 0, 0)
    for t in (1, 2):
        sum_step(t, 1)
    when(even, sum_step, 3, 1)
    far_b_here = far_b(raw_b.at[1])
    far_a_here = far_a(raw_a.at[1])

    @pl.when(even)
    def _():
        far_b_here.wait_recv()
        grow(0, 3, 3)

    when(odd, grow, 1, 3, 6)
    for s in (2, 3):
        for t in (1, 2):
            sum_step(t, s)
        when(even, sum_step, 3, s)
    end_1()
    end_2()
    gather(0, -1)
    when(even, end_3_even)
    loss_part()
    for d in range(1, NZ):
        loss_z(d).start()
    hand_take(4)
    hand_take(5)
    gather(1, -1)
    gather(0, 0)
    when(even, hand_take, 6)
    when(odd, hand_take, 3)
    gather(4, -1)
    gather(1, 0)
    gather(0, 1)
    gather(4, 0)
    gather(1, 1)
    gather(0, 2)
    loss_start()
    gather(4, 1)
    gather(1, 2)
    gather(0, 3)
    grow(0, 1 + y_lo, lane_tile[0])
    loss_step(0)
    gather(4, 2)
    gather(1, 3)
    grow(1, 1 + y_lo, lane_tile[1])
    loss_step(1)
    gather(4, 3)
    gather_other(0, other_tile[0])
    grow(0, 2 - y_lo, other_tile[0])
    loss_step(2)
    gather_other(1, other_tile[1])
    grow(1, 2 - y_lo, other_tile[1])
    loss_step(3)

    @pl.when(odd)
    def _():
        far_b_here.wait_recv()
        grow(0, 3, 3)

    @pl.when(even)
    def _():
        far_a_here.wait_recv()
        grow(1, 3, 6)

    loss_ref[0, 0] = jnp.sum(l_send[4]) * (1.0 / features)

    diagonal = []
    one_block = (
        lax.broadcasted_iota(jnp.int32, (128, 128), 0) == lax.broadcasted_iota(jnp.int32, (128, 128), 1)
    )
    for j in range(width // 128):
        block = cfull[0, j * 128:(j + 1) * 128, j * 128:(j + 1) * 128]
        diagonal.append(jnp.sum(jnp.where(one_block, block, 0.0), axis=0, keepdims=True))
    diagonal = jnp.concatenate(diagonal, axis=1)
    change = -(1.0 - diagonal) - off_weight * diagonal
    row_squares = jnp.sum(squares[...].T, axis=0, keepdims=True)
    column_squares = jnp.sum(columns[...], axis=0, keepdims=True)
    back_a = off_weight * row_squares + change * diagonal
    back_b = off_weight * column_squares + change * diagonal
    mean_a = off_weight * means[0, pl.ds(0, 1), :] + st_b[0, pl.ds(2, 1), :] * change
    mean_b = off_weight * means[1, pl.ds(0, 1), :] + st_a[0, pl.ds(2, 1), :] * change

    def out_copy(view, i):
        src, dst = ((g_a, ga_hbm), (g_b, gb_hbm))[view]
        return pltpu.make_async_copy(src.at[band_of(i)], dst.at[band_of(i)], out_sem.at[view, i])

    def finish(i, carry):
        here = band_of(i)
        n_a = normal(raw_a, st_a, 0, here)
        n_b = normal(raw_b, st_b, 0, here)
        g_a[here, :] = (off_weight * g_a[here, :] + n_b * change - mean_a - n_a * back_a) * st_a[0, pl.ds(1, 1), :]
        out_copy(0, i).start()
        g_b[here, :] = (off_weight * g_b[here, :] + n_a * change - mean_b - n_b * back_b) * st_b[0, pl.ds(1, 1), :]
        out_copy(1, i).start()
        return carry

    lax.fori_loop(0, BANDS, finish, 0)

    for view, edge in ((1, first_x), (0, last_x)):
        for c in range(PARTS):
            direct(view, c).wait_send()
            forward(view, c).wait_send()
    far_a(a_hbm).wait_send()
    far_b(b_hbm).wait_send()

    @pl.when(seam)
    def _():
        for r in range(PARTS // 2):
            from_relay(0, r).wait_send()

    for d in range(1, NZ):
        stat_z(d).wait_send()
    stat_y.wait_send()
    for k in (1, 2, 3):
        for view in (0, 1):
            stat_f(view, k).wait_send()
    for t in range(4):
        for s in range(HOPS):
            for copy in sum_send(t, s):
                copy.wait_send()
        y_copy(t).wait_send()
    hand1.wait_send()
    hand2.wait_send()
    hand3.wait_send()

    @pl.when(even)
    def _():
        hand6.wait_send()

    for lane in range(5):
        for s in range(HOPS):
            for copy in gather_send(lane, lane_tile[lane], s):
                copy.wait_send()
            if lane < 2:
                for i in (0, 1):
                    across(lane, lane_tile[lane], s, i).wait_send()
    for d in range(1, NZ):
        loss_z(d).wait_send()
    for r in range(4):
        loss_copy(r).wait_send()
    for view in (0, 1):
        for i in range(BANDS):
            out_copy(view, i).wait()


def local(view_a, view_b):
    rows, width = view_a.shape
    part = rows // PARTS
    band = rows // BANDS
    chunk = width // NZ
    dma = pltpu.SemaphoreType.DMA
    anywhere = pl.BlockSpec(memory_space=pl.ANY)
    grad_a, grad_b, loss = pl.pallas_call(
        kernel,
        out_shape=(
            jax.ShapeDtypeStruct((rows, width), F32),
            jax.ShapeDtypeStruct((rows, width), F32),
            jax.ShapeDtypeStruct((1, 1), F32),
        ),
        in_specs=[anywhere, anywhere],
        out_specs=(anywhere, anywhere, pl.BlockSpec(memory_space=pltpu.SMEM)),
        scratch_shapes=[
            pltpu.VMEM((4, rows, width), F32),
            pltpu.VMEM((4, rows, width), F32),
            pltpu.VMEM((BANDS + 1, width, band), BF16),
            pltpu.VMEM((BANDS + 1, width, band), BF16),
            pltpu.VMEM((band, width), BF16),
            pltpu.VMEM((band, width), BF16),
            pltpu.VMEM((4, width, width), F32),
            pltpu.VMEM((4, HOPS, chunk, width), F32),
            pltpu.VMEM((4, HOPS, chunk, width), F32),
            pltpu.VMEM((4, chunk, width), F32),
            pltpu.VMEM((chunk, width), F32),
            pltpu.VMEM((7, width, width), F32),
            pltpu.VMEM((width, width), BF16),
            pltpu.VMEM((width, width), BF16),
            pltpu.VMEM((rows, width), F32),
            pltpu.VMEM((rows, width), F32),
            pltpu.VMEM((PARTS // 2, part, width), F32),
            pltpu.VMEM((NZ, 8, width), F32),
            pltpu.VMEM((2, 8, width), F32),
            pltpu.VMEM((4, 8, width), F32),
            pltpu.VMEM((4, 8, width), F32),
            pltpu.VMEM((width, 128), F32),
            pltpu.VMEM((8, width), F32),
            pltpu.VMEM((2, 16, width), F32),
            pltpu.VMEM((NZ, 8, 128), F32),
            pltpu.VMEM((5, 8, 128), F32),
            pltpu.VMEM((4, 8, 128), F32),
            dma((2,)),
            dma((2, BANDS)),
            dma((2, PARTS)), dma((2, PARTS)),
            dma((2, PARTS)), dma((2, PARTS)),
            dma((2,)), dma((2,)),
            dma((PARTS // 2,)), dma((PARTS // 2,)),
            dma((NZ,)), dma((NZ,)),
            dma(()), dma(()),
            dma((2, 4)), dma((2, 4)),
            dma((2, 4, HOPS)), dma((2, 4, HOPS)),
            dma((4,)), dma((4,)),
            dma((4,)), dma((7,)),
            dma((2, 5, HOPS)), dma((2, 5, HOPS)),
            dma((2, 2, HOPS)), dma((2, 2, HOPS)),
            dma((NZ,)), dma((NZ,)),
            dma((4,)), dma((4,)),
        ],
        compiler_params=pltpu.CompilerParams(
            collective_id=0, has_side_effects=True, vmem_limit_bytes=60 * 1024 * 1024
        ),
        cost_estimate=pl.CostEstimate(
            flops=2 * 3 * 12 * rows * width * width, bytes_accessed=16 * rows * width, transcendentals=0
        ),
    )(view_a, view_b)
    return grad_a, grad_b, loss[0, 0]


def solution(mesh):
    spec = P("batch", "feat")
    return jax.shard_map(
        local, mesh=mesh, in_specs=(spec, spec), out_specs=(spec, spec, P()), check_vma=False
    )
```

```python
import functools

import jax
import jax.numpy as jnp
from jax import lax
from jax.experimental import pallas as pl
from jax.experimental.pallas import tpu as pltpu
from jax.sharding import PartitionSpec as P

MESH = pl.DeviceIdType.MESH
F32 = jnp.float32
BF16 = jnp.bfloat16

eps = 1e-05
off_weight = 0.25

NZ = 8
NX = 4
NY = 4
NF = 16
PARTS = 8
AHEAD = 2
BANDS = 4
HOPS = 4


def mod(value, n):
    return lax.rem(value + n, n)


def split(value):
    hi = value.astype(BF16)
    return hi, (value - hi.astype(F32)).astype(BF16)


def dot3(left, right, transposed=False):
    dims = (((1,), (1 if transposed else 0,)), ((), ()))
    dot = functools.partial(lax.dot_general, dimension_numbers=dims, preferred_element_type=F32)
    return dot(left[0], right[0]) + dot(left[0], right[1]) + dot(left[1], right[0])


def kernel(
    a_hbm, b_hbm, ga_hbm, gb_hbm, loss_ref,
    raw_a, raw_b, at_hi, at_lo, b_hi, b_lo, tiles, rs_p, rs_m, y_recv, fin, cfull, c_hi, c_lo,
    g_a, g_b, relay, st_z, st_y, st_a, st_b, squares, columns, means, l_z, l_send, l_recv,
    in_sem, out_sem, direct_s, direct_r, fwd_s, fwd_r, far_s, far_r, rel_s, rel_r,
    stz_s, stz_r, sty_s, sty_r, stf_s, stf_r, rs_s, rs_r, y_s, y_r, hand_s, hand_r,
    ag_s, ag_r, ay_s, ay_r, lz_s, lz_r, loss_s, loss_r,
):
    rows, width = a_hbm.shape
    part = rows // PARTS
    band = rows // BANDS
    chunk = width // NZ
    half = chunk // 2
    total = float(rows * 2 * NZ)
    features = float(width * NF)

    batch = lax.axis_index("batch")
    feat = lax.axis_index("feat")
    z = lax.div(batch, 2)
    y_lo = lax.rem(batch, 2)
    y = lax.div(feat, 2 * NX) * 2 + y_lo
    x = lax.rem(lax.div(feat, 2), NX)
    core = lax.rem(feat, 2)
    even = core == 0
    odd = core == 1
    first_x = x == 0
    last_x = x == NX - 1
    seam = jnp.logical_or(first_x, last_x)

    def at_feat(f):
        return {"batch": batch, "feat": f}

    def at_z(z_other):
        return {"batch": z_other * 2 + y_lo, "feat": feat}

    def at_xy(x_other, y_other):
        f = lax.div(y_other, 2) * (2 * NX) + x_other * 2 + core
        return {"batch": z * 2 + lax.rem(y_other, 2), "feat": f}

    def neighbour(steps):
        return at_feat(mod(feat + steps, NF))

    def crossed(stride):
        return at_feat(feat + stride - 2 * stride * lax.rem(lax.div(feat, stride), 2))

    other_core = crossed(1)
    other_y = {"batch": batch + 1 - 2 * y_lo, "feat": feat}
    above = at_z(mod(z + 1, NZ))
    below = at_z(mod(z - 1, NZ))
    mirror_x = NX - 1 - x
    ahead_crossed = at_feat(mod(feat + 3 - 2 * core, NF))

    def send(src, dst, s_sem, r_sem, device):
        return pltpu.make_async_remote_copy(
            src_ref=src, dst_ref=dst, send_sem=s_sem, recv_sem=r_sem,
            device_id=device, device_id_type=MESH,
        )

    def landed(dst, r_sem, s_sem):
        send(dst, dst, s_sem, r_sem, other_core).wait_recv()

    load_b = pltpu.make_async_copy(b_hbm, raw_b.at[0], in_sem.at[0])
    load_a = pltpu.make_async_copy(a_hbm, raw_a.at[0], in_sem.at[1])
    load_b.start()
    load_a.start()

    barrier = pltpu.get_barrier_semaphore()
    friends = [neighbour(k) for k in (-3, -2, -1, 1, 2, 3)]
    friends += [crossed(k) for k in (2, 4, 8)]
    friends += [at_z(mod(z + d, NZ)) for d in range(1, NZ)]
    friends += [other_y]
    for friend in friends:
        pl.semaphore_signal(barrier, inc=1, device_id=friend, device_id_type=MESH)

    @pl.when(seam)
    def _():
        for friend in (
            at_xy(mirror_x, mod(y - 1, NY)), at_xy(mirror_x, mod(y + 1, NY)),
            at_xy(x, mod(y - 1, NY)), at_xy(x, mod(y + 1, NY)),
        ):
            pl.semaphore_signal(barrier, inc=1, device_id=friend, device_id_type=MESH)

    pl.semaphore_wait(barrier, jnp.where(seam, len(friends) + 4, len(friends)))


    def piece(c):
        return pl.ds(pl.multiple_of(c * part, part), part)

    def direct(view, c):
        src, raw, steps = ((a_hbm, raw_a, 2), (b_hbm, raw_b, -2))[view]
        return send(
            src.at[piece(c)], raw.at[1, piece(c)], direct_s.at[view, c], direct_r.at[view, c],
            neighbour(steps),
        )

    def to_relay(view, c):
        src = (a_hbm, b_hbm)[view]
        return send(
            src.at[piece(c)], relay.at[c - PARTS // 2], direct_s.at[view, c],
            rel_r.at[c - PARTS // 2], at_xy(mirror_x, mod(y - 1, NY)),
        )

    def from_relay(view, r):
        raw = (raw_a, raw_b)[view]
        c = r + PARTS // 2
        return send(
            relay.at[r], raw.at[1, piece(c)], rel_s.at[r], direct_r.at[view, c],
            at_xy(x, mod(y - 1, NY)),
        )

    def piece_start(c):
        for view, edge in ((1, first_x), (0, last_x)):
            if c < PARTS // 2:
                direct(view, c).start()
            else:
                @pl.when(edge)
                def _():
                    to_relay(view, c).start()

                @pl.when(jnp.logical_not(edge))
                def _():
                    direct(view, c).start()

    for c in range(AHEAD):
        piece_start(c)

    def far_b(src):
        return send(src, raw_b.at[3], far_s.at[1], far_r.at[1], neighbour(-1))

    def far_a(src):
        return send(src, raw_a.at[3], far_s.at[0], far_r.at[0], neighbour(1))

    @pl.when(odd)
    def _():
        far_b(b_hbm).start()

    @pl.when(even)
    def _():
        far_a(a_hbm).start()

    load_b.wait()
    load_a.wait()
    strip = 128
    for view, raw in ((0, raw_a), (1, raw_b)):
        def add_up(i, acc):
            v = raw[0, pl.ds(pl.multiple_of(i * strip, strip), strip), :]
            return acc + jnp.sum(v.reshape(strip // 8, 8, width), axis=0)

        zeros = jnp.zeros((8, width), F32)
        acc = lax.fori_loop(0, rows // strip, add_up, zeros)
        mean = jnp.sum(acc, axis=0, keepdims=True) * (1.0 / rows)

        def add_up_squares(i, carry):
            rest, square = carry
            v = raw[0, pl.ds(pl.multiple_of(i * strip, strip), strip), :] - mean
            v = v.reshape(strip // 8, 8, width)
            return rest + jnp.sum(v, axis=0), square + jnp.sum(v * v, axis=0)

        rest, square = lax.fori_loop(0, rows // strip, add_up_squares, (zeros, zeros))
        st_z[z, pl.ds(3 * view, 1), :] = mean
        st_z[z, pl.ds(3 * view + 1, 1), :] = jnp.sum(square, axis=0, keepdims=True)
        st_z[z, pl.ds(3 * view + 2, 1), :] = jnp.sum(rest, axis=0, keepdims=True)

    def stat_z(d):
        return send(
            st_z.at[z], st_z.at[z], stz_s.at[d], stz_r.at[d], at_z(mod(z + d, NZ))
        )

    for d in range(1, NZ):
        stat_z(d).start()
    for d in range(1, NZ):
        landed(st_z.at[mod(z - d, NZ)], stz_r.at[d], stz_s.at[d])
    for view in (0, 1):
        means_z = [st_z[i, pl.ds(3 * view, 1), :] for i in range(NZ)]
        mean = sum(means_z[1:], means_z[0]) * (1.0 / NZ)
        square = jnp.zeros((1, width), F32)
        rest = jnp.zeros((1, width), F32)
        for i in range(NZ):
            off = means_z[i] - mean
            square = square + (st_z[i, pl.ds(3 * view + 1, 1), :] + float(rows) * off * off)
            rest = rest + (st_z[i, pl.ds(3 * view + 2, 1), :] + float(rows) * off)
        st_y[0, pl.ds(3 * view, 1), :] = mean
        st_y[0, pl.ds(3 * view + 1, 1), :] = square
        st_y[0, pl.ds(3 * view + 2, 1), :] = rest
    stat_y = send(st_y.at[0], st_y.at[1], sty_s, sty_r, other_y)
    stat_y.start()
    stat_y.wait_recv()
    rows_z = float(rows * NZ)
    for view, st in ((0, st_a), (1, st_b)):
        mean0, mean1 = (st_y[i, pl.ds(3 * view, 1), :] for i in (0, 1))
        mean = 0.5 * (mean0 + mean1)
        off0, off1 = mean0 - mean, mean1 - mean
        square = (
            st_y[0, pl.ds(3 * view + 1, 1), :] + st_y[1, pl.ds(3 * view + 1, 1), :]
            + rows_z * (off0 * off0 + off1 * off1)
        )
        rest = (
            st_y[0, pl.ds(3 * view + 2, 1), :] + st_y[1, pl.ds(3 * view + 2, 1), :]
            + rows_z * (off0 + off1)
        )
        inverse = 1.0 / jnp.sqrt(square * (1.0 / total) + eps)
        st[0, pl.ds(0, 1), :] = mean
        st[0, pl.ds(1, 1), :] = inverse
        st[0, pl.ds(2, 1), :] = rest * (1.0 / total) * inverse

    def stat_f(view, k):
        st = (st_a, st_b)[view]
        if k == 2:
            slot = 1
        elif (k == 1) == (view == 1):
            slot = 2 + core
        else:
            slot = 3 - core
        return send(
            st.at[0], st.at[slot], stf_s.at[view, k], stf_r.at[view, slot],
            neighbour(-k if view == 1 else k),
        )

    for k in (2, 1, 3):
        for view in (1, 0):
            stat_f(view, k).start()

    def normal(raw, st, slot, rows_here):
        return (raw[slot, rows_here, :] - st[slot, pl.ds(0, 1), :]) * st[slot, pl.ds(1, 1), :]

    def add_tile(t, c, left_hi, left_lo, first):
        right = (b_hi[...], b_lo[...])
        def rows_of(i, carry):
            here = pl.ds(pl.multiple_of(i * (width // 2), width // 2), width // 2)
            out = dot3((left_hi[c, here, :], left_lo[c, here, :]), right)
            if first:
                tiles[t, here, :] = out
            else:
                tiles[t, here, :] = tiles[t, here, :] + out
            return carry
        lax.fori_loop(0, 2, rows_of, 0)

    def band_of(c):
        return pl.ds(pl.multiple_of(c * band, band), band)

    def turn_a(slot, c, index):
        hi, lo = split(normal(raw_a, st_a, slot, band_of(c)).T)
        at_hi[index] = hi
        at_lo[index] = lo

    def take_b(slot, c):
        hi, lo = split(normal(raw_b, st_b, slot, band_of(c)))
        b_hi[...] = hi
        b_lo[...] = lo

    def clear(t, carry):
        tiles[t] = jnp.zeros((width, width), F32)
        return carry

    lax.fori_loop(0, 4, clear, 0)

    def own_tile(c, carry):
        turn_a(0, c, c)
        take_b(0, c)
        add_tile(0, c, at_hi, at_lo, False)
        return carry

    lax.fori_loop(0, BANDS, own_tile, 0)

    def dest(q):
        return pl.multiple_of(mod(q, NZ) * chunk, chunk)

    def sum_send(t, s):
        if s == 0:
            up = pl.ds(dest(z + HOPS), half)
            down = pl.ds(pl.multiple_of(dest(z + HOPS) + half, half), half)
            up_to, down_to = pl.ds(0, half), pl.ds(half, half)
        else:
            up, down = pl.ds(dest(z + HOPS - s), chunk), pl.ds(dest(z - HOPS + s), chunk)
            up_to = down_to = pl.ds(0, chunk)
        return (
            send(tiles.at[t, up], rs_p.at[t, s, up_to], rs_s.at[0, t, s], rs_r.at[0, t, s], above),
            send(tiles.at[t, down], rs_m.at[t, s, down_to], rs_s.at[1, t, s], rs_r.at[1, t, s], below),
        )

    def sum_start(t, s):
        for copy in sum_send(t, s):
            copy.start()

    def sum_take(t, s):
        for copy in sum_send(t, s):
            copy.wait_recv()
        for recv, q, low in ((rs_p, z + HOPS - 1 - s, 0), (rs_m, z - HOPS + 1 + s, half)):
            if s == 0:
                here = pl.ds(pl.multiple_of(dest(q) + low, half), half)
                tiles[t, here, :] = tiles[t, here, :] + recv[t, s, pl.ds(low, half), :]
            else:
                here = pl.ds(dest(q), chunk)
                tiles[t, here, :] = tiles[t, here, :] + recv[t, s]

    mine = pl.ds(dest(z), chunk)

    def y_copy(t):
        return send(tiles.at[t, mine], y_recv.at[t], y_s.at[t], y_r.at[t], other_y)

    def sum_end(t):
        sum_take(t, HOPS - 1)
        y_copy(t).start()

    def sum_all(t):
        y_copy(t).wait_recv()
        return (tiles[t, mine, :] + y_recv[t]) * (1.0 / total)

    def gather_part(s, mover):
        up, down = z - s - mover, z + s + mover
        if s < HOPS - 1:
            return pl.ds(dest(up), chunk), pl.ds(dest(down), chunk)
        return pl.ds(dest(up), half), pl.ds(pl.multiple_of(dest(down) + half, half), half)

    def gather_send(lane, u, s):
        up, down = gather_part(s, 0)
        return (
            send(cfull.at[u, up], cfull.at[u, up], ag_s.at[0, lane, s], ag_r.at[0, lane, s], above),
            send(cfull.at[u, down], cfull.at[u, down], ag_s.at[1, lane, s], ag_r.at[1, lane, s], below),
        )

    def gather_start(lane, u, s):
        for copy in gather_send(lane, u, s):
            copy.start()

    def across(lane, u, s, i):
        p = gather_part(s, 1)[i]
        return send(cfull.at[u, p], cfull.at[u, p], ay_s.at[i, lane, s], ay_r.at[i, lane, s], other_y)

    def gather_take(lane, u, s):
        for i, p in enumerate(gather_part(s, 1)):
            landed(cfull.at[u, p], ag_r.at[i, lane, s], ag_s.at[i, lane, s])
            if lane < 2:
                across(lane, u, s, i).start()
        if s < HOPS - 1:
            gather_start(lane, u, s + 1)

    def gather_other(lane, u):
        for s in range(HOPS):
            for i in (0, 1):
                across(lane, u, s, i).wait_recv()

    lane_tile = (1 + y_lo, 4 + y_lo, 0, 3 + 3 * core, 6 - 3 * core)
    other_tile = (2 - y_lo, 5 - y_lo)

    def gather(lane, s):
        if s < 0:
            gather_start(lane, lane_tile[lane], 0)
        else:
            gather_take(lane, lane_tile[lane], s)

    hand1 = send(cfull.at[1, mine], cfull.at[4, mine], hand_s.at[0], hand_r.at[4], neighbour(2))
    hand2 = send(cfull.at[2, mine], cfull.at[5, mine], hand_s.at[1], hand_r.at[5], ahead_crossed)
    hand3 = send(fin, cfull.at[3, mine], hand_s.at[2], hand_r.at[3], neighbour(-1))
    hand6 = send(fin, cfull.at[6, mine], hand_s.at[3], hand_r.at[6], neighbour(2))

    def hand_take(u):
        landed(cfull.at[u, mine], hand_r.at[u], hand_s.at[0])

    def when(cond, f, *args):
        @pl.when(cond)
        def _():
            f(*args)

    def sum_step(t, s):
        if s < HOPS - 1:
            sum_take(t, s)
            sum_start(t, s + 1)
        else:
            sum_end(t)

    def end_0():
        cfull[0, mine, :] = sum_all(0)

    def end_1():
        cfull[1, mine, :] = sum_all(1)
        hand1.start()

    def end_2():
        cfull[2, mine, :] = sum_all(2)
        hand2.start()

    def end_3_odd():
        last = sum_all(3)
        fin[...] = last
        hand3.start()
        cfull[6, mine, :] = last

    def end_3_even():
        fin[...] = sum_all(3)
        hand3.start()
        hand6.start()

    def forward(view, c):
        raw = (raw_a, raw_b)[view]
        return send(
            raw.at[1, piece(c)], raw.at[2, piece(c)], fwd_s.at[view, c], fwd_r.at[view, c],
            other_core,
        )

    sum_start(0, 0)
    for slot in (3, 1, 2):
        for view, st in ((1, st_b), (0, st_a)):
            landed(st.at[slot], stf_r.at[view, slot], stf_s.at[view, slot])

    @pl.when(odd)
    def _():
        far_a(a_hbm).wait_recv()

        def fourth_tile(c, carry):
            turn_a(3, c, BANDS)
            take_b(0, c)
            add_tile(3, BANDS, at_hi, at_lo, False)
            return carry

        lax.fori_loop(0, BANDS, fourth_tile, 0)
        sum_start(3, 0)

    def early(j):
        if j < HOPS:
            sum_step(0, j)
            when(odd, sum_step, 3, j)
        elif j == 4:
            end_0()
            gather(2, -1)
            when(odd, end_3_odd)
        elif j == 5:
            gather(2, 0)
            when(even, hand_take, 3)
            gather(3, -1)
        else:
            gather(2, j - 5)
            gather(3, j - 6)

    for c in range(BANDS):
        for j in (2 * c, 2 * c + 1):
            r = j - (PARTS // 2 - 1)
            if 0 <= r < PARTS // 2:
                for view, edge in ((1, last_x), (0, first_x)):
                    @pl.when(edge)
                    def _():
                        landed(relay.at[r], rel_r.at[r], rel_s.at[r])
                        from_relay(view, r).start()

            for view in (1, 0):
                direct(view, j).wait_recv()
                forward(view, j).start()
            if j + AHEAD < PARTS:
                piece_start(j + AHEAD)
            early(j)
        take_b(1, c)
        add_tile(1, c, at_hi, at_lo, False)

        @pl.when(even)
        def _():
            for j in (2 * c, 2 * c + 1):
                forward(0, j).wait_recv()
            turn_a(2, c, BANDS)
            add_tile(3, BANDS, at_hi, at_lo, False)

        for j in (2 * c, 2 * c + 1):
            forward(1, j).wait_recv()
        take_b(2, c)
        add_tile(2, c, at_hi, at_lo, False)

    @pl.when(odd)
    def _():
        for j in range(PARTS):
            forward(0, j).wait_recv()

    for t in (1, 2):
        sum_start(t, 0)
    when(even, sum_start, 3, 0)
    when(even, far_b(raw_b.at[1]).start)
    when(odd, far_a(raw_a.at[1]).start)

    squares[...] = jnp.zeros_like(squares)
    columns[...] = jnp.zeros_like(columns)
    means[...] = jnp.zeros_like(means)

    def clear_g(i, carry):
        g_a[band_of(i), :] = jnp.zeros((band, width), F32)
        g_b[band_of(i), :] = jnp.zeros((band, width), F32)
        return carry

    lax.fori_loop(0, BANDS, clear_g, 0)

    def grow(view, slot, u):
        g, raw, st = ((g_a, raw_b, st_b), (g_b, raw_a, st_a))[view]
        c = cfull[u]
        hi, lo = split(c)
        c_hi[...] = hi
        c_lo[...] = lo
        if view == 0:
            acc = squares[...]
            for j in range(width // 128):
                part_j = c[:, j * 128:(j + 1) * 128]
                acc = acc + part_j * part_j
            squares[...] = acc
        else:
            columns[...] = columns[...] + jnp.sum((c * c).reshape(width // 8, 8, width), axis=0)

        def body(i, carry):
            here = band_of(i)
            n = split(normal(raw, st, slot, here))
            g[here, :] = g[here, :] + dot3(n, (c_hi[...], c_lo[...]), view == 0)
            return carry

        lax.fori_loop(0, BANDS, body, 0)
        m = split(jnp.broadcast_to(st[slot, pl.ds(2, 1), :], (16, width)))
        means[view] = means[view] + dot3(m, (c_hi[...], c_lo[...]), view == 0)

    def loss_part():
        value = jnp.zeros((8, 128), F32)
        for t in range(4):
            c = fin[...] if t == 3 else cfull[t, mine, :]
            terms = off_weight * c * c
            if t == 0:
                shape = (chunk, width)
                on = lax.broadcasted_iota(jnp.int32, shape, 1) == (
                    lax.broadcasted_iota(jnp.int32, shape, 0) + z * chunk
                )
                terms = jnp.where(on, (1.0 - c) * (1.0 - c), terms)
            terms = jnp.sum(terms.reshape(chunk // 8, 8, width), axis=0)
            for j in range(width // 128):
                value = value + terms[:, j * 128:(j + 1) * 128]
        l_z[z] = value

    def loss_z(d):
        return send(l_z.at[z], l_z.at[z], lz_s.at[d], lz_r.at[d], at_z(mod(z + d, NZ)))

    def loss_copy(r):
        return send(l_send.at[r], l_recv.at[r], loss_s.at[r], loss_r.at[r], crossed(1 << r))

    def loss_start():
        for d in range(1, NZ):
            landed(l_z.at[mod(z - d, NZ)], lz_r.at[d], lz_s.at[d])
        value = l_z[0]
        for i in range(1, NZ):
            value = value + l_z[i]
        l_send[0] = value
        loss_copy(0).start()

    def loss_step(r):
        loss_copy(r).wait_recv()
        l_send[r + 1] = l_send[r] + l_recv[r]
        if r < 3:
            loss_copy(r + 1).start()

    gather(2, 3)
    gather(3, 2)
    grow(0, 0, 0)
    gather(3, 3)
    for t in (1, 2):
        sum_step(t, 0)
    when(even, sum_step, 3, 0)
    grow(1, 0, 0)
    for t in (1, 2):
        sum_step(t, 1)
    when(even, sum_step, 3, 1)
    far_b_here = far_b(raw_b.at[1])
    far_a_here = far_a(raw_a.at[1])

    @pl.when(even)
    def _():
        far_b_here.wait_recv()
        grow(0, 3, 3)

    when(odd, grow, 1, 3, 6)
    for s in (2, 3):
        for t in (1, 2):
            sum_step(t, s)
        when(even, sum_step, 3, s)
    end_1()
    end_2()
    gather(0, -1)
    when(even, end_3_even)
    loss_part()
    for d in range(1, NZ):
        loss_z(d).start()
    hand_take(4)
    hand_take(5)
    gather(1, -1)
    gather(0, 0)
    when(even, hand_take, 6)
    when(odd, hand_take, 3)
    gather(4, -1)
    gather(1, 0)
    gather(0, 1)
    gather(4, 0)
    gather(1, 1)
    gather(0, 2)
    loss_start()
    gather(4, 1)
    gather(1, 2)
    gather(0, 3)
    grow(0, 1 + y_lo, lane_tile[0])
    loss_step(0)
    gather(4, 2)
    gather(1, 3)
    grow(1, 1 + y_lo, lane_tile[1])
    loss_step(1)
    gather(4, 3)
    gather_other(0, other_tile[0])
    grow(0, 2 - y_lo, other_tile[0])
    loss_step(2)
    gather_other(1, other_tile[1])
    grow(1, 2 - y_lo, other_tile[1])
    loss_step(3)

    @pl.when(odd)
    def _():
        far_b_here.wait_recv()
        grow(0, 3, 3)

    @pl.when(even)
    def _():
        far_a_here.wait_recv()
        grow(1, 3, 6)

    loss_ref[0, 0] = jnp.sum(l_send[4]) * (1.0 / features)

    diagonal = []
    one_block = (
        lax.broadcasted_iota(jnp.int32, (128, 128), 0) == lax.broadcasted_iota(jnp.int32, (128, 128), 1)
    )
    for j in range(width // 128):
        block = cfull[0, j * 128:(j + 1) * 128, j * 128:(j + 1) * 128]
        diagonal.append(jnp.sum(jnp.where(one_block, block, 0.0), axis=0, keepdims=True))
    diagonal = jnp.concatenate(diagonal, axis=1)
    change = -(1.0 - diagonal) - off_weight * diagonal
    row_squares = jnp.sum(squares[...].T, axis=0, keepdims=True)
    column_squares = jnp.sum(columns[...], axis=0, keepdims=True)
    back_a = off_weight * row_squares + change * diagonal
    back_b = off_weight * column_squares + change * diagonal
    mean_a = off_weight * means[0, pl.ds(0, 1), :] + st_b[0, pl.ds(2, 1), :] * change
    mean_b = off_weight * means[1, pl.ds(0, 1), :] + st_a[0, pl.ds(2, 1), :] * change

    def out_copy(view, i):
        src, dst = ((g_a, ga_hbm), (g_b, gb_hbm))[view]
        return pltpu.make_async_copy(src.at[band_of(i)], dst.at[band_of(i)], out_sem.at[view, i])

    def finish(i, carry):
        here = band_of(i)
        n_a = normal(raw_a, st_a, 0, here)
        n_b = normal(raw_b, st_b, 0, here)
        g_a[here, :] = (off_weight * g_a[here, :] + n_b * change - mean_a - n_a * back_a) * st_a[0, pl.ds(1, 1), :]
        out_copy(0, i).start()
        g_b[here, :] = (off_weight * g_b[here, :] + n_a * change - mean_b - n_b * back_b) * st_b[0, pl.ds(1, 1), :]
        out_copy(1, i).start()
        return carry

    lax.fori_loop(0, BANDS, finish, 0)

    for view, edge in ((1, first_x), (0, last_x)):
        for c in range(PARTS):
            direct(view, c).wait_send()
            forward(view, c).wait_send()
    far_a(a_hbm).wait_send()
    far_b(b_hbm).wait_send()

    @pl.when(seam)
    def _():
        for r in range(PARTS // 2):
            from_relay(0, r).wait_send()

    for d in range(1, NZ):
        stat_z(d).wait_send()
    stat_y.wait_send()
    for k in (1, 2, 3):
        for view in (0, 1):
            stat_f(view, k).wait_send()
    for t in range(4):
        for s in range(HOPS):
            for copy in sum_send(t, s):
                copy.wait_send()
        y_copy(t).wait_send()
    hand1.wait_send()
    hand2.wait_send()
    hand3.wait_send()

    @pl.when(even)
    def _():
        hand6.wait_send()

    for lane in range(5):
        for s in range(HOPS):
            for copy in gather_send(lane, lane_tile[lane], s):
                copy.wait_send()
            if lane < 2:
                for i in (0, 1):
                    across(lane, lane_tile[lane], s, i).wait_send()
    for d in range(1, NZ):
        loss_z(d).wait_send()
    for r in range(4):
        loss_copy(r).wait_send()
    for view in (0, 1):
        for i in range(BANDS):
            out_copy(view, i).wait()


def local(view_a, view_b):
    rows, width = view_a.shape
    part = rows // PARTS
    band = rows // BANDS
    chunk = width // NZ
    dma = pltpu.SemaphoreType.DMA
    anywhere = pl.BlockSpec(memory_space=pl.ANY)
    grad_a, grad_b, loss = pl.pallas_call(
        kernel,
        out_shape=(
            jax.ShapeDtypeStruct((rows, width), F32),
            jax.ShapeDtypeStruct((rows, width), F32),
            jax.ShapeDtypeStruct((1, 1), F32),
        ),
        in_specs=[anywhere, anywhere],
        out_specs=(anywhere, anywhere, pl.BlockSpec(memory_space=pltpu.SMEM)),
        scratch_shapes=[
            pltpu.VMEM((4, rows, width), F32),
            pltpu.VMEM((4, rows, width), F32),
            pltpu.VMEM((BANDS + 1, width, band), BF16),
            pltpu.VMEM((BANDS + 1, width, band), BF16),
            pltpu.VMEM((band, width), BF16),
            pltpu.VMEM((band, width), BF16),
            pltpu.VMEM((4, width, width), F32),
            pltpu.VMEM((4, HOPS, chunk, width), F32),
            pltpu.VMEM((4, HOPS, chunk, width), F32),
            pltpu.VMEM((4, chunk, width), F32),
            pltpu.VMEM((chunk, width), F32),
            pltpu.VMEM((7, width, width), F32),
            pltpu.VMEM((width, width), BF16),
            pltpu.VMEM((width, width), BF16),
            pltpu.VMEM((rows, width), F32),
            pltpu.VMEM((rows, width), F32),
            pltpu.VMEM((PARTS // 2, part, width), F32),
            pltpu.VMEM((NZ, 8, width), F32),
            pltpu.VMEM((2, 8, width), F32),
            pltpu.VMEM((4, 8, width), F32),
            pltpu.VMEM((4, 8, width), F32),
            pltpu.VMEM((width, 128), F32),
            pltpu.VMEM((8, width), F32),
            pltpu.VMEM((2, 16, width), F32),
            pltpu.VMEM((NZ, 8, 128), F32),
            pltpu.VMEM((5, 8, 128), F32),
            pltpu.VMEM((4, 8, 128), F32),
            dma((2,)),
            dma((2, BANDS)),
            dma((2, PARTS)), dma((2, PARTS)),
            dma((2, PARTS)), dma((2, PARTS)),
            dma((2,)), dma((2,)),
            dma((PARTS // 2,)), dma((PARTS // 2,)),
            dma((NZ,)), dma((NZ,)),
            dma(()), dma(()),
            dma((2, 4)), dma((2, 4)),
            dma((2, 4, HOPS)), dma((2, 4, HOPS)),
            dma((4,)), dma((4,)),
            dma((4,)), dma((7,)),
            dma((2, 5, HOPS)), dma((2, 5, HOPS)),
            dma((2, 2, HOPS)), dma((2, 2, HOPS)),
            dma((NZ,)), dma((NZ,)),
            dma((4,)), dma((4,)),
        ],
        compiler_params=pltpu.CompilerParams(
            collective_id=0, has_side_effects=True, vmem_limit_bytes=60 * 1024 * 1024
        ),
        cost_estimate=pl.CostEstimate(
            flops=2 * 3 * 12 * rows * width * width, bytes_accessed=16 * rows * width, transcendentals=0
        ),
    )(view_a, view_b)
    return grad_a, grad_b, loss[0, 0]


def solution(mesh):
    spec = P("batch", "feat")
    return jax.shard_map(
        local, mesh=mesh, in_specs=(spec, spec), out_specs=(spec, spec, P()), check_vma=False
    )
```
